256 devices in a mesh: blocks: 8 (over z), views: 4 (over y), rows: 8 (over x, core).
Axes of the slice: x: 4, y: 4, z: 8, core: 2. Of those that a mesh axis runs over, the one named last changes fastest.
Arguments:
- estimate: float32 [64, 1024, 256], P('rows', 'blocks'), may hold values from 0.5 to 2
- views_data: float32 [4, 64, 1024, 256], P('views', 'rows', 'blocks'), may hold values from 0.2 to 5
- target: int32 [4, 64, 1024, 2], P('views', 'rows', 'blocks'), may hold values from 0 to 131071, as said below
- psf_taps: float32 [4, 3, 7], P('views'), may hold values from 0.2 to 1
- shifts: int32 [4], P('views'), may hold values from 0 to 127
Outputs:
- restored: float32 [64, 1024, 256], P('rows', 'blocks')
The draws below stay inside these ranges and needn't reach their ends.
Inputs may be any that keep to these rules, and one draw needn't show every extreme that they name: `target`: for each view every output brick is named exactly once. The bricks of one view held by one device name at most 64 = 64 output bricks held by any one device, and exactly 64 of some device.
All inputs are finite; a program needn't handle non-finite values.
Results may differ from the reference program's by a relative error of at most 0.00002.
Values sent between devices are 32-bit elements; how exact they have to be, the bound alone decides.
No kernel may reach another device: no remote copies, remote signals or barrier semaphores. Data moves between devices by JAX's collectives and lax.ppermute only.
A program may use at most 64 MiB of HBM per device.

```python
import math
import jax
import jax.numpy as jnp
from jax import lax

VIEWS = 4
NY = 1024
NZ = 256
BRICK = 128
HALO = 3
ITERS = 2
CX = 8
NX = 64
CY = 128
NZB = 2


def draw_target(key, part):
    key = jax.random.fold_in(key, 7)
    row_devices = NX // CX
    peer_count = row_devices * (NY // CY)
    brick_count = CX * CY * NZB
    quota = brick_count // peer_count
    half_quota = quota // 2
    grid_x = lax.broadcasted_iota(jnp.int32, (NX, NY, NZB), 0)
    grid_y = lax.broadcasted_iota(jnp.int32, (NX, NY, NZB), 1)
    grid_z = lax.broadcasted_iota(jnp.int32, (NX, NY, NZB), 2)
    source_dev = grid_y // CY * row_devices + grid_x // CX
    local_slot = (grid_x % CX * CY + grid_y % CY) * NZB + grid_z
    slot_ids = jnp.arange(brick_count, dtype=jnp.int32)

    def one_view(view_key):
        keys = jax.random.split(view_key, 4)
        order = jax.random.permutation(keys[0], brick_count).astype(jnp.int32)
        spread = jax.random.randint(keys[1], (peer_count // 2 - 1,), -half_quota, half_quota + 1).astype(jnp.int32)
        middle = jnp.stack([quota + spread, quota - spread], axis=1).reshape(-1)
        counts = jnp.concatenate([jnp.full((1,), 2 * quota, jnp.int32), middle, jnp.zeros((1,), jnp.int32)])
        bounds = jnp.cumsum(counts)
        sorted_labels = jnp.sum((slot_ids[:, None] >= bounds[None, :]).astype(jnp.int32), axis=1)
        scramble = jax.random.permutation(keys[2], brick_count).astype(jnp.int32)
        labels = sorted_labels[scramble]
        offsets = jax.random.permutation(keys[3], peer_count).astype(jnp.int32)
        dest_slot = order[local_slot]
        dest_dev = (source_dev + offsets[labels[dest_slot]]) % peer_count
        dest_block = dest_dev // row_devices
        dest_row = dest_dev % row_devices
        slot_x = dest_slot // (CY * NZB)
        slot_y = dest_slot // NZB % CY
        slot_z = dest_slot % NZB
        return ((dest_row * CX + slot_x) * NY + dest_block * CY + slot_y) * NZB + slot_z
    view_keys = jax.random.split(key, VIEWS)
    return jax.vmap(one_view)(view_keys).astype(jnp.int32)


def touch_ends(array, key, least, high):
    index_at = [jax.random.randint(jax.random.fold_in(key, axis), (), 0, length) for axis, length in enumerate(array.shape)]
    longest = array.shape.index(max(array.shape))
    next_to = index_at[:longest] + [(index_at[longest] + 1) % array.shape[longest]] + index_at[longest + 1:]
    return array.at[tuple(index_at)].set(least).at[tuple(next_to)].set(high)


def level_of(rng, dims, shards, smallest, top_value):
    def one(position, shards_of):
        heights = jax.random.uniform(jax.random.fold_in(jax.random.fold_in(rng, 6), position), (shards_of,), jnp.float32, smallest / len(shards), top_value / len(shards))
        return jnp.repeat(jnp.exp(heights), dims[position] // shards_of).reshape((-1,) + (1,) * (len(dims) - position - 1))

    factor_of = one(*shards[0])
    for cut in shards[1:]:
        factor_of = factor_of * one(*cut)
    return factor_of


def setup_inputs(seed: int = 0) -> dict:
    streams_of = jax.random.split(jax.random.key(seed), 6)
    return {
        "estimate": jnp.clip(jnp.exp(math.log(2.0) - 1.3862944 * jax.random.uniform(streams_of[0], (NX, NY, NZ), jnp.float32) ** level_of(streams_of[0], (NX, NY, NZ), ((0, 8), (1, 8)), -0.2, 0.2)), 0.5, 2.0),
        "views_data": jnp.clip(jnp.exp(math.log(5.0) - 3.218876 * jax.random.uniform(streams_of[1], (VIEWS, NX, NY, NZ), jnp.float32) ** level_of(streams_of[1], (VIEWS, NX, NY, NZ), ((0, 4), (1, 8), (2, 8)), -0.2, 0.2)), 0.2, 5.0),
        "target": draw_target(jax.random.fold_in(streams_of[5], 71), 0),
        "psf_taps": jnp.clip(jnp.exp(math.log(1.0) - 1.609438 * jax.random.uniform(streams_of[3], (VIEWS, 3, 2 * HALO + 1), jnp.float32) ** level_of(streams_of[3], (VIEWS, 3, 2 * HALO + 1), ((0, 4),), -0.2, 0.2)), 0.2, 1.0),
        "shifts": touch_ends(jax.random.randint(streams_of[4], (VIEWS,), 0, BRICK), jax.random.fold_in(streams_of[4], 1), 0, BRICK - 1).astype(jnp.int32),
    }


def axis_blur(volume, weights, dim_index):
    length_along = volume.shape[dim_index]
    pad_shape = [(0, 0)] * volume.ndim
    pad_shape[dim_index] = (HALO, HALO)
    padded = jnp.pad(volume, pad_shape)
    result = jnp.zeros_like(volume)
    for offset in range(2 * HALO + 1):
        result = result + weights[offset] * lax.slice_in_dim(padded, offset, offset + length_along, axis=dim_index)
    return result


def blur_field(volume, weights):
    result = axis_blur(volume, weights[0], 0)
    result = axis_blur(result, weights[1], 1)
    return axis_blur(result, weights[2], 2)


def rotate_bricks(bricks, start_at):
    doubled = jnp.concatenate([bricks, bricks], axis=1)
    return lax.dynamic_slice_in_dim(doubled, start_at.astype(jnp.int32), BRICK, 1)


def reference(estimate, views_data, target, psf_taps, shifts):
    weights = psf_taps / jnp.sum(psf_taps, axis=2, keepdims=True)
    flipped = weights[:, :, ::-1]
    for iteration in range(ITERS):
        combined = jnp.zeros_like(estimate)
        for view_index in range(VIEWS):
            blurred = blur_field(estimate, weights[view_index]).reshape(NX * NY * NZB, BRICK)
            indices = target[view_index].reshape(-1).astype(jnp.int32)
            forward = jnp.take(blurred, indices, axis=0)
            predicted = rotate_bricks(forward, shifts[view_index])
            quotient = views_data[view_index].reshape(NX * NY * NZB, BRICK) / predicted
            returned_ratio = rotate_bricks(quotient, BRICK - shifts[view_index])
            placed = jnp.zeros_like(blurred).at[indices].set(returned_ratio)
            combined = combined + blur_field(placed.reshape(NX, NY, NZ), flipped[view_index])
        estimate = estimate * combined / VIEWS
    return estimate
```

```python
import jax
import jax.numpy as jnp
from jax import lax
from jax.sharding import PartitionSpec as P

BRICK = 128
HALO = 3
ITERS = 2


def with_halo(value, sides, width):
    for axis, dim in sides:
        count, length = (lax.axis_size(axis), value.shape[dim])
        up = [(i, (i + 1) % count) for i in range(count - 1)]
        down = [(j, i) for i, j in up]
        last = lax.slice_in_dim(value, length - width, length, axis=dim)
        leading = lax.slice_in_dim(value, 0, width, axis=dim)
        before = lax.ppermute(last, axis, up)
        after = lax.ppermute(leading, axis, down)
        value = jnp.concatenate([before, value, after], axis=dim)
    return value


def axis_blur(volume, weights, dim_index, length_along):
    result = jnp.zeros(
        volume.shape[:dim_index] + (length_along,) + volume.shape[dim_index + 1 :], jnp.float32
    )
    for offset in range(2 * HALO + 1):
        result = result + weights[offset] * lax.slice_in_dim(
            volume, offset, offset + length_along, axis=dim_index
        )
    return result


def blur_local(volume, weights):
    x_cells, y_cells, z_cells = volume.shape
    extended = with_halo(volume, (("rows", 0),), HALO)
    result = axis_blur(extended, weights[0], 0, x_cells)
    widened = with_halo(result, (("blocks", 1),), HALO)
    result = axis_blur(widened, weights[1], 1, y_cells)
    padded = jnp.pad(result, ((0, 0), (0, 0), (HALO, HALO)))
    return axis_blur(padded, weights[2], 2, z_cells)


def rotate_bricks(bricks, start_at):
    doubled = jnp.concatenate([bricks, bricks], axis=1)
    return lax.dynamic_slice_in_dim(doubled, start_at, BRICK, 1)


def send_to_blocks(buffer):
    result = lax.all_to_all(buffer, ("blocks", "rows"), split_axis=0, concat_axis=0, tiled=True)
    return result


def per_device(estimate, views_data, target, psf_taps, shifts):
    x_cells, y_cells, z_cells = estimate.shape
    block_count = lax.axis_size("blocks")
    row_count = lax.axis_size("rows")
    peer_count = block_count * row_count
    view_count = lax.axis_size("views")
    brick_cols = z_cells // BRICK
    brick_count = x_cells * y_cells * brick_cols
    capacity = 2 * brick_count // peer_count
    all_cols = y_cells * block_count
    targets = target.reshape(brick_count)
    brick_z = targets % brick_cols
    column = targets // brick_cols % all_cols
    row_line = targets // (brick_cols * all_cols)
    dest_dev = column // y_cells * row_count + row_line // x_cells
    dest_slot = (row_line % x_cells * y_cells + column % y_cells) * brick_cols + brick_z
    one_hot = (dest_dev[:, None] == jnp.arange(peer_count, dtype=jnp.int32)[None, :]).astype(
        jnp.int32
    )
    before = jnp.cumsum(one_hot, axis=0) - one_hot
    rank_in = jnp.sum(before * one_hot, axis=1)
    position = dest_dev * capacity + rank_in
    request_list = (
        jnp.full((peer_count * capacity,), brick_count, jnp.int32).at[position].set(dest_slot)
    )
    wanted = lax.all_to_all(
        request_list.reshape(peer_count, capacity),
        ("blocks", "rows"),
        split_axis=0,
        concat_axis=0,
        tiled=True,
    ).reshape(-1)
    weights = psf_taps[0] / jnp.sum(psf_taps[0], axis=1, keepdims=True)
    flipped = weights[:, ::-1]
    shift_by = shifts[0]
    observed = rotate_bricks(views_data.reshape(brick_count, BRICK), BRICK - shift_by)
    outgoing = (
        jnp.zeros((peer_count * capacity, BRICK), jnp.float32).at[position].set(observed)
    )
    arrived = send_to_blocks(outgoing.reshape(peer_count, capacity, BRICK))
    moved = (
        jnp.zeros((brick_count, BRICK), jnp.float32)
        .at[wanted]
        .set(arrived.reshape(peer_count * capacity, BRICK), mode="drop")
    ).reshape(x_cells, y_cells, z_cells)
    for iteration in range(ITERS):
        placed = moved / blur_local(estimate, weights)
        projected = blur_local(placed, flipped)
        combined = lax.psum(projected, "views")
        estimate = estimate * combined / view_count
    return estimate


def solution(mesh):
    placed = (
        P("rows", "blocks", None),
        P("views", "rows", "blocks", None),
        P("views", "rows", "blocks", None),
        P("views", None, None),
        P("views"),
    )
    return jax.shard_map(
        per_device, mesh=mesh, in_specs=placed, out_specs=P("rows", "blocks", None), check_vma=False
    )
```

```python
import functools
import jax
import jax.numpy as jnp
from jax import lax
from jax.experimental import pallas as pl
from jax.experimental.pallas import tpu as pltpu
from jax.sharding import PartitionSpec as P

VMEM = pltpu.VMEM
BRICK = 128
HALO = 3
ITERS = 2
UNROLL = 8


def with_halo(value, sides, width):
    for axis, dim in sides:
        count, length = (lax.axis_size(axis), value.shape[dim])
        up = [(i, (i + 1) % count) for i in range(count - 1)]
        down = [(j, i) for i, j in up]
        last = lax.slice_in_dim(value, length - width, length, axis=dim)
        leading = lax.slice_in_dim(value, 0, width, axis=dim)
        before = lax.ppermute(last, axis, up)
        after = lax.ppermute(leading, axis, down)
        value = jnp.concatenate([before, value, after], axis=dim)
    return value


def axis_blur(volume, weights, dim_index, length_along):
    result = jnp.zeros(
        volume.shape[:dim_index] + (length_along,) + volume.shape[dim_index + 1 :], jnp.float32
    )
    for offset in range(2 * HALO + 1):
        result = result + weights[offset] * lax.slice_in_dim(
            volume, offset, offset + length_along, axis=dim_index
        )
    return result


def blur_local(volume, weights):
    x_cells, y_cells, z_cells = volume.shape
    extended = with_halo(volume, (("rows", 0),), HALO)
    result = axis_blur(extended, weights[0], 0, x_cells)
    widened = with_halo(result, (("blocks", 1),), HALO)
    result = axis_blur(widened, weights[1], 1, y_cells)
    padded = jnp.pad(result, ((0, 0), (0, 0), (HALO, HALO)))
    return axis_blur(padded, weights[2], 2, z_cells)


def lane_sum(x):
    return jnp.sum(x, axis=1, keepdims=True)


def pack_kernel(geo, shift_ref, target_ref, views_ref, out_ref, rolled, pos_v, pos_s, sem):
    peers, cap, x_cells, y_cells, brick_cols, row_count, all_cols = geo
    groups = brick_cols * x_cells
    rows_per = cap + 1
    t = target_ref[...]
    bz = t % brick_cols
    column = t // brick_cols % all_cols
    line = t // (brick_cols * all_cols)
    dest = column // y_cells * row_count + line // x_cells
    slot = (bz * x_cells + line % x_cells) * y_cells + column % y_cells + 1
    high, low = slot // 64, slot % 64
    peer_id = lax.broadcasted_iota(jnp.int32, (peers, y_cells), 0)
    before = (
        lax.broadcasted_iota(jnp.int32, (y_cells, y_cells), 0)
        < lax.broadcasted_iota(jnp.int32, (y_cells, y_cells), 1)
    ).astype(jnp.bfloat16)
    kid = lax.broadcasted_iota(jnp.int32, (BRICK, y_cells), 0)
    carry = jnp.zeros((peers, 1), jnp.float32)
    listed = jnp.zeros((2 * peers, BRICK), jnp.float32)
    for g in range(groups):
        d = dest[g : g + 1, :]
        hot = d == peer_id
        hot_f = hot.astype(jnp.float32)
        ahead = jnp.dot(hot_f.astype(jnp.bfloat16), before, preferred_element_type=jnp.float32)
        ranks = jnp.sum(hot_f * (ahead + carry), axis=0, keepdims=True)
        carry = carry + lane_sum(hot_f)
        rank_i = ranks.astype(jnp.int32)
        pos_v[g : g + 1, :] = d * rows_per + rank_i
        h = hot_f * high[g : g + 1, :].astype(jnp.float32)
        l = hot_f * low[g : g + 1, :].astype(jnp.float32)
        both = jnp.concatenate([h, l], axis=0).astype(jnp.bfloat16)
        at = (rank_i == kid).astype(jnp.float32).astype(jnp.bfloat16)
        listed = listed + lax.dot_general(
            both, at, (((1,), (1,)), ((), ())), preferred_element_type=jnp.float32
        )
    copy = pltpu.make_async_copy(pos_v, pos_s, sem)
    copy.start()
    entries = 64.0 * listed[:peers] + listed[peers:]
    for p in range(peers):
        out_ref[p * rows_per + cap] = entries[p : p + 1, :]
    shift = shift_ref[0]
    for bz_i in range(brick_cols):
        for x in range(x_cells):
            rolled[bz_i * x_cells + x] = pltpu.roll(
                views_ref[x, :, bz_i * BRICK : (bz_i + 1) * BRICK], shift, 1
            )
    copy.wait()

    def body(i, c):
        g = i // (y_cells // UNROLL)
        base = i % (y_cells // UNROLL) * UNROLL
        for s in range(UNROLL):
            out_ref[pos_s[g, base + s]] = rolled[g, pl.ds(base + s, 1), :]
        return c

    lax.fori_loop(0, groups * y_cells // UNROLL, body, 0)


def pack(shift, target, views, geo):
    peers, cap, x_cells, y_cells, brick_cols, row_count, all_cols = geo
    groups = brick_cols * x_cells
    return pl.pallas_call(
        functools.partial(pack_kernel, geo),
        out_shape=jax.ShapeDtypeStruct((peers * (cap + 1), 1, BRICK), jnp.float32),
        in_specs=[
            pl.BlockSpec(memory_space=pltpu.SMEM),
            pl.BlockSpec(memory_space=pltpu.VMEM),
            pl.BlockSpec(memory_space=pltpu.VMEM),
        ],
        out_specs=pl.BlockSpec(memory_space=pltpu.VMEM),
        scratch_shapes=[
            pltpu.VMEM((groups, y_cells, BRICK), jnp.float32),
            pltpu.VMEM((groups, y_cells), jnp.int32),
            pltpu.SMEM((groups, y_cells), jnp.int32),
            pltpu.SemaphoreType.DMA,
        ],
        name="pack",
    )(shift, target, views)


def unpack_kernel(peers, cap, slots, in_ref, out_ref, list_v, idx_v, idx_s, sem):
    rows_per = cap + 1
    for p in range(peers):
        list_v[p : p + 1, :] = in_ref[p * rows_per + cap]
    e = list_v[...].astype(jnp.int32)
    count = jnp.sum((e > 0).astype(jnp.int32), axis=1, keepdims=True)
    idx_v[...] = jnp.where(
        lax.broadcasted_iota(jnp.int32, (peers, BRICK), 1) == cap,
        count,
        jnp.where(e > 0, e - 1, slots),
    )
    copy = pltpu.make_async_copy(idx_v, idx_s, sem)
    copy.start()
    copy.wait()

    def per_peer(p, c):
        def body(i, c):
            for s in range(UNROLL):
                k = i * UNROLL + s
                out_ref[pl.ds(idx_s[p, k], 1), :] = in_ref[p * rows_per + k]
            return c

        lax.fori_loop(0, (idx_s[p, cap] + UNROLL - 1) // UNROLL, body, 0)
        return c

    lax.fori_loop(0, peers, per_peer, 0)


def unpack(arrived, peers, cap, slots):
    return pl.pallas_call(
        functools.partial(unpack_kernel, peers, cap, slots),
        out_shape=jax.ShapeDtypeStruct((slots + UNROLL, BRICK), jnp.float32),
        in_specs=[pl.BlockSpec(memory_space=pltpu.VMEM)],
        out_specs=pl.BlockSpec(memory_space=pltpu.VMEM),
        scratch_shapes=[
            pltpu.VMEM((peers, BRICK), jnp.float32),
            pltpu.VMEM((peers, BRICK), jnp.int32),
            pltpu.SMEM((peers, BRICK), jnp.int32),
            pltpu.SemaphoreType.DMA,
        ],
        name="unpack",
    )(arrived)


def per_device(estimate, views_data, target, psf_taps, shifts):
    x_cells, y_cells, z_cells = estimate.shape
    row_count = lax.axis_size("rows")
    block_count = lax.axis_size("blocks")
    peer_count = block_count * row_count
    view_count = lax.axis_size("views")
    brick_cols = z_cells // BRICK
    brick_count = x_cells * y_cells * brick_cols
    capacity = 2 * brick_count // peer_count
    geo = (peer_count, capacity, x_cells, y_cells, brick_cols, row_count, y_cells * block_count)
    targets = target[0].transpose(2, 0, 1).reshape(brick_cols * x_cells, y_cells)
    outgoing = pack(shifts, targets, views_data[0], geo)
    arrived = lax.all_to_all(
        outgoing.reshape(peer_count, capacity + 1, 1, BRICK),
        ("blocks", "rows"), split_axis=0, concat_axis=0, tiled=True,
    ).reshape(peer_count * (capacity + 1), 1, BRICK)
    moved = unpack(arrived, peer_count, capacity, brick_count)[:brick_count]
    moved = (
        moved.reshape(brick_cols, x_cells, y_cells, BRICK)
        .transpose(1, 2, 0, 3)
        .reshape(x_cells, y_cells, z_cells)
    )
    weights = psf_taps[0] / jnp.sum(psf_taps[0], axis=1, keepdims=True)
    flipped = weights[:, ::-1]
    for iteration in range(ITERS):
        placed = moved / blur_local(estimate, weights)
        projected = blur_local(placed, flipped)
        combined = lax.psum(projected, "views")
        estimate = estimate * combined / view_count
    return estimate


def solution(mesh):
    placed = (
        P("rows", "blocks", None),
        P("views", "rows", "blocks", None),
        P("views", "rows", "blocks", None),
        P("views", None, None),
        P("views"),
    )
    return jax.shard_map(
        per_device, mesh=mesh, in_specs=placed, out_specs=P("rows", "blocks", None), check_vma=False
    )
```

```python
import functools
import jax
import jax.numpy as jnp
from jax import lax
from jax.experimental import pallas as pl
from jax.experimental.pallas import tpu as pltpu
from jax.sharding import PartitionSpec as P

VMEM = pltpu.VMEM
BRICK = 128
HALO = 3
ITERS = 2
UNROLL = 8
TAPS = 2 * HALO + 1
EDGE = 8
ROWS = 32


def lane_sum(x):
    return jnp.sum(x, axis=1, keepdims=True)


def pack_kernel(geo, shift_ref, target_ref, views_ref, out_ref, rolled, pos_v, pos_s, sem):
    peers, cap, x_cells, y_cells, brick_cols, row_count, all_cols = geo
    groups = brick_cols * x_cells
    rows_per = cap + 1
    t = target_ref[...]
    bz = t % brick_cols
    column = t // brick_cols % all_cols
    line = t // (brick_cols * all_cols)
    dest = column // y_cells * row_count + line // x_cells
    slot = (bz * x_cells + line % x_cells) * y_cells + column % y_cells + 1
    high, low = slot // 64, slot % 64
    peer_id = lax.broadcasted_iota(jnp.int32, (peers, y_cells), 0)
    before = (
        lax.broadcasted_iota(jnp.int32, (y_cells, y_cells), 0)
        < lax.broadcasted_iota(jnp.int32, (y_cells, y_cells), 1)
    ).astype(jnp.bfloat16)
    kid = lax.broadcasted_iota(jnp.int32, (BRICK, y_cells), 0)
    carry = jnp.zeros((peers, 1), jnp.float32)
    listed = jnp.zeros((2 * peers, BRICK), jnp.float32)
    for g in range(groups):
        d = dest[g : g + 1, :]
        hot = d == peer_id
        hot_f = hot.astype(jnp.float32)
        ahead = jnp.dot(hot_f.astype(jnp.bfloat16), before, preferred_element_type=jnp.float32)
        ranks = jnp.sum(hot_f * (ahead + carry), axis=0, keepdims=True)
        carry = carry + lane_sum(hot_f)
        rank_i = ranks.astype(jnp.int32)
        pos_v[g : g + 1, :] = d * rows_per + rank_i
        h = hot_f * high[g : g + 1, :].astype(jnp.float32)
        l = hot_f * low[g : g + 1, :].astype(jnp.float32)
        both = jnp.concatenate([h, l], axis=0).astype(jnp.bfloat16)
        at = (rank_i == kid).astype(jnp.float32).astype(jnp.bfloat16)
        listed = listed + lax.dot_general(
            both, at, (((1,), (1,)), ((), ())), preferred_element_type=jnp.float32
        )
    copy = pltpu.make_async_copy(pos_v, pos_s, sem)
    copy.start()
    entries = 64.0 * listed[:peers] + listed[peers:]
    for p in range(peers):
        out_ref[p * rows_per + cap] = entries[p : p + 1, :]
    shift = shift_ref[0]
    for bz_i in range(brick_cols):
        for x in range(x_cells):
            rolled[bz_i * x_cells + x] = pltpu.roll(
                views_ref[x, :, bz_i * BRICK : (bz_i + 1) * BRICK], shift, 1
            )
    copy.wait()

    def body(i, c):
        g = i // (y_cells // UNROLL)
        base = i % (y_cells // UNROLL) * UNROLL
        for s in range(UNROLL):
            out_ref[pos_s[g, base + s]] = rolled[g, pl.ds(base + s, 1), :]
        return c

    lax.fori_loop(0, groups * y_cells // UNROLL, body, 0)


def pack(shift, target, views, geo):
    peers, cap, x_cells, y_cells, brick_cols, row_count, all_cols = geo
    groups = brick_cols * x_cells
    return pl.pallas_call(
        functools.partial(pack_kernel, geo),
        out_shape=jax.ShapeDtypeStruct((peers * (cap + 1), 1, BRICK), jnp.float32),
        in_specs=[
            pl.BlockSpec(memory_space=pltpu.SMEM),
            pl.BlockSpec(memory_space=pltpu.VMEM),
            pl.BlockSpec(memory_space=pltpu.VMEM),
        ],
        out_specs=pl.BlockSpec(memory_space=pltpu.VMEM),
        scratch_shapes=[
            pltpu.VMEM((groups, y_cells, BRICK), jnp.float32),
            pltpu.VMEM((groups, y_cells), jnp.int32),
            pltpu.SMEM((groups, y_cells), jnp.int32),
            pltpu.SemaphoreType.DMA,
        ],
        name="pack",
    )(shift, target, views)


def unpack_kernel(peers, cap, slots, in_ref, out_ref, list_v, idx_v, idx_s, sem):
    rows_per = cap + 1
    for p in range(peers):
        list_v[p : p + 1, :] = in_ref[p * rows_per + cap]
    e = list_v[...].astype(jnp.int32)
    count = jnp.sum((e > 0).astype(jnp.int32), axis=1, keepdims=True)
    idx_v[...] = jnp.where(
        lax.broadcasted_iota(jnp.int32, (peers, BRICK), 1) == cap,
        count,
        jnp.where(e > 0, e - 1, slots),
    )
    copy = pltpu.make_async_copy(idx_v, idx_s, sem)
    copy.start()
    copy.wait()

    def per_peer(p, c):
        def body(i, c):
            for s in range(UNROLL):
                k = i * UNROLL + s
                out_ref[pl.ds(idx_s[p, k], 1), :] = in_ref[p * rows_per + k]
            return c

        lax.fori_loop(0, (idx_s[p, cap] + UNROLL - 1) // UNROLL, body, 0)
        return c

    lax.fori_loop(0, peers, per_peer, 0)


def unpack(arrived, peers, cap, slots):
    return pl.pallas_call(
        functools.partial(unpack_kernel, peers, cap, slots),
        out_shape=jax.ShapeDtypeStruct((slots + UNROLL, BRICK), jnp.float32),
        in_specs=[pl.BlockSpec(memory_space=pltpu.VMEM)],
        out_specs=pl.BlockSpec(memory_space=pltpu.VMEM),
        scratch_shapes=[
            pltpu.VMEM((peers, BRICK), jnp.float32),
            pltpu.VMEM((peers, BRICK), jnp.int32),
            pltpu.SMEM((peers, BRICK), jnp.int32),
            pltpu.SemaphoreType.DMA,
        ],
        name="unpack",
    )(arrived)


def vmem():
    return pl.BlockSpec(memory_space=pltpu.VMEM)


def smem():
    return pl.BlockSpec(memory_space=pltpu.SMEM)


def f32(*shape):
    return jax.ShapeDtypeStruct(shape, jnp.float32)


def call(kernel, name, outs, args, scalars=1, scratch=(), work=4_000_000):
    return pl.pallas_call(
        kernel,
        out_shape=outs,
        in_specs=[smem()] * scalars + [vmem()] * (len(args) - scalars),
        out_specs=[vmem()] * len(outs),
        scratch_shapes=list(scratch),
        cost_estimate=pl.CostEstimate(flops=work, bytes_accessed=work, transcendentals=0),
        compiler_params=pltpu.CompilerParams(vmem_limit_bytes=32 * 1024 * 1024),
        name=name,
    )(*args)


def taps_of(w_ref, dim, flip):
    return [w_ref[dim * TAPS + (TAPS - 1 - k if flip else k)] for k in range(TAPS)]


def blur_z(a, b, w):
    lane = lax.broadcasted_iota(jnp.int32, a.shape, 1)
    out_a, out_b = w[HALO] * a, w[HALO] * b
    for s in range(1, HALO + 1):
        keep = lane < BRICK - s
        ra, rb = pltpu.roll(a, BRICK - s, 1), pltpu.roll(b, BRICK - s, 1)
        out_a += w[HALO + s] * jnp.where(keep, ra, rb)
        out_b += w[HALO + s] * jnp.where(keep, rb, 0.0)
        fresh = lane < s
        la, lb = pltpu.roll(a, s, 1), pltpu.roll(b, s, 1)
        out_a += w[HALO - s] * jnp.where(fresh, 0.0, la)
        out_b += w[HALO - s] * jnp.where(fresh, la, lb)
    return out_a, out_b


def put_edges(field, first, last, x, y_cells):
    for c in range(2):
        first[c, x] = field[c, x, 0:EDGE, :]
        last[c, x] = field[c, x, y_cells - EDGE : y_cells, :]


def z_first_kernel(w_ref, est_ref, out_ref, first, last):
    x_cells, y_cells, _ = est_ref.shape
    w = taps_of(w_ref, 2, False)

    def body(x, carry):
        for y in range(0, y_cells, ROWS):
            at = pl.ds(y, ROWS)
            a, b = blur_z(est_ref[x, at, 0:BRICK], est_ref[x, at, BRICK : 2 * BRICK], w)
            out_ref[0, x, at, :] = a
            out_ref[1, x, at, :] = b
        put_edges(out_ref, first, last, x, y_cells)
        return carry

    lax.fori_loop(0, x_cells, body, 0)


def z_first(w, estimate):
    x, y, _ = estimate.shape
    outs = [f32(2, x, y, BRICK), f32(2, x, EDGE, BRICK), f32(2, x, EDGE, BRICK)]
    return call(z_first_kernel, "z_blur", outs, (w, estimate))


def z_pieces_kernel(views, w_ref, v_ref, *refs):
    pieces, (out_ref, first, last) = refs[: 2 * views], refs[2 * views :]
    depth, y_cells, _ = pieces[0].shape
    w = taps_of(w_ref, 2, False)
    for d in range(views):
        base = lax.rem(v_ref[0] + d, views) * depth

        def body(i, carry, d=d, base=base):
            for y in range(0, y_cells, ROWS):
                at = pl.ds(y, ROWS)
                a, b = blur_z(pieces[2 * d][i, at, :], pieces[2 * d + 1][i, at, :], w)
                out_ref[0, base + i, at, :] = a
                out_ref[1, base + i, at, :] = b
            put_edges(out_ref, first, last, base + i, y_cells)
            return carry

        lax.fori_loop(0, depth, body, 0)


def z_pieces(w, v, pieces):
    views = len(pieces) // 2
    depth, y, _ = pieces[0].shape
    x = views * depth
    outs = [f32(2, x, y, BRICK), f32(2, x, EDGE, BRICK), f32(2, x, EDGE, BRICK)]
    return call(
        functools.partial(z_pieces_kernel, views), "z_blur_pieces", outs, (w, v, *pieces), 2
    )


def y_kernel(flip, w_ref, in_ref, lo, hi, out_ref, first, last, wide):
    _, x_cells, y_cells, _ = in_ref.shape
    w = taps_of(w_ref, 1, flip)

    def body(x, carry):
        for c in range(2):
            wide[c, 0:EDGE, :] = lo[c, x]
            wide[c, pl.ds(EDGE, y_cells), :] = in_ref[c, x]
            wide[c, EDGE + y_cells : 2 * EDGE + y_cells, :] = hi[c, x]
            for y in range(0, y_cells, ROWS):
                total = w[0] * wide[c, pl.ds(EDGE - HALO + y, ROWS), :]
                for k in range(1, TAPS):
                    total += w[k] * wide[c, pl.ds(EDGE - HALO + k + y, ROWS), :]
                out_ref[c, x, pl.ds(y, ROWS), :] = total
        return carry

    lax.fori_loop(0, x_cells, body, 0)
    for c in range(2):
        for i in range(HALO):
            first[c, i] = out_ref[c, i]
            last[c, i] = out_ref[c, x_cells - HALO + i]


def y_blur(w, field, lo, hi, flip):
    _, x, y, _ = field.shape
    outs = [f32(2, x, y, BRICK), f32(2, HALO, y, BRICK), f32(2, HALO, y, BRICK)]
    return call(
        functools.partial(y_kernel, flip), "y_blur", outs, (w, field, lo, hi),
        scratch=[pltpu.VMEM((2, y + 2 * EDGE, BRICK), jnp.float32)],
    )


def x_layers(lo, field, hi, c, at):
    x_cells = field.shape[1]
    return (
        [lo[c, i, at, :] for i in range(HALO)]
        + [field[c, i, at, :] for i in range(x_cells)]
        + [hi[c, i, at, :] for i in range(HALO)]
    )


def weigh(layers, w):
    total = w[0] * layers[0]
    for k in range(1, TAPS):
        total += w[k] * layers[k]
    return total


def ratio_kernel(w_ref, field, lo, hi, obs, out_ref, first, last):
    _, x_cells, y_cells, _ = field.shape
    w = taps_of(w_ref, 0, False)
    u = taps_of(w_ref, 2, True)

    def body(t, carry):
        at = pl.ds(pl.multiple_of(t * EDGE, EDGE), EDGE)
        la, lb = x_layers(lo, field, hi, 0, at), x_layers(lo, field, hi, 1, at)
        for x in range(x_cells):
            rows = [
                obs[pl.ds(pl.multiple_of((c * x_cells + x) * y_cells + t * EDGE, EDGE), EDGE), :]
                for c in range(2)
            ]
            a, b = blur_z(
                rows[0] / weigh(la[x : x + TAPS], w), rows[1] / weigh(lb[x : x + TAPS], w), u
            )
            out_ref[0, x, at, :] = a
            out_ref[1, x, at, :] = b
        return carry

    lax.fori_loop(0, y_cells // EDGE, body, 0)
    for x in range(x_cells):
        put_edges(out_ref, first, last, x, y_cells)


def ratio(w, field, lo, hi, obs):
    _, x, y, _ = field.shape
    outs = [f32(2, x, y, BRICK), f32(2, x, EDGE, BRICK), f32(2, x, EDGE, BRICK)]
    return call(ratio_kernel, "ratio", outs, (w, field, lo, hi, obs), work=8_000_000)


def split_kernel(views, w_ref, v_ref, field, lo, hi, a2, b2, a1, b1, a3, b3, a0, b0, wide):
    _, x_cells, y_cells, _ = field.shape
    depth = x_cells // views
    w = taps_of(w_ref, 0, True)
    for c in range(2):
        for i in range(HALO):
            wide[c, i] = lo[c, i]
            wide[c, HALO + x_cells + i] = hi[c, i]
        for i in range(x_cells):
            wide[c, HALO + i] = field[c, i]
    outs = ((0, a0, b0), (1, a1, b1), (2, a2, b2), (3, a3, b3))
    for r, out_a, out_b in outs:
        base = lax.rem(v_ref[0] + r, views) * depth

        def body(t, carry, base=base, pair=(out_a, out_b)):
            at = pl.ds(pl.multiple_of(t * EDGE, EDGE), EDGE)
            for c in range(2):
                layers = [wide[c, base + i, at, :] for i in range(depth + 2 * HALO)]
                for i in range(depth):
                    pair[c][i, at, :] = weigh(layers[i : i + TAPS], w)
            return carry

        lax.fori_loop(0, y_cells // EDGE, body, 0, unroll=2)


def split(w, v, views, field, lo, hi):
    _, x, y, _ = field.shape
    outs = [f32(x // views, y, BRICK)] * 8
    return call(
        functools.partial(split_kernel, views), "x_blur_split", outs, (w, v, field, lo, hi), 2,
        scratch=[pltpu.VMEM((2, x + 2 * HALO, y, BRICK), jnp.float32)],
    )


def add_kernel(a, ra, b, rb, out_a, out_b):
    out_a[...] = a[...] + ra[...]
    out_b[...] = b[...] + rb[...]


def update_first_kernel(views, v_ref, est, a, a1, a2, b, b1, b2, out_a, out_b):
    depth = a.shape[0]
    base = v_ref[0] * depth
    for i in range(depth):
        row = est[base + i]
        out_a[i] = row[:, 0:BRICK] * (a[i] + a1[i] + a2[i]) / views
        out_b[i] = row[:, BRICK : 2 * BRICK] * (b[i] + b1[i] + b2[i]) / views


def update_kernel(views, est_a, est_b, a, a1, a2, b, b1, b2, out_a, out_b):
    out_a[...] = est_a[...] * (a[...] + a1[...] + a2[...]) / views
    out_b[...] = est_b[...] * (b[...] + b1[...] + b2[...]) / views


def join_kernel(views, v_ref, *refs):
    pieces, out_ref = refs[: 2 * views], refs[2 * views]
    depth = pieces[0].shape[0]
    for d in range(views):
        base = lax.rem(v_ref[0] + d, views) * depth
        for i in range(depth):
            out_ref[base + i, :, 0:BRICK] = pieces[2 * d][i]
            out_ref[base + i, :, BRICK : 2 * BRICK] = pieces[2 * d + 1][i]


def exchange(first, last, axis):
    count = lax.axis_size(axis)
    up = [(i, i + 1) for i in range(count - 1)]
    down = [(i + 1, i) for i in range(count - 1)]
    return lax.ppermute(last, axis, up), lax.ppermute(first, axis, down)


def turn(value, step, count):
    return lax.ppermute(value, "views", [(i, (i + step) % count) for i in range(count)])


def per_device(estimate, views_data, target, psf_taps, shifts):
    x_cells, y_cells, z_cells = estimate.shape
    row_count = lax.axis_size("rows")
    block_count = lax.axis_size("blocks")
    peer_count = block_count * row_count
    view_count = lax.axis_size("views")
    brick_cols = z_cells // BRICK
    brick_count = x_cells * y_cells * brick_cols
    capacity = 2 * brick_count // peer_count
    geo = (peer_count, capacity, x_cells, y_cells, brick_cols, row_count, y_cells * block_count)
    targets = target[0].transpose(2, 0, 1).reshape(brick_cols * x_cells, y_cells)
    outgoing = pack(shifts, targets, views_data[0], geo)
    arrived = lax.all_to_all(
        outgoing.reshape(peer_count, capacity + 1, 1, BRICK),
        ("blocks", "rows"), split_axis=0, concat_axis=0, tiled=True,
    ).reshape(peer_count * (capacity + 1), 1, BRICK)
    w = (psf_taps[0] / jnp.sum(psf_taps[0], axis=1, keepdims=True)).reshape(-1)
    v = lax.axis_index("views").astype(jnp.int32).reshape(1)
    depth = x_cells // view_count
    pair = [f32(depth, y_cells, BRICK)] * 2
    pieces = None
    for iteration in range(ITERS):
        if pieces is None:
            field, first, last = z_first(w, estimate)
        else:
            field, first, last = z_pieces(w, v, pieces)
        field, first, last = y_blur(w, field, *exchange(first, last, "blocks"), False)
        lo, hi = exchange(first, last, "rows")
        if pieces is None:
            moved = unpack(arrived, peer_count, capacity, brick_count)
        field, first, last = ratio(w, field, lo, hi, moved)
        field, first, last = y_blur(w, field, *exchange(first, last, "blocks"), True)
        lo, hi = exchange(first, last, "rows")
        a2, b2, a1, b1, a3, b3, a0, b0 = split(w, v, view_count, field, lo, hi)
        ra, rb = turn(a2, 1, view_count), turn(b2, -1, view_count)
        near_b, near_a = turn(b1, 1, view_count), turn(a3, -1, view_count)
        a1, b3 = call(add_kernel, "add", pair, (a1, ra, b3, rb), 0)
        far_a, far_b = turn(a1, 1, view_count), turn(b3, -1, view_count)
        sums = (a0, near_a, far_a, b0, near_b, far_b)
        if pieces is None:
            own = call(
                functools.partial(update_first_kernel, view_count), "update", pair,
                (v, estimate, *sums),
            )
        else:
            own = call(
                functools.partial(update_kernel, view_count), "update", pair,
                (*pieces[:2], *sums), 0,
            )
        prev_a, next_b = turn(own[0], 1, view_count), turn(own[1], -1, view_count)
        prev_b, next_a = turn(own[1], 1, view_count), turn(own[0], -1, view_count)
        far_a, far_b = turn(prev_a, 1, view_count), turn(next_b, -1, view_count)
        pieces = (*own, next_a, next_b, far_a, far_b, prev_a, prev_b)
    return call(
        functools.partial(join_kernel, view_count), "join", [f32(x_cells, y_cells, z_cells)],
        (v, *pieces),
    )[0]


def solution(mesh):
    placed = (
        P("rows", "blocks", None),
        P("views", "rows", "blocks", None),
        P("views", "rows", "blocks", None),
        P("views", None, None),
        P("views"),
    )
    return jax.shard_map(
        per_device, mesh=mesh, in_specs=placed, out_specs=P("rows", "blocks", None), check_vma=False
    )
```

```python
import functools
import jax
import jax.numpy as jnp
from jax import lax
from jax.experimental import pallas as pl
from jax.experimental.pallas import tpu as pltpu
from jax.sharding import PartitionSpec as P

VMEM = pltpu.VMEM
BRICK = 128
HALO = 3
ITERS = 2
GROUP = 16
SPARE = 8
TAPS = 2 * HALO + 1
TILE = 8
TRIM = 4
DEEP = 16
ROWS = 32


def lane_sum(x):
    return jnp.sum(x, axis=1, keepdims=True)


def pack_kernel(geo, shift_ref, target_ref, views_ref, out_ref, rolled, pos_v, pos_s, sem):
    peers, cap, x_cells, y_cells, brick_cols, row_count, all_cols = geo
    groups = brick_cols * x_cells
    rows_per = cap + 1
    t = target_ref[...]
    bz = t % brick_cols
    column = t // brick_cols % all_cols
    line = t // (brick_cols * all_cols)
    dest = column // y_cells * row_count + line // x_cells
    slot = (bz * x_cells + line % x_cells) * y_cells + column % y_cells + 1
    high, low = slot // 64, slot % 64
    peer_id = lax.broadcasted_iota(jnp.int32, (peers, y_cells), 0)
    before = (
        lax.broadcasted_iota(jnp.int32, (y_cells, y_cells), 0)
        < lax.broadcasted_iota(jnp.int32, (y_cells, y_cells), 1)
    ).astype(jnp.bfloat16)
    kid = lax.broadcasted_iota(jnp.int32, (BRICK, y_cells), 0)
    carry = jnp.zeros((peers, 1), jnp.float32)
    listed = jnp.zeros((2 * peers, BRICK), jnp.float32)
    for g in range(groups):
        d = dest[g : g + 1, :]
        hot = d == peer_id
        hot_f = hot.astype(jnp.float32)
        ahead = jnp.dot(hot_f.astype(jnp.bfloat16), before, preferred_element_type=jnp.float32)
        ranks = jnp.sum(hot_f * (ahead + carry), axis=0, keepdims=True)
        carry = carry + lane_sum(hot_f)
        rank_i = ranks.astype(jnp.int32)
        pos_v[g : g + 1, :] = d * rows_per + rank_i
        h = hot_f * high[g : g + 1, :].astype(jnp.float32)
        l = hot_f * low[g : g + 1, :].astype(jnp.float32)
        both = jnp.concatenate([h, l], axis=0).astype(jnp.bfloat16)
        at = (rank_i == kid).astype(jnp.float32).astype(jnp.bfloat16)
        listed = listed + lax.dot_general(
            both, at, (((1,), (1,)), ((), ())), preferred_element_type=jnp.float32
        )
    copy = pltpu.make_async_copy(pos_v, pos_s, sem)
    copy.start()
    entries = 64.0 * listed[:peers] + listed[peers:]
    for p in range(peers):
        out_ref[p * rows_per + cap] = entries[p : p + 1, :]
    shift = shift_ref[0]
    for bz_i in range(brick_cols):
        for x in range(x_cells):
            rolled[bz_i * x_cells + x] = pltpu.roll(
                views_ref[x, :, bz_i * BRICK : (bz_i + 1) * BRICK], shift, 1
            )
    copy.wait()

    def body(g, c):
        for base in range(0, y_cells, GROUP):
            places = [pos_s[g, base + i] for i in range(GROUP)]
            rows = [rolled[g, base + i : base + i + 1, :] for i in range(GROUP)]
            for place, row in zip(places, rows):
                out_ref[place] = row
        return c

    lax.fori_loop(0, groups, body, 0)


def pack(shift, target, views, geo):
    peers, cap, x_cells, y_cells, brick_cols, row_count, all_cols = geo
    groups = brick_cols * x_cells
    return pl.pallas_call(
        functools.partial(pack_kernel, geo),
        out_shape=jax.ShapeDtypeStruct((peers * (cap + 1), 1, BRICK), jnp.float32),
        in_specs=[
            pl.BlockSpec(memory_space=pltpu.SMEM),
            pl.BlockSpec(memory_space=pltpu.VMEM),
            pl.BlockSpec(memory_space=pltpu.VMEM),
        ],
        out_specs=pl.BlockSpec(memory_space=pltpu.VMEM),
        scratch_shapes=[
            pltpu.VMEM((groups, y_cells, BRICK), jnp.float32),
            pltpu.VMEM((groups, y_cells), jnp.int32),
            pltpu.SMEM((groups, y_cells), jnp.int32),
            pltpu.SemaphoreType.DMA,
        ],
        name="pack",
    )(shift, target, views)


def unpack_kernel(peers, cap, slots, in_ref, out_ref, list_v, idx_v, idx_s, sem):
    rows_per = cap + 1
    for p in range(peers):
        list_v[p : p + 1, :] = in_ref[p * rows_per + cap]
    e = list_v[...].astype(jnp.int32)
    idx_v[...] = jnp.where(e > 0, e - 1, slots)
    copy = pltpu.make_async_copy(idx_v, idx_s, sem)
    copy.start()
    copy.wait()

    def per_peer(p, c):
        for base in range(0, cap, GROUP):
            places = [idx_s[p, base + i] for i in range(GROUP)]
            rows = [in_ref[p * rows_per + base + i] for i in range(GROUP)]
            for place, row in zip(places, rows):
                out_ref[pl.ds(place, 1), :] = row
        return c

    lax.fori_loop(0, peers, per_peer, 0)


def unpack(arrived, peers, cap, slots):
    return pl.pallas_call(
        functools.partial(unpack_kernel, peers, cap, slots),
        out_shape=jax.ShapeDtypeStruct((slots + SPARE, BRICK), jnp.float32),
        in_specs=[pl.BlockSpec(memory_space=pltpu.VMEM)],
        out_specs=pl.BlockSpec(memory_space=pltpu.VMEM),
        scratch_shapes=[
            pltpu.VMEM((peers, BRICK), jnp.float32),
            pltpu.VMEM((peers, BRICK), jnp.int32),
            pltpu.SMEM((peers, BRICK), jnp.int32),
            pltpu.SemaphoreType.DMA,
        ],
        name="unpack",
    )(arrived)


def vmem():
    return pl.BlockSpec(memory_space=pltpu.VMEM)


def smem():
    return pl.BlockSpec(memory_space=pltpu.SMEM)


def f32(*shape):
    return jax.ShapeDtypeStruct(shape, jnp.float32)


def call(kernel, name, outs, args, scalars=1, scratch=(), work=4_000_000):
    return pl.pallas_call(
        kernel,
        out_shape=outs,
        in_specs=[smem()] * scalars + [vmem()] * (len(args) - scalars),
        out_specs=[vmem()] * len(outs),
        scratch_shapes=list(scratch),
        cost_estimate=pl.CostEstimate(flops=work, bytes_accessed=work, transcendentals=0),
        compiler_params=pltpu.CompilerParams(vmem_limit_bytes=32 * 1024 * 1024),
        name=name,
    )(*args)


def taps_of(w_ref, dim, flip):
    return [w_ref[dim * TAPS + (TAPS - 1 - k if flip else k)] for k in range(TAPS)]


def blur_z(a, b, w):
    lane = lax.broadcasted_iota(jnp.int32, a.shape, 1)
    out_a, out_b = w[HALO] * a, w[HALO] * b
    for s in range(1, HALO + 1):
        keep = lane < BRICK - s
        ra, rb = pltpu.roll(a, BRICK - s, 1), pltpu.roll(b, BRICK - s, 1)
        out_a += w[HALO + s] * jnp.where(keep, ra, rb)
        out_b += w[HALO + s] * jnp.where(keep, rb, 0.0)
        fresh = lane < s
        la, lb = pltpu.roll(a, s, 1), pltpu.roll(b, s, 1)
        out_a += w[HALO - s] * jnp.where(fresh, 0.0, la)
        out_b += w[HALO - s] * jnp.where(fresh, la, lb)
    return out_a, out_b


def row_parts(rows):
    return [(y, min(ROWS, rows - y)) for y in range(0, rows, ROWS)]


def z_first_kernel(w_ref, est_ref, lo, hi, out_ref):
    x_cells, y_cells, _ = est_ref.shape
    w = taps_of(w_ref, 2, False)
    spans = [(lo, 0, 0, DEEP), (hi, 0, DEEP + y_cells, DEEP)]
    spans += [(est_ref, y, DEEP + y, n) for y, n in row_parts(y_cells)]

    def body(x, carry):
        for ref, y, to, n in spans:
            a, b = blur_z(ref[x, y : y + n, 0:BRICK], ref[x, y : y + n, BRICK : 2 * BRICK], w)
            out_ref[0, x, to : to + n, :] = a
            out_ref[1, x, to : to + n, :] = b
        return carry

    lax.fori_loop(0, x_cells, body, 0)


def z_first(w, estimate, lo, hi):
    x, y, _ = estimate.shape
    return call(z_first_kernel, "z_blur", [f32(2, x, y + 2 * DEEP, BRICK)], (w, estimate, lo, hi))[0]


def z_pieces_kernel(views, w_ref, id_ref, *refs):
    pieces, out_ref = refs[: 2 * views], refs[2 * views]
    depth, y_cells, _ = pieces[0].shape
    w = taps_of(w_ref, 2, False)
    for d in range(views):
        base = lax.rem(id_ref[0] + d, views) * depth

        def body(i, carry, d=d, base=base):
            for y, n in row_parts(y_cells):
                at = pl.ds(y, n)
                a, b = blur_z(pieces[2 * d][i, at, :], pieces[2 * d + 1][i, at, :], w)
                out_ref[0, base + i, at, :] = a
                out_ref[1, base + i, at, :] = b
            return carry

        lax.fori_loop(0, depth, body, 0)


def z_pieces(w, ids, pieces):
    views = len(pieces) // 2
    depth, y, _ = pieces[0].shape
    return call(
        functools.partial(z_pieces_kernel, views), "z_blur_pieces",
        [f32(2, views * depth, y, BRICK)], (w, ids, *pieces), 2,
    )[0]


def y_kernel(flip, w_ref, id_ref, in_ref, out_ref, inner, outer):
    _, x_cells, y_cells, _ = out_ref.shape
    w = taps_of(w_ref, 1, flip)

    def body(x, carry):
        for c in range(2):
            for y, n in row_parts(y_cells):
                total = w[0] * in_ref[c, x, pl.ds(TRIM - HALO + y, n), :]
                for k in range(1, TAPS):
                    total += w[k] * in_ref[c, x, pl.ds(TRIM - HALO + k + y, n), :]
                out_ref[c, x, pl.ds(y, n), :] = total
        return carry

    lax.fori_loop(0, x_cells, body, 0)
    odd = id_ref[1]
    for c in range(2):
        for i in range(HALO):
            inner[c, i] = out_ref[c, (1 - odd) * (x_cells - HALO) + i]
            outer[c, i] = out_ref[c, odd * (x_cells - HALO) + i]


def y_blur(w, ids, field, flip):
    _, x, y, _ = field.shape
    y -= 2 * TRIM
    outs = [f32(2, x, y, BRICK), f32(2, HALO, y, BRICK), f32(2, HALO, y, BRICK)]
    field, inner, outer = call(
        functools.partial(y_kernel, flip), "y_blur", outs, (w, ids, field), 2
    )
    count = lax.axis_size("rows")
    links = [(i, i + 1) for i in range(1, count - 1, 2)]
    outer = lax.ppermute(outer, "rows", links + [(j, i) for i, j in links])
    inner = lax.ppermute(inner, "rows", [(i, i ^ 1) for i in range(count)])
    return field, inner, outer


def set_sides(id_ref, inner, outer, side):
    odd = id_ref[1]
    for c in range(2):
        for i in range(HALO):
            side[1 - odd, c, i] = inner[c, i]
            side[odd, c, i] = outer[c, i]


def sides(field):
    _, _, y, _ = field.shape
    return pltpu.VMEM((2, 2, HALO, y, BRICK), jnp.float32)


def x_layers(field, side, c, at):
    x_cells = field.shape[1]
    return (
        [side[0, c, i, at, :] for i in range(HALO)]
        + [field[c, i, at, :] for i in range(x_cells)]
        + [side[1, c, i, at, :] for i in range(HALO)]
    )


def weigh(layers, w):
    total = w[0] * layers[0]
    for k in range(1, TAPS):
        total += w[k] * layers[k]
    return total


def x_kernel(w_ref, id_ref, field, inner, outer, out_ref, side):
    _, x_cells, y_cells, _ = field.shape
    w = taps_of(w_ref, 0, False)
    set_sides(id_ref, inner, outer, side)

    def body(t, carry):
        at = pl.ds(pl.multiple_of(t * TILE, TILE), TILE)
        for c in range(2):
            layers = x_layers(field, side, c, at)
            for x in range(x_cells):
                out_ref[c, x, at, :] = weigh(layers[x : x + TAPS], w)
        return carry

    lax.fori_loop(0, y_cells // TILE, body, 0)


def x_blur(w, ids, field, inner, outer):
    return call(
        x_kernel, "x_blur", [f32(*field.shape)], (w, ids, field, inner, outer), 2,
        scratch=[sides(field)],
    )[0]


def inside(id_ref, y, shape):
    row = lax.broadcasted_iota(jnp.int32, shape, 0) + y
    return (row >= id_ref[2]) & (row < id_ref[3])


def edges_kernel(moved, first, last):
    _, x_cells, deep, _ = first.shape
    y_cells = (moved.shape[0] - SPARE) // (2 * x_cells)
    for c in range(2):
        for x in range(x_cells):
            at = (c * x_cells + x) * y_cells
            first[c, x] = moved[at : at + deep, :]
            last[c, x] = moved[at + y_cells - deep : at + y_cells, :]


def ratio_first_kernel(w_ref, id_ref, below, moved, lo, hi, out_ref, obs):
    _, x_cells, y_cells, _ = below.shape
    own = obs.shape[2] - 2 * DEEP
    u = taps_of(w_ref, 2, True)
    base = (own - y_cells) // 2

    def body(x, carry):
        for c in range(2):
            at = pl.multiple_of((c * x_cells + x) * own, own)
            obs[c, x, 0:DEEP, :] = lo[c, x]
            obs[c, x, DEEP : DEEP + own, :] = moved[pl.ds(at, own), :]
            obs[c, x, DEEP + own : 2 * DEEP + own, :] = hi[c, x]
        for y, n in row_parts(y_cells):
            ok = inside(id_ref, base + y, (n, BRICK))
            rows = [
                jnp.where(
                    ok, obs[c, x, DEEP + base + y : DEEP + base + y + n, :] / below[c, x, y : y + n, :], 0.0
                )
                for c in range(2)
            ]
            a, b = blur_z(*rows, u)
            out_ref[0, x, y : y + n, :] = a
            out_ref[1, x, y : y + n, :] = b
        return carry

    lax.fori_loop(0, x_cells, body, 0)


def ratio_kernel(w_ref, id_ref, field, inner, outer, obs, out_ref, side):
    _, x_cells, y_cells, _ = field.shape
    skip = (obs.shape[2] - y_cells) // 2
    w = taps_of(w_ref, 0, False)
    u = taps_of(w_ref, 2, True)
    set_sides(id_ref, inner, outer, side)

    def body(t, carry):
        start = pl.multiple_of(t * TILE, TILE)
        at = pl.ds(start, TILE)
        ok = inside(id_ref, start + skip - DEEP, (TILE, BRICK))
        la, lb = x_layers(field, side, 0, at), x_layers(field, side, 1, at)
        for x in range(x_cells):
            rows = [
                jnp.where(ok, obs[c, x, pl.ds(start + skip, TILE), :] / weigh(l[x : x + TAPS], w), 0.0)
                for c, l in ((0, la), (1, lb))
            ]
            a, b = blur_z(*rows, u)
            out_ref[0, x, at, :] = a
            out_ref[1, x, at, :] = b
        return carry

    lax.fori_loop(0, y_cells // TILE, body, 0)


def split_kernel(views, w_ref, id_ref, field, inner, outer, a2, b2, a1, b1, a3, b3, a0, b0, wide):
    _, x_cells, y_cells, _ = field.shape
    depth = x_cells // views
    w = taps_of(w_ref, 0, True)
    odd = id_ref[1]
    for c in range(2):
        for i in range(HALO):
            wide[c, (1 - odd) * (HALO + x_cells) + i] = inner[c, i]
            wide[c, odd * (HALO + x_cells) + i] = outer[c, i]
        for i in range(x_cells):
            wide[c, HALO + i] = field[c, i]
    outs = ((0, a0, b0), (1, a1, b1), (2, a2, b2), (3, a3, b3))
    for r, out_a, out_b in outs:
        base = lax.rem(id_ref[0] + r, views) * depth

        def body(t, carry, base=base, pair=(out_a, out_b)):
            at = pl.ds(pl.multiple_of(t * TILE, TILE), TILE)
            for c in range(2):
                layers = [wide[c, base + i, at, :] for i in range(depth + 2 * HALO)]
                for i in range(depth):
                    pair[c][i, at, :] = weigh(layers[i : i + TAPS], w)
            return carry

        lax.fori_loop(0, y_cells // TILE, body, 0, unroll=2)


def split(w, ids, views, field, inner, outer):
    _, x, y, _ = field.shape
    outs = [f32(x // views, y, BRICK)] * 8
    return call(
        functools.partial(split_kernel, views), "x_blur_split", outs,
        (w, ids, field, inner, outer), 2,
        scratch=[pltpu.VMEM((2, x + 2 * HALO, y, BRICK), jnp.float32)],
    )


def add_kernel(a, ra, b, rb, out_a, out_b):
    out_a[...] = a[...] + ra[...]
    out_b[...] = b[...] + rb[...]


def update_first_kernel(views, id_ref, est, lo, hi, a, a1, a2, b, b1, b2, out_a, out_b):
    depth, y_cells, _ = a.shape
    own = est.shape[1]
    side = (y_cells - own) // 2
    base = id_ref[0] * depth
    spans = ((lo, DEEP - side, 0, side), (est, 0, side, own), (hi, 0, side + own, side))
    for i in range(depth):
        for ref, y, to, n in spans:
            at = slice(to, to + n)
            row = ref[base + i, y : y + n, :]
            out_a[i, at, :] = row[:, 0:BRICK] * (a[i, at, :] + a1[i, at, :] + a2[i, at, :]) / views
            out_b[i, at, :] = (
                row[:, BRICK : 2 * BRICK] * (b[i, at, :] + b1[i, at, :] + b2[i, at, :]) / views
            )


def update_kernel(views, est_a, est_b, a, a1, a2, b, b1, b2, out_a, out_b):
    side = (est_a.shape[1] - a.shape[1]) // 2
    at = slice(side, side + a.shape[1])
    out_a[...] = est_a[:, at, :] * (a[...] + a1[...] + a2[...]) / views
    out_b[...] = est_b[:, at, :] * (b[...] + b1[...] + b2[...]) / views


def join_kernel(views, id_ref, *refs):
    pieces, out_ref = refs[: 2 * views], refs[2 * views]
    depth = pieces[0].shape[0]
    for d in range(views):
        base = lax.rem(id_ref[0] + d, views) * depth
        for i in range(depth):
            out_ref[base + i, :, 0:BRICK] = pieces[2 * d][i]
            out_ref[base + i, :, BRICK : 2 * BRICK] = pieces[2 * d + 1][i]


def exchange(first, last, axis):
    count = lax.axis_size(axis)
    up = [(i, i + 1) for i in range(count - 1)]
    down = [(i + 1, i) for i in range(count - 1)]
    return lax.ppermute(last, axis, up), lax.ppermute(first, axis, down)


def turn(value, step, count):
    return lax.ppermute(value, "views", [(i, (i + step) % count) for i in range(count)])


def per_device(estimate, views_data, target, psf_taps, shifts):
    x_cells, y_cells, z_cells = estimate.shape
    row_count = lax.axis_size("rows")
    block_count = lax.axis_size("blocks")
    peer_count = block_count * row_count
    view_count = lax.axis_size("views")
    brick_cols = z_cells // BRICK
    brick_count = x_cells * y_cells * brick_cols
    capacity = 2 * brick_count // peer_count
    geo = (peer_count, capacity, x_cells, y_cells, brick_cols, row_count, y_cells * block_count)
    est_lo, est_hi = exchange(estimate[:, :DEEP], estimate[:, y_cells - DEEP :], "blocks")
    targets = target[0].transpose(2, 0, 1).reshape(brick_cols * x_cells, y_cells)
    outgoing = pack(shifts, targets, views_data[0], geo)
    outgoing, est_lo, est_hi = lax.optimization_barrier((outgoing, est_lo, est_hi))
    arrived = lax.all_to_all(
        outgoing.reshape(peer_count, capacity + 1, 1, BRICK),
        ("blocks", "rows"), split_axis=0, concat_axis=0, tiled=True,
    ).reshape(peer_count * (capacity + 1), 1, BRICK)
    w = (psf_taps[0] / jnp.sum(psf_taps[0], axis=1, keepdims=True)).reshape(-1)
    block = lax.axis_index("blocks")
    ids = jnp.stack([
        lax.axis_index("views"),
        lax.axis_index("rows") % 2,
        jnp.where(block == 0, 0, -DEEP),
        jnp.where(block == block_count - 1, y_cells, y_cells + DEEP),
    ]).astype(jnp.int32)
    pieces = None
    for iteration in range(ITERS):
        if pieces is None:
            field = z_first(w, estimate, est_lo, est_hi)
            below = x_blur(w, ids, *y_blur(w, ids, field, False))
            moved = unpack(arrived, peer_count, capacity, brick_count)
            edge = f32(2, x_cells, DEEP, BRICK)
            lo, hi = exchange(*call(edges_kernel, "edges", [edge, edge], (moved,), 0), "blocks")
            field, obs = call(
                ratio_first_kernel, "ratio_first",
                [f32(*below.shape), f32(2, x_cells, y_cells + 2 * DEEP, BRICK)],
                (w, ids, below, moved, lo, hi), 2,
            )
        else:
            field, inner, outer = y_blur(w, ids, z_pieces(w, ids, pieces), False)
            field = call(
                ratio_kernel, "ratio", [f32(*field.shape)], (w, ids, field, inner, outer, obs), 2,
                scratch=[sides(field)],
            )[0]
        a2, b2, a1, b1, a3, b3, a0, b0 = split(w, ids, view_count, *y_blur(w, ids, field, True))
        pair = [f32(*a0.shape)] * 2
        ra, rb = turn(a2, 1, view_count), turn(b2, -1, view_count)
        near_b, near_a = turn(b1, 1, view_count), turn(a3, -1, view_count)
        a1, b3 = call(add_kernel, "add", pair, (a1, ra, b3, rb), 0)
        far_a, far_b = turn(a1, 1, view_count), turn(b3, -1, view_count)
        sums = (a0, near_a, far_a, b0, near_b, far_b)
        if pieces is None:
            own = call(
                functools.partial(update_first_kernel, view_count), "update_first", pair,
                (ids, estimate, est_lo, est_hi, *sums),
            )
        else:
            own = call(
                functools.partial(update_kernel, view_count), "update", pair,
                (*pieces[:2], *sums), 0,
            )
        prev_a, next_b = turn(own[0], 1, view_count), turn(own[1], -1, view_count)
        prev_b, next_a = turn(own[1], 1, view_count), turn(own[0], -1, view_count)
        far_a, far_b = turn(prev_a, 1, view_count), turn(next_b, -1, view_count)
        pieces = (*own, next_a, next_b, far_a, far_b, prev_a, prev_b)
    return call(
        functools.partial(join_kernel, view_count), "join", [f32(x_cells, y_cells, z_cells)],
        (ids, *pieces),
    )[0]


def solution(mesh):
    placed = (
        P("rows", "blocks", None),
        P("views", "rows", "blocks", None),
        P("views", "rows", "blocks", None),
        P("views", None, None),
        P("views"),
    )
    return jax.shard_map(
        per_device, mesh=mesh, in_specs=placed, out_specs=P("rows", "blocks", None), check_vma=False
    )
```

```python
import functools
import jax
import jax.numpy as jnp
from jax import lax
from jax.experimental import pallas as pl
from jax.experimental.pallas import tpu as pltpu
from jax.sharding import PartitionSpec as P

VMEM = pltpu.VMEM
BRICK = 128
HALO = 3
ITERS = 2
GROUP = 16
SPARE = 8
TAPS = 2 * HALO + 1
TILE = 8
TRIM = 4
DEEP = 16
ROWS = 32


def lane_sum(x):
    return jnp.sum(x, axis=1, keepdims=True)


def pack_kernel(geo, shift_ref, target_ref, views_ref, out_ref, rolled, pos_v, pos_s, sem):
    peers, cap, x_cells, y_cells, brick_cols, row_count, all_cols = geo
    groups = brick_cols * x_cells
    rows_per = cap + 1
    t = target_ref[...]
    bz = t % brick_cols
    column = t // brick_cols % all_cols
    line = t // (brick_cols * all_cols)
    dest = column // y_cells * row_count + line // x_cells
    slot = (bz * x_cells + line % x_cells) * y_cells + column % y_cells + 1
    high, low = slot // 64, slot % 64
    peer_id = lax.broadcasted_iota(jnp.int32, (peers, y_cells), 0)
    before = (
        lax.broadcasted_iota(jnp.int32, (y_cells, y_cells), 0)
        < lax.broadcasted_iota(jnp.int32, (y_cells, y_cells), 1)
    ).astype(jnp.bfloat16)
    kid = lax.broadcasted_iota(jnp.int32, (BRICK, y_cells), 0)
    carry = jnp.zeros((peers, 1), jnp.float32)
    listed = jnp.zeros((2 * peers, BRICK), jnp.float32)
    for g in range(groups):
        here = (g % x_cells, slice(g // x_cells, g // x_cells + 1))
        d = dest[here]
        hot = d == peer_id
        hot_f = hot.astype(jnp.float32)
        ahead = jnp.dot(hot_f.astype(jnp.bfloat16), before, preferred_element_type=jnp.float32)
        ranks = jnp.sum(hot_f * (ahead + carry), axis=0, keepdims=True)
        carry = carry + lane_sum(hot_f)
        rank_i = ranks.astype(jnp.int32)
        pos_v[g : g + 1, :] = d * rows_per + rank_i
        h = hot_f * high[here].astype(jnp.float32)
        l = hot_f * low[here].astype(jnp.float32)
        both = jnp.concatenate([h, l], axis=0).astype(jnp.bfloat16)
        at = (rank_i == kid).astype(jnp.float32).astype(jnp.bfloat16)
        listed = listed + lax.dot_general(
            both, at, (((1,), (1,)), ((), ())), preferred_element_type=jnp.float32
        )
    copy = pltpu.make_async_copy(pos_v, pos_s, sem)
    copy.start()
    entries = 64.0 * listed[:peers] + listed[peers:]
    for p in range(peers):
        out_ref[p * rows_per + cap] = entries[p : p + 1, :]
    shift = shift_ref[0]
    for bz_i in range(brick_cols):
        for x in range(x_cells):
            rolled[bz_i * x_cells + x] = pltpu.roll(
                views_ref[x, :, bz_i * BRICK : (bz_i + 1) * BRICK], shift, 1
            )
    copy.wait()

    def body(g, c):
        for base in range(0, y_cells, GROUP):
            places = [pos_s[g, base + i] for i in range(GROUP)]
            rows = [rolled[g, base + i : base + i + 1, :] for i in range(GROUP)]
            for place, row in zip(places, rows):
                out_ref[place] = row
        return c

    lax.fori_loop(0, groups, body, 0)


def pack(shift, target, views, geo):
    peers, cap, x_cells, y_cells, brick_cols, row_count, all_cols = geo
    groups = brick_cols * x_cells
    return pl.pallas_call(
        functools.partial(pack_kernel, geo),
        out_shape=jax.ShapeDtypeStruct((peers * (cap + 1), 1, BRICK), jnp.float32),
        in_specs=[
            pl.BlockSpec(memory_space=pltpu.SMEM),
            pl.BlockSpec(memory_space=pltpu.VMEM),
            pl.BlockSpec(memory_space=pltpu.VMEM),
        ],
        out_specs=pl.BlockSpec(memory_space=pltpu.VMEM),
        scratch_shapes=[
            pltpu.VMEM((groups, y_cells, BRICK), jnp.float32),
            pltpu.VMEM((groups, y_cells), jnp.int32),
            pltpu.SMEM((groups, y_cells), jnp.int32),
            pltpu.SemaphoreType.DMA,
        ],
        name="pack",
    )(shift, target, views)


def unpack_kernel(peers, cap, slots, id_ref, in_ref, out_ref, inner, outer, list_v, idx_v, idx_s, sem):
    rows_per = cap + 1
    for p in range(peers):
        list_v[p : p + 1, :] = in_ref[p * rows_per + cap]
    e = list_v[...].astype(jnp.int32)
    idx_v[...] = jnp.where(e > 0, e - 1, slots)
    copy = pltpu.make_async_copy(idx_v, idx_s, sem)
    copy.start()
    copy.wait()

    def per_peer(p, c):
        for base in range(0, cap, GROUP):
            places = [idx_s[p, base + i] for i in range(GROUP)]
            rows = [in_ref[p * rows_per + base + i] for i in range(GROUP)]
            for place, row in zip(places, rows):
                out_ref[pl.ds(place, 1), :] = row
        return c

    lax.fori_loop(0, peers, per_peer, 0)
    _, x_cells, deep, _ = inner.shape
    y_cells = slots // (2 * x_cells)
    odd = id_ref[4]
    for c in range(2):
        for x in range(x_cells):
            at = (c * x_cells + x) * y_cells
            near = pl.multiple_of(at + odd * (y_cells - deep), deep)
            far = pl.multiple_of(at + (1 - odd) * (y_cells - deep), deep)
            inner[c, x] = out_ref[pl.ds(far, deep), :]
            outer[c, x] = out_ref[pl.ds(near, deep), :]


def unpack(ids, arrived, peers, cap, x_cells, y_cells):
    slots = 2 * x_cells * y_cells
    edge = f32(2, x_cells, DEEP, BRICK)
    return call(
        functools.partial(unpack_kernel, peers, cap, slots), "unpack",
        [f32(slots + SPARE, BRICK), edge, edge], (ids, arrived),
        scratch=[
            pltpu.VMEM((peers, BRICK), jnp.float32),
            pltpu.VMEM((peers, BRICK), jnp.int32),
            pltpu.SMEM((peers, BRICK), jnp.int32),
            pltpu.SemaphoreType.DMA,
        ],
    )


def vmem():
    return pl.BlockSpec(memory_space=pltpu.VMEM)


def smem():
    return pl.BlockSpec(memory_space=pltpu.SMEM)


def f32(*shape):
    return jax.ShapeDtypeStruct(shape, jnp.float32)


def call(kernel, name, outs, args, scalars=1, scratch=(), work=1000):
    return pl.pallas_call(
        kernel,
        out_shape=outs,
        in_specs=[smem()] * scalars + [vmem()] * (len(args) - scalars),
        out_specs=[vmem()] * len(outs),
        scratch_shapes=list(scratch),
        cost_estimate=pl.CostEstimate(flops=work, bytes_accessed=work, transcendentals=0),
        compiler_params=pltpu.CompilerParams(vmem_limit_bytes=32 * 1024 * 1024),
        name=name,
    )(*args)


def taps_of(w_ref, dim, flip):
    return [w_ref[dim * TAPS + (TAPS - 1 - k if flip else k)] for k in range(TAPS)]


def blur_z(a, b, w):
    lane = lax.broadcasted_iota(jnp.int32, a.shape, 1)
    out_a, out_b = w[HALO] * a, w[HALO] * b
    for s in range(1, HALO + 1):
        keep = lane < BRICK - s
        ra, rb = pltpu.roll(a, BRICK - s, 1), pltpu.roll(b, BRICK - s, 1)
        out_a += w[HALO + s] * jnp.where(keep, ra, rb)
        out_b += w[HALO + s] * jnp.where(keep, rb, 0.0)
        fresh = lane < s
        la, lb = pltpu.roll(a, s, 1), pltpu.roll(b, s, 1)
        out_a += w[HALO - s] * jnp.where(fresh, 0.0, la)
        out_b += w[HALO - s] * jnp.where(fresh, la, lb)
    return out_a, out_b


def row_parts(rows):
    return [(y, min(ROWS, rows - y)) for y in range(0, rows, ROWS)]


def z_first_kernel(w_ref, est_ref, lo, hi, out_ref):
    x_cells, y_cells, _ = est_ref.shape
    w = taps_of(w_ref, 2, False)
    spans = [(lo, 0, 0, DEEP), (hi, 0, DEEP + y_cells, DEEP)]
    spans += [(est_ref, y, DEEP + y, n) for y, n in row_parts(y_cells)]

    def body(x, carry):
        for ref, y, to, n in spans:
            a, b = blur_z(ref[x, y : y + n, 0:BRICK], ref[x, y : y + n, BRICK : 2 * BRICK], w)
            out_ref[0, x, to : to + n, :] = a
            out_ref[1, x, to : to + n, :] = b
        return carry

    lax.fori_loop(0, x_cells, body, 0)


def z_first(w, estimate, lo, hi):
    x, y, _ = estimate.shape
    return call(z_first_kernel, "z_blur", [f32(2, x, y + 2 * DEEP, BRICK)], (w, estimate, lo, hi))[0]


def z_piece_kernel(w_ref, in_a, in_b, out_a, out_b):
    depth, y_cells, _ = in_a.shape
    w = taps_of(w_ref, 2, False)

    def body(i, carry):
        for y, n in row_parts(y_cells):
            at = pl.ds(y, n)
            out_a[i, at, :], out_b[i, at, :] = blur_z(in_a[i, at, :], in_b[i, at, :], w)
        return carry

    lax.fori_loop(0, depth, body, 0)


def z_piece(w, a, b):
    return call(z_piece_kernel, "z_piece", [f32(*a.shape)] * 2, (w, a, b))


def y_rows(ref, at, trim, w, y, n):
    total = w[0] * ref[(*at, pl.ds(trim - HALO + y, n))]
    for k in range(1, TAPS):
        total += w[k] * ref[(*at, pl.ds(trim - HALO + k + y, n))]
    return total


def put_layers(id_ref, field, inner, outer):
    x_cells = field.shape[1]
    odd = id_ref[1]
    for c in range(2):
        for i in range(HALO):
            inner[c, i] = field[c, (1 - odd) * (x_cells - HALO) + i]
            outer[c, i] = field[c, odd * (x_cells - HALO) + i]


def y_kernel(flip, trim, w_ref, id_ref, in_ref, out_ref, inner, outer):
    _, x_cells, y_cells, _ = out_ref.shape
    w = taps_of(w_ref, 1, flip)

    def body(x, carry):
        for c in range(2):
            for y, n in row_parts(y_cells):
                out_ref[c, x, pl.ds(y, n), :] = y_rows(in_ref, (c, x), trim, w, y, n)
        return carry

    lax.fori_loop(0, x_cells, body, 0)
    put_layers(id_ref, out_ref, inner, outer)


def y_pieces_kernel(views, w_ref, id_ref, *refs):
    pieces, (out_ref, inner, outer) = refs[: 2 * views], refs[2 * views :]
    depth = pieces[0].shape[0]
    w = taps_of(w_ref, 1, False)
    for d in range(views):
        base = lax.rem(id_ref[0] + d, views) * depth
        for c in range(2):
            for i in range(depth):
                for y, n in row_parts(out_ref.shape[2]):
                    out_ref[c, base + i, pl.ds(y, n), :] = y_rows(pieces[2 * d + c], (i,), TRIM, w, y, n)
    put_layers(id_ref, out_ref, inner, outer)


def swap_layers(field, inner, outer):
    count = lax.axis_size("rows")
    links = [(i, i + 1) for i in range(1, count - 1, 2)]
    outer = lax.ppermute(outer, "rows", links + [(j, i) for i, j in links])
    inner = lax.ppermute(inner, "rows", [(i, i ^ 1) for i in range(count)])
    return field, inner, outer


def swap_rows(inner, outer):
    count = lax.axis_size("blocks")
    links = [(i, i + 1) for i in range(1, count - 1, 2)]
    outer = lax.ppermute(outer, "blocks", links + [(j, i) for i, j in links])
    inner = lax.ppermute(inner, "blocks", [(i, i ^ 1) for i in range(count)])
    return inner, outer


def field_and_layers(x, y):
    return [f32(2, x, y, BRICK), f32(2, HALO, y, BRICK), f32(2, HALO, y, BRICK)]


def y_blur(w, ids, field, flip, trim):
    _, x, y, _ = field.shape
    return swap_layers(*call(
        functools.partial(y_kernel, flip, trim), "y_blur", field_and_layers(x, y - 2 * trim),
        (w, ids, field), 2,
    ))


def set_sides(id_ref, inner, outer, side):
    odd = id_ref[1]
    for c in range(2):
        for i in range(HALO):
            side[1 - odd, c, i] = inner[c, i]
            side[odd, c, i] = outer[c, i]


def sides(field):
    _, _, y, _ = field.shape
    return pltpu.VMEM((2, 2, HALO, y, BRICK), jnp.float32)


def x_layers(field, side, c, at):
    x_cells = field.shape[1]
    return (
        [side[0, c, i, at, :] for i in range(HALO)]
        + [field[c, i, at, :] for i in range(x_cells)]
        + [side[1, c, i, at, :] for i in range(HALO)]
    )


def weigh(layers, w):
    total = w[0] * layers[0]
    for k in range(1, TAPS):
        total += w[k] * layers[k]
    return total


def x_kernel(w_ref, id_ref, field, inner, outer, out_ref, side):
    _, x_cells, y_cells, _ = field.shape
    w = taps_of(w_ref, 0, False)
    set_sides(id_ref, inner, outer, side)

    def body(t, carry):
        at = pl.ds(pl.multiple_of(t * TILE, TILE), TILE)
        for c in range(2):
            layers = x_layers(field, side, c, at)
            for x in range(x_cells):
                out_ref[c, x, at, :] = weigh(layers[x : x + TAPS], w)
        return carry

    lax.fori_loop(0, y_cells // TILE, body, 0)


def x_blur(w, ids, field, inner, outer):
    return call(
        x_kernel, "x_blur", [f32(*field.shape)], (w, ids, field, inner, outer), 2,
        scratch=[sides(field)],
    )[0]


def inside(id_ref, y, shape):
    row = lax.broadcasted_iota(jnp.int32, shape, 0) + y
    return (row >= id_ref[2]) & (row < id_ref[3])


def ratio_own_kernel(w_ref, below, moved, out_ref):
    _, x_cells, own, _ = out_ref.shape
    u = taps_of(w_ref, 2, True)
    skip = (below.shape[2] - own) // 2

    def body(x, carry):
        for y, n in row_parts(own):
            rows = [
                moved[pl.ds(pl.multiple_of((c * x_cells + x) * own + y, TILE), n), :]
                / below[c, x, pl.ds(skip + y, n), :]
                for c in range(2)
            ]
            a, b = blur_z(*rows, u)
            out_ref[0, x, pl.ds(y, n), :] = a
            out_ref[1, x, pl.ds(y, n), :] = b
        return carry

    lax.fori_loop(0, x_cells, body, 0)


def rim_kernel(w_ref, id_ref, below, own_ref, inner, outer, out_ref, layers_in, layers_out, halo, strip):
    _, x_cells, own, _ = own_ref.shape
    u = taps_of(w_ref, 2, True)
    w = taps_of(w_ref, 1, True)
    skip = (below.shape[2] - own) // 2
    span = DEEP + 2 * TRIM
    odd = id_ref[4]
    for c in range(2):
        halo[1 - odd, c] = inner[c]
        halo[odd, c] = outer[c]
    sides = (
        (0, DEEP - skip, 0, -skip, 0, skip, 0),
        (1, 0, skip + own, own, skip, 0, own - skip),
    )

    def body(x, carry):
        for side, obs_at, below_at, row, here, there, rest in sides:
            ok = inside(id_ref, row, (skip, BRICK))
            rows = [
                jnp.where(
                    ok,
                    halo[side, c, x, obs_at : obs_at + skip, :]
                    / below[c, x, below_at : below_at + skip, :],
                    0.0,
                )
                for c in range(2)
            ]
            for c, value in enumerate(blur_z(*rows, u)):
                strip[c, here : here + skip, :] = value
                strip[c, there : there + skip, :] = own_ref[c, x, rest : rest + skip, :]
                out_ref[c, x, side * DEEP : (side + 1) * DEEP, :] = y_rows(strip, (c,), TRIM, w, 0, DEEP)
        return carry

    lax.fori_loop(0, x_cells, body, 0)
    put_layers(id_ref, out_ref, layers_in, layers_out)


def rim(w, ids, below, own, inner, outer):
    _, x, y, _ = own.shape
    skip = (below.shape[2] - y) // 2
    return swap_layers(*call(
        rim_kernel, "rim", field_and_layers(x, 2 * DEEP), (w, ids, below, own, inner, outer), 2,
        scratch=[
            pltpu.VMEM((2, 2, x, DEEP, BRICK), jnp.float32),
            pltpu.VMEM((2, 2 * skip, BRICK), jnp.float32),
        ],
    ))


def widen_kernel(id_ref, moved, inner, outer, obs):
    _, x_cells, rows, _ = obs.shape
    own = rows - 2 * DEEP
    odd = id_ref[4]
    for c in range(2):
        for x in range(x_cells):
            at = (c * x_cells + x) * own
            obs[c, x, DEEP : DEEP + own, :] = moved[at : at + own, :]
            low = pl.multiple_of((1 - odd) * (DEEP + own), DEEP)
            high = pl.multiple_of(odd * (DEEP + own), DEEP)
            obs[c, x, pl.ds(low, DEEP), :] = inner[c, x]
            obs[c, x, pl.ds(high, DEEP), :] = outer[c, x]


def ratio_kernel(w_ref, id_ref, field, inner, outer, obs, out_ref, side):
    _, x_cells, y_cells, _ = field.shape
    skip = (obs.shape[2] - y_cells) // 2
    w = taps_of(w_ref, 0, False)
    u = taps_of(w_ref, 2, True)
    set_sides(id_ref, inner, outer, side)

    def body(t, carry):
        start = pl.multiple_of(t * TILE, TILE)
        at = pl.ds(start, TILE)
        ok = inside(id_ref, start + skip - DEEP, (TILE, BRICK))
        la, lb = x_layers(field, side, 0, at), x_layers(field, side, 1, at)
        for x in range(x_cells):
            rows = [
                jnp.where(ok, obs[c, x, pl.ds(start + skip, TILE), :] / weigh(l[x : x + TAPS], w), 0.0)
                for c, l in ((0, la), (1, lb))
            ]
            a, b = blur_z(*rows, u)
            out_ref[0, x, at, :] = a
            out_ref[1, x, at, :] = b
        return carry

    lax.fori_loop(0, y_cells // TILE, body, 0)


def split_kernel(views, parts, w_ref, id_ref, *refs):
    fields, outs, wide = refs[: 3 * len(parts)], refs[3 * len(parts) : -1], refs[-1]
    x_cells = fields[0].shape[1]
    y_cells = wide.shape[2]
    depth = x_cells // views
    w = taps_of(w_ref, 0, True)
    odd = id_ref[1]
    for p, spans in enumerate(parts):
        field, inner, outer = fields[3 * p : 3 * p + 3]
        for y, to, n in spans:
            for c in range(2):
                for i in range(HALO):
                    wide[c, (1 - odd) * (HALO + x_cells) + i, to : to + n, :] = inner[c, i, y : y + n, :]
                    wide[c, odd * (HALO + x_cells) + i, to : to + n, :] = outer[c, i, y : y + n, :]
                for i in range(x_cells):
                    wide[c, HALO + i, to : to + n, :] = field[c, i, y : y + n, :]
    for r in range(views):
        base = lax.rem(id_ref[0] + r, views) * depth

        def body(t, carry, base=base, pair=outs[2 * r : 2 * r + 2]):
            at = pl.ds(pl.multiple_of(t * TILE, TILE), TILE)
            for c in range(2):
                layers = [wide[c, base + i, at, :] for i in range(depth + 2 * HALO)]
                for i in range(depth):
                    pair[c][i, at, :] = weigh(layers[i : i + TAPS], w)
            return carry

        lax.fori_loop(0, y_cells // TILE, body, 0, unroll=2)


def split(w, ids, views, fields, parts):
    x = fields[0].shape[1]
    y = sum(n for spans in parts for _, _, n in spans)
    outs = [f32(x // views, y, BRICK)] * (2 * views)
    return call(
        functools.partial(split_kernel, views, parts), "x_blur_split", outs, (w, ids, *fields), 2,
        scratch=[pltpu.VMEM((2, x + 2 * HALO, y, BRICK), jnp.float32)],
    )


def add_kernel(a, ra, b, rb, out_a, out_b):
    out_a[...] = a[...] + ra[...]
    out_b[...] = b[...] + rb[...]


def update_first_kernel(views, id_ref, est, lo, hi, a, a1, a2, b, b1, b2, out_a, out_b):
    depth, y_cells, _ = a.shape
    own = est.shape[1]
    side = (y_cells - own) // 2
    base = id_ref[0] * depth
    spans = ((lo, DEEP - side, 0, side), (est, 0, side, own), (hi, 0, side + own, side))
    for i in range(depth):
        for ref, y, to, n in spans:
            at = slice(to, to + n)
            row = ref[base + i, y : y + n, :]
            out_a[i, at, :] = row[:, 0:BRICK] * (a[i, at, :] + a1[i, at, :] + a2[i, at, :]) / views
            out_b[i, at, :] = (
                row[:, BRICK : 2 * BRICK] * (b[i, at, :] + b1[i, at, :] + b2[i, at, :]) / views
            )


def update_kernel(views, est_a, est_b, a, a1, a2, b, b1, b2, out_a, out_b):
    side = (est_a.shape[1] - a.shape[1]) // 2
    at = slice(side, side + a.shape[1])
    out_a[...] = est_a[:, at, :] * (a[...] + a1[...] + a2[...]) / views
    out_b[...] = est_b[:, at, :] * (b[...] + b1[...] + b2[...]) / views


def join_kernel(views, id_ref, *refs):
    pieces, out_ref, sems = refs[: 2 * views], refs[2 * views], refs[2 * views + 1]
    depth = pieces[0].shape[0]
    copies = []
    for d in range(views):
        base = lax.rem(id_ref[0] + d, views) * depth
        for c in range(2):
            part = out_ref.at[pl.ds(base, depth), :, pl.ds(c * BRICK, BRICK)]
            copies.append(pltpu.make_async_copy(pieces[2 * d + c], part, sems.at[2 * d + c]))
    for copy in copies:
        copy.start()
    for copy in copies:
        copy.wait()


def join(views, shape, ids, pieces):
    return pl.pallas_call(
        functools.partial(join_kernel, views),
        out_shape=f32(*shape),
        in_specs=[smem()] + [pl.BlockSpec(memory_space=pl.ANY)] * len(pieces),
        out_specs=pl.BlockSpec(memory_space=pl.ANY),
        scratch_shapes=[pltpu.SemaphoreType.DMA((len(pieces),))],
        name="join",
    )(ids, *pieces)


def turn(value, step, count):
    return lax.ppermute(value, "views", [(i, (i + step) % count) for i in range(count)])


def per_device(estimate, views_data, target, psf_taps, shifts):
    x_cells, y_cells, z_cells = estimate.shape
    row_count = lax.axis_size("rows")
    block_count = lax.axis_size("blocks")
    peer_count = block_count * row_count
    view_count = lax.axis_size("views")
    brick_cols = z_cells // BRICK
    brick_count = x_cells * y_cells * brick_cols
    capacity = 2 * brick_count // peer_count
    geo = (peer_count, capacity, x_cells, y_cells, brick_cols, row_count, y_cells * block_count)
    block, row = lax.axis_index("blocks"), lax.axis_index("rows")
    odd = block % 2
    sent = [
        lax.dynamic_slice_in_dim(estimate, at * (y_cells - DEEP), DEEP, 1) for at in (1 - odd, odd)
    ]
    est_in, est_out = swap_rows(*sent)
    targets = target[0].transpose(0, 2, 1)
    outgoing = pack(shifts, targets, views_data[0], geo)
    outgoing, est_in, est_out = lax.optimization_barrier((outgoing, est_in, est_out))
    est_lo = jnp.where(odd == 1, est_in, est_out)
    est_hi = jnp.where(odd == 1, est_out, est_in)
    arrived = lax.all_to_all(
        outgoing.reshape(peer_count, capacity + 1, 1, BRICK),
        ("blocks", "rows"), split_axis=0, concat_axis=0, tiled=True,
    ).reshape(peer_count * (capacity + 1), 1, BRICK)
    w = (psf_taps[0] / jnp.sum(psf_taps[0], axis=1, keepdims=True)).reshape(-1)
    ids = jnp.stack([
        lax.axis_index("views"),
        row % 2,
        jnp.where(block == 0, 0, -DEEP),
        jnp.where(block == block_count - 1, y_cells, y_cells + DEEP),
        odd,
    ]).astype(jnp.int32)
    pieces = None
    for iteration in range(ITERS):
        if pieces is None:
            field = z_first(w, estimate, est_lo, est_hi)
            below = x_blur(w, ids, *y_blur(w, ids, field, False, TRIM))
            arrived, below = lax.optimization_barrier((arrived, below))
            moved, inner, outer = unpack(ids, arrived, peer_count, capacity, x_cells, y_cells)
            inner, outer = swap_rows(inner, outer)
            own = call(
                ratio_own_kernel, "ratio_own", [f32(2, x_cells, y_cells, BRICK)], (w, below, moved)
            )[0]
            middle = y_blur(w, ids, own, True, TILE)
            ends = rim(w, ids, below, own, inner, outer)
            obs = call(
                widen_kernel, "widen", [f32(2, x_cells, y_cells + 2 * DEEP, BRICK)],
                (ids, moved, inner, outer),
            )[0]
            wider = y_cells + 2 * TILE
            parts = (((0, DEEP, wider - 2 * DEEP),), ((0, 0, DEEP), (DEEP, wider - DEEP, DEEP)))
            sent = split(w, ids, view_count, (*middle, *ends), parts)
        else:
            y = pieces[0].shape[1] - 2 * TRIM
            field, inner, outer = swap_layers(*call(
                functools.partial(y_pieces_kernel, view_count), "y_blur_pieces",
                field_and_layers(x_cells, y),
                (w, ids, *(z for d in range(view_count) for z in z_piece(w, *pieces[2 * d : 2 * d + 2]))),
                2,
            ))
            field = call(
                ratio_kernel, "ratio", [f32(*field.shape)], (w, ids, field, inner, outer, obs), 2,
                scratch=[sides(field)],
            )[0]
            sent = split(w, ids, view_count, y_blur(w, ids, field, True, TRIM), (((0, 0, y_cells),),))
        a0, b0, a1, b1, a2, b2, a3, b3 = sent
        pair = [f32(*a0.shape)] * 2
        ra, rb = turn(a2, 1, view_count), turn(b2, -1, view_count)
        near_b, near_a = turn(b1, 1, view_count), turn(a3, -1, view_count)
        a1, b3 = call(add_kernel, "add", pair, (a1, ra, b3, rb), 0)
        far_a, far_b = turn(a1, 1, view_count), turn(b3, -1, view_count)
        sums = (a0, near_a, far_a, b0, near_b, far_b)
        if pieces is None:
            own = call(
                functools.partial(update_first_kernel, view_count), "update_first", pair,
                (ids, estimate, est_lo, est_hi, *sums),
            )
        else:
            own = call(
                functools.partial(update_kernel, view_count), "update", pair,
                (*pieces[:2], *sums), 0,
            )
        prev_a, next_b = turn(own[0], 1, view_count), turn(own[1], -1, view_count)
        prev_b, next_a = turn(own[1], 1, view_count), turn(own[0], -1, view_count)
        far_a, far_b = turn(prev_a, 1, view_count), turn(next_b, -1, view_count)
        pieces = (*own, next_a, next_b, far_a, far_b, prev_a, prev_b)
    return join(view_count, estimate.shape, ids, pieces)


def solution(mesh):
    placed = (
        P("rows", "blocks", None),
        P("views", "rows", "blocks", None),
        P("views", "rows", "blocks", None),
        P("views", None, None),
        P("views"),
    )
    return jax.shard_map(
        per_device, mesh=mesh, in_specs=placed, out_specs=P("rows", "blocks", None), check_vma=False
    )
```

```python
import functools
import jax
import jax.numpy as jnp
from jax import lax
from jax.experimental import pallas as pl
from jax.experimental.pallas import tpu as pltpu
from jax.sharding import PartitionSpec as P

VMEM = pltpu.VMEM
BRICK = 128
HALO = 3
ITERS = 2
GROUP = 16
SPARE = 8
TAPS = 2 * HALO + 1
TILE = 8
TRIM = 4
DEEP = 16
ROWS = 32


def lane_sum(x):
    return jnp.sum(x, axis=1, keepdims=True)


def pack_kernel(geo, shift_ref, target_ref, views_ref, out_ref, rolled, pos_v, pos_s, sem):
    peers, cap, x_cells, y_cells, brick_cols, row_count, all_cols = geo
    groups = brick_cols * x_cells
    rows_per = cap + 1
    t = target_ref[...]
    bz = t % brick_cols
    column = t // brick_cols % all_cols
    line = t // (brick_cols * all_cols)
    dest = column // y_cells * row_count + line // x_cells
    slot = (bz * x_cells + line % x_cells) * y_cells + column % y_cells + 1
    high, low = slot // 64, slot % 64
    peer_id = lax.broadcasted_iota(jnp.int32, (peers, y_cells), 0)
    before = (
        lax.broadcasted_iota(jnp.int32, (y_cells, y_cells), 0)
        < lax.broadcasted_iota(jnp.int32, (y_cells, y_cells), 1)
    ).astype(jnp.bfloat16)
    kid = lax.broadcasted_iota(jnp.int32, (BRICK, y_cells), 0)
    carry = jnp.zeros((peers, 1), jnp.float32)
    listed = jnp.zeros((2 * peers, BRICK), jnp.float32)
    for g in range(groups):
        here = (g % x_cells, slice(g // x_cells, g // x_cells + 1))
        d = dest[here]
        hot = d == peer_id
        hot_f = hot.astype(jnp.float32)
        ahead = jnp.dot(hot_f.astype(jnp.bfloat16), before, preferred_element_type=jnp.float32)
        ranks = jnp.sum(hot_f * (ahead + carry), axis=0, keepdims=True)
        carry = carry + lane_sum(hot_f)
        rank_i = ranks.astype(jnp.int32)
        pos_v[g : g + 1, :] = d * rows_per + rank_i
        h = hot_f * high[here].astype(jnp.float32)
        l = hot_f * low[here].astype(jnp.float32)
        both = jnp.concatenate([h, l], axis=0).astype(jnp.bfloat16)
        at = (rank_i == kid).astype(jnp.float32).astype(jnp.bfloat16)
        listed = listed + lax.dot_general(
            both, at, (((1,), (1,)), ((), ())), preferred_element_type=jnp.float32
        )
    copy = pltpu.make_async_copy(pos_v, pos_s, sem)
    copy.start()
    entries = 64.0 * listed[:peers] + listed[peers:]
    for p in range(peers):
        out_ref[p * rows_per + cap] = entries[p : p + 1, :]
    shift = shift_ref[0]
    for bz_i in range(brick_cols):
        for x in range(x_cells):
            rolled[bz_i * x_cells + x] = pltpu.roll(
                views_ref[x, :, bz_i * BRICK : (bz_i + 1) * BRICK], shift, 1
            )
    copy.wait()

    def body(g, c):
        for base in range(0, y_cells, GROUP):
            places = [pos_s[g, base + i] for i in range(GROUP)]
            rows = [rolled[g, base + i : base + i + 1, :] for i in range(GROUP)]
            for place, row in zip(places, rows):
                out_ref[place] = row
        return c

    lax.fori_loop(0, groups, body, 0)


def pack(shift, target, views, geo):
    peers, cap, x_cells, y_cells, brick_cols, row_count, all_cols = geo
    groups = brick_cols * x_cells
    return pl.pallas_call(
        functools.partial(pack_kernel, geo),
        out_shape=jax.ShapeDtypeStruct((peers * (cap + 1), 1, BRICK), jnp.float32),
        in_specs=[
            pl.BlockSpec(memory_space=pltpu.SMEM),
            pl.BlockSpec(memory_space=pltpu.VMEM),
            pl.BlockSpec(memory_space=pltpu.VMEM),
        ],
        out_specs=pl.BlockSpec(memory_space=pltpu.VMEM),
        scratch_shapes=[
            pltpu.VMEM((groups, y_cells, BRICK), jnp.float32),
            pltpu.VMEM((groups, y_cells), jnp.int32),
            pltpu.SMEM((groups, y_cells), jnp.int32),
            pltpu.SemaphoreType.DMA,
        ],
        name="pack",
    )(shift, target, views)


def unpack_kernel(peers, cap, slots, id_ref, in_ref, out_ref, inner, outer, list_v, idx_v, idx_s, sem):
    rows_per = cap + 1
    for p in range(peers):
        list_v[p : p + 1, :] = in_ref[p * rows_per + cap]
    e = list_v[...].astype(jnp.int32)
    idx_v[...] = jnp.where(e > 0, e - 1, slots)
    copy = pltpu.make_async_copy(idx_v, idx_s, sem)
    copy.start()
    copy.wait()

    def per_peer(p, c):
        for base in range(0, cap, GROUP):
            places = [idx_s[p, base + i] for i in range(GROUP)]
            rows = [in_ref[p * rows_per + base + i] for i in range(GROUP)]
            for place, row in zip(places, rows):
                out_ref[pl.ds(place, 1), :] = row
        return c

    lax.fori_loop(0, peers, per_peer, 0)
    _, x_cells, deep, _ = inner.shape
    y_cells = slots // (2 * x_cells)
    odd = id_ref[4]
    for c in range(2):
        for x in range(x_cells):
            at = (c * x_cells + x) * y_cells
            near = pl.multiple_of(at + odd * (y_cells - deep), deep)
            far = pl.multiple_of(at + (1 - odd) * (y_cells - deep), deep)
            inner[c, x] = out_ref[pl.ds(far, deep), :]
            outer[c, x] = out_ref[pl.ds(near, deep), :]


def unpack(ids, arrived, peers, cap, x_cells, y_cells):
    slots = 2 * x_cells * y_cells
    edge = f32(2, x_cells, DEEP, BRICK)
    return call(
        functools.partial(unpack_kernel, peers, cap, slots), "unpack",
        [f32(slots + SPARE, BRICK), edge, edge], (ids, arrived),
        scratch=[
            pltpu.VMEM((peers, BRICK), jnp.float32),
            pltpu.VMEM((peers, BRICK), jnp.int32),
            pltpu.SMEM((peers, BRICK), jnp.int32),
            pltpu.SemaphoreType.DMA,
        ],
    )


def vmem():
    return pl.BlockSpec(memory_space=pltpu.VMEM)


def smem():
    return pl.BlockSpec(memory_space=pltpu.SMEM)


def f32(*shape):
    return jax.ShapeDtypeStruct(shape, jnp.float32)


def call(kernel, name, outs, args, scalars=1, scratch=(), work=1000):
    return pl.pallas_call(
        kernel,
        out_shape=outs,
        in_specs=[smem()] * scalars + [vmem()] * (len(args) - scalars),
        out_specs=[vmem()] * len(outs),
        scratch_shapes=list(scratch),
        cost_estimate=pl.CostEstimate(flops=work, bytes_accessed=work, transcendentals=0),
        compiler_params=pltpu.CompilerParams(vmem_limit_bytes=32 * 1024 * 1024),
        name=name,
    )(*args)


def taps_of(w_ref, dim, flip):
    return [w_ref[dim * TAPS + (TAPS - 1 - k if flip else k)] for k in range(TAPS)]


def blur_z(a, b, w):
    lane = lax.broadcasted_iota(jnp.int32, a.shape, 1)
    out_a, out_b = w[HALO] * a, w[HALO] * b
    for s in range(1, HALO + 1):
        keep = lane < BRICK - s
        ra, rb = pltpu.roll(a, BRICK - s, 1), pltpu.roll(b, BRICK - s, 1)
        out_a += w[HALO + s] * jnp.where(keep, ra, rb)
        out_b += w[HALO + s] * jnp.where(keep, rb, 0.0)
        fresh = lane < s
        la, lb = pltpu.roll(a, s, 1), pltpu.roll(b, s, 1)
        out_a += w[HALO - s] * jnp.where(fresh, 0.0, la)
        out_b += w[HALO - s] * jnp.where(fresh, la, lb)
    return out_a, out_b


def row_parts(rows):
    return [(y, min(ROWS, rows - y)) for y in range(0, rows, ROWS)]


def z_first_kernel(w_ref, est_ref, lo, hi, out_ref):
    x_cells, y_cells, _ = est_ref.shape
    w = taps_of(w_ref, 2, False)
    spans = [(lo, 0, 0, DEEP), (hi, 0, DEEP + y_cells, DEEP)]
    spans += [(est_ref, y, DEEP + y, n) for y, n in row_parts(y_cells)]

    def body(x, carry):
        for ref, y, to, n in spans:
            a, b = blur_z(ref[x, y : y + n, 0:BRICK], ref[x, y : y + n, BRICK : 2 * BRICK], w)
            out_ref[0, x, to : to + n, :] = a
            out_ref[1, x, to : to + n, :] = b
        return carry

    lax.fori_loop(0, x_cells, body, 0)


def z_first(w, estimate, lo, hi):
    x, y, _ = estimate.shape
    return call(z_first_kernel, "z_blur", [f32(2, x, y + 2 * DEEP, BRICK)], (w, estimate, lo, hi))[0]


def z_piece_kernel(w_ref, in_a, in_b, out_a, out_b):
    depth, y_cells, _ = in_a.shape
    w = taps_of(w_ref, 2, False)

    def body(i, carry):
        for y, n in row_parts(y_cells):
            at = pl.ds(y, n)
            out_a[i, at, :], out_b[i, at, :] = blur_z(in_a[i, at, :], in_b[i, at, :], w)
        return carry

    lax.fori_loop(0, depth, body, 0)


def z_piece(w, a, b):
    return call(z_piece_kernel, "z_piece", [f32(*a.shape)] * 2, (w, a, b))


def y_rows(ref, at, trim, w, y, n):
    total = w[0] * ref[(*at, pl.ds(trim - HALO + y, n))]
    for k in range(1, TAPS):
        total += w[k] * ref[(*at, pl.ds(trim - HALO + k + y, n))]
    return total


def put_layers(id_ref, field, inner, outer):
    x_cells = field.shape[1]
    odd = id_ref[1]
    for c in range(2):
        for i in range(HALO):
            inner[c, i] = field[c, (1 - odd) * (x_cells - HALO) + i]
            outer[c, i] = field[c, odd * (x_cells - HALO) + i]


def y_kernel(flip, trim, w_ref, id_ref, in_ref, out_ref, *layers):
    _, x_cells, y_cells, _ = out_ref.shape
    w = taps_of(w_ref, 1, flip)

    def body(x, carry):
        for c in range(2):
            for y, n in row_parts(y_cells):
                out_ref[c, x, pl.ds(y, n), :] = y_rows(in_ref, (c, x), trim, w, y, n)
        return carry

    lax.fori_loop(0, x_cells, body, 0)
    if layers:
        put_layers(id_ref, out_ref, *layers)


def y_pieces_kernel(views, w_ref, id_ref, *refs):
    pieces, (out_ref, inner, outer) = refs[: 2 * views], refs[2 * views :]
    depth = pieces[0].shape[0]
    w = taps_of(w_ref, 1, False)
    for d in range(views):
        base = lax.rem(id_ref[0] + d, views) * depth
        for c in range(2):
            for i in range(depth):
                for y, n in row_parts(out_ref.shape[2]):
                    out_ref[c, base + i, pl.ds(y, n), :] = y_rows(pieces[2 * d + c], (i,), TRIM, w, y, n)
    put_layers(id_ref, out_ref, inner, outer)


def swap_layers(field, inner, outer):
    count = lax.axis_size("rows")
    links = [(i, i + 1) for i in range(1, count - 1, 2)]
    outer = lax.ppermute(outer, "rows", links + [(j, i) for i, j in links])
    inner = lax.ppermute(inner, "rows", [(i, i ^ 1) for i in range(count)])
    return field, inner, outer


def swap_rows(inner, outer):
    count = lax.axis_size("blocks")
    links = [(i, i + 1) for i in range(1, count - 1, 2)]
    outer = lax.ppermute(outer, "blocks", links + [(j, i) for i, j in links])
    inner = lax.ppermute(inner, "blocks", [(i, i ^ 1) for i in range(count)])
    return inner, outer


def field_and_layers(x, y):
    return [f32(2, x, y, BRICK), f32(2, HALO, y, BRICK), f32(2, HALO, y, BRICK)]


def y_blur(w, ids, field, flip, trim):
    _, x, y, _ = field.shape
    return swap_layers(*call(
        functools.partial(y_kernel, flip, trim), "y_blur", field_and_layers(x, y - 2 * trim),
        (w, ids, field), 2,
    ))


def set_sides(id_ref, inner, outer, side):
    odd = id_ref[1]
    for c in range(2):
        for i in range(HALO):
            side[1 - odd, c, i] = inner[c, i]
            side[odd, c, i] = outer[c, i]


def sides(field):
    _, _, y, _ = field.shape
    return pltpu.VMEM((2, 2, HALO, y, BRICK), jnp.float32)


def x_layers(field, side, c, at):
    x_cells = field.shape[1]
    return (
        [side[0, c, i, at, :] for i in range(HALO)]
        + [field[c, i, at, :] for i in range(x_cells)]
        + [side[1, c, i, at, :] for i in range(HALO)]
    )


def weigh(layers, w):
    total = w[0] * layers[0]
    for k in range(1, TAPS):
        total += w[k] * layers[k]
    return total


def x_kernel(w_ref, id_ref, field, inner, outer, out_ref, side):
    _, x_cells, y_cells, _ = field.shape
    w = taps_of(w_ref, 0, False)
    set_sides(id_ref, inner, outer, side)

    def body(t, carry):
        at = pl.ds(pl.multiple_of(t * TILE, TILE), TILE)
        for c in range(2):
            layers = x_layers(field, side, c, at)
            for x in range(x_cells):
                out_ref[c, x, at, :] = weigh(layers[x : x + TAPS], w)
        return carry

    lax.fori_loop(0, y_cells // TILE, body, 0)


def x_blur(w, ids, field, inner, outer):
    return call(
        x_kernel, "x_blur", [f32(*field.shape)], (w, ids, field, inner, outer), 2,
        scratch=[sides(field)],
    )[0]


def inside(id_ref, y, shape):
    row = lax.broadcasted_iota(jnp.int32, shape, 0) + y
    return (row >= id_ref[2]) & (row < id_ref[3])


def ratio_own_kernel(w_ref, below, moved, out_ref):
    _, x_cells, own, _ = out_ref.shape
    u = taps_of(w_ref, 2, True)
    skip = (below.shape[2] - own) // 2

    def body(x, carry):
        for y, n in row_parts(own):
            rows = [
                moved[pl.ds(pl.multiple_of((c * x_cells + x) * own + y, TILE), n), :]
                / below[c, x, pl.ds(skip + y, n), :]
                for c in range(2)
            ]
            a, b = blur_z(*rows, u)
            out_ref[0, x, pl.ds(y, n), :] = a
            out_ref[1, x, pl.ds(y, n), :] = b
        return carry

    lax.fori_loop(0, x_cells, body, 0)


def rim_kernel(w_ref, id_ref, below, own_ref, middle, inner, outer, out_ref, *scratch):
    _, x_cells, own, _ = own_ref.shape
    layers_in, layers_out, halo, strip = scratch
    u = taps_of(w_ref, 2, True)
    w = taps_of(w_ref, 1, True)
    rows_out = out_ref.shape[2]
    skip = (below.shape[2] - own) // 2
    span = DEEP + 2 * TRIM
    odd = id_ref[4]
    for c in range(2):
        halo[1 - odd, c] = inner[c]
        halo[odd, c] = outer[c]
    sides = (
        (0, DEEP - skip, 0, -skip, 0, skip, 0),
        (1, 0, skip + own, own, skip, 0, own - skip),
    )

    def body(x, carry):
        for side, obs_at, below_at, row, here, there, rest in sides:
            ok = inside(id_ref, row, (skip, BRICK))
            rows = [
                jnp.where(
                    ok,
                    halo[side, c, x, obs_at : obs_at + skip, :]
                    / below[c, x, below_at : below_at + skip, :],
                    0.0,
                )
                for c in range(2)
            ]
            for c, value in enumerate(blur_z(*rows, u)):
                strip[c, here : here + skip, :] = value
                strip[c, there : there + skip, :] = own_ref[c, x, rest : rest + skip, :]
                at = side * (rows_out - DEEP)
                out_ref[c, x, at : at + DEEP, :] = y_rows(strip, (c,), TRIM, w, 0, DEEP)
        for c in range(2):
            out_ref[c, x, DEEP : rows_out - DEEP, :] = middle[c, x]
        return carry

    lax.fori_loop(0, x_cells, body, 0)
    put_layers(id_ref, out_ref, layers_in, layers_out)


def rim(w, ids, below, own, middle, inner, outer):
    _, x, y, _ = own.shape
    skip = (below.shape[2] - y) // 2
    return swap_layers(*call(
        rim_kernel, "rim", field_and_layers(x, middle.shape[2] + 2 * DEEP),
        (w, ids, below, own, middle, inner, outer), 2,
        scratch=[
            pltpu.VMEM((2, 2, x, DEEP, BRICK), jnp.float32),
            pltpu.VMEM((2, 2 * skip, BRICK), jnp.float32),
        ],
    ))


def widen_kernel(id_ref, moved, inner, outer, obs):
    _, x_cells, rows, _ = obs.shape
    own = rows - 2 * DEEP
    odd = id_ref[4]
    for c in range(2):
        for x in range(x_cells):
            at = (c * x_cells + x) * own
            obs[c, x, DEEP : DEEP + own, :] = moved[at : at + own, :]
            low = pl.multiple_of((1 - odd) * (DEEP + own), DEEP)
            high = pl.multiple_of(odd * (DEEP + own), DEEP)
            obs[c, x, pl.ds(low, DEEP), :] = inner[c, x]
            obs[c, x, pl.ds(high, DEEP), :] = outer[c, x]


def ratio_kernel(w_ref, id_ref, field, inner, outer, obs, out_ref, side):
    _, x_cells, y_cells, _ = field.shape
    skip = (obs.shape[2] - y_cells) // 2
    w = taps_of(w_ref, 0, False)
    u = taps_of(w_ref, 2, True)
    set_sides(id_ref, inner, outer, side)

    def body(t, carry):
        start = pl.multiple_of(t * TILE, TILE)
        at = pl.ds(start, TILE)
        ok = inside(id_ref, start + skip - DEEP, (TILE, BRICK))
        la, lb = x_layers(field, side, 0, at), x_layers(field, side, 1, at)
        for x in range(x_cells):
            rows = [
                jnp.where(ok, obs[c, x, pl.ds(start + skip, TILE), :] / weigh(l[x : x + TAPS], w), 0.0)
                for c, l in ((0, la), (1, lb))
            ]
            a, b = blur_z(*rows, u)
            out_ref[0, x, at, :] = a
            out_ref[1, x, at, :] = b
        return carry

    lax.fori_loop(0, y_cells // TILE, body, 0)


def split_kernel(views, w_ref, id_ref, field, inner, outer, *refs):
    outs, wide = refs[:-1], refs[-1]
    _, x_cells, y_cells, _ = field.shape
    depth = x_cells // views
    w = taps_of(w_ref, 0, True)
    odd = id_ref[1]
    for c in range(2):
        for i in range(HALO):
            wide[c, (1 - odd) * (HALO + x_cells) + i] = inner[c, i]
            wide[c, odd * (HALO + x_cells) + i] = outer[c, i]
        for i in range(x_cells):
            wide[c, HALO + i] = field[c, i]
    for r in range(views):
        base = lax.rem(id_ref[0] + r, views) * depth

        def body(t, carry, base=base, pair=outs[2 * r : 2 * r + 2]):
            at = pl.ds(pl.multiple_of(t * TILE, TILE), TILE)
            for c in range(2):
                layers = [wide[c, base + i, at, :] for i in range(depth + 2 * HALO)]
                for i in range(depth):
                    pair[c][i, at, :] = weigh(layers[i : i + TAPS], w)
            return carry

        lax.fori_loop(0, y_cells // TILE, body, 0, unroll=2)


def split(w, ids, views, field, inner, outer):
    _, x, y, _ = field.shape
    outs = [f32(x // views, y, BRICK)] * (2 * views)
    return call(
        functools.partial(split_kernel, views), "x_blur_split", outs,
        (w, ids, field, inner, outer), 2,
        scratch=[pltpu.VMEM((2, x + 2 * HALO, y, BRICK), jnp.float32)],
    )


def add_kernel(a, ra, b, rb, out_a, out_b):
    out_a[...] = a[...] + ra[...]
    out_b[...] = b[...] + rb[...]


def update_first_kernel(views, id_ref, est, lo, hi, a, a1, a2, b, b1, b2, out_a, out_b):
    depth, y_cells, _ = a.shape
    own = est.shape[1]
    side = (y_cells - own) // 2
    base = id_ref[0] * depth
    spans = ((lo, DEEP - side, 0, side), (est, 0, side, own), (hi, 0, side + own, side))
    for i in range(depth):
        for ref, y, to, n in spans:
            at = slice(to, to + n)
            row = ref[base + i, y : y + n, :]
            out_a[i, at, :] = row[:, 0:BRICK] * (a[i, at, :] + a1[i, at, :] + a2[i, at, :]) / views
            out_b[i, at, :] = (
                row[:, BRICK : 2 * BRICK] * (b[i, at, :] + b1[i, at, :] + b2[i, at, :]) / views
            )


def update_kernel(views, est_a, est_b, a, a1, a2, b, b1, b2, out_a, out_b):
    side = (est_a.shape[1] - a.shape[1]) // 2
    at = slice(side, side + a.shape[1])
    out_a[...] = est_a[:, at, :] * (a[...] + a1[...] + a2[...]) / views
    out_b[...] = est_b[:, at, :] * (b[...] + b1[...] + b2[...]) / views


def join_kernel(views, id_ref, *refs):
    pieces, out_ref = refs[: 2 * views], refs[2 * views]
    depth = pieces[0].shape[0]
    for d in range(views):
        base = lax.rem(id_ref[0] + d, views) * depth
        for i in range(depth):
            out_ref[base + i, :, 0:BRICK] = pieces[2 * d][i]
            out_ref[base + i, :, BRICK : 2 * BRICK] = pieces[2 * d + 1][i]


def turn(value, step, count):
    return lax.ppermute(value, "views", [(i, (i + step) % count) for i in range(count)])


def per_device(estimate, views_data, target, psf_taps, shifts):
    x_cells, y_cells, z_cells = estimate.shape
    row_count = lax.axis_size("rows")
    block_count = lax.axis_size("blocks")
    peer_count = block_count * row_count
    view_count = lax.axis_size("views")
    brick_cols = z_cells // BRICK
    brick_count = x_cells * y_cells * brick_cols
    capacity = 2 * brick_count // peer_count
    geo = (peer_count, capacity, x_cells, y_cells, brick_cols, row_count, y_cells * block_count)
    block, row = lax.axis_index("blocks"), lax.axis_index("rows")
    odd = block % 2
    sent = [
        lax.dynamic_slice_in_dim(estimate, at * (y_cells - DEEP), DEEP, 1) for at in (1 - odd, odd)
    ]
    est_in, est_out = swap_rows(*sent)
    targets = target[0].transpose(0, 2, 1)
    outgoing = pack(shifts, targets, views_data[0], geo)
    outgoing, est_in, est_out = lax.optimization_barrier((outgoing, est_in, est_out))
    est_lo = jnp.where(odd == 1, est_in, est_out)
    est_hi = jnp.where(odd == 1, est_out, est_in)
    arrived = lax.all_to_all(
        outgoing.reshape(peer_count, capacity + 1, 1, BRICK),
        ("blocks", "rows"), split_axis=0, concat_axis=0, tiled=True,
    ).reshape(peer_count * (capacity + 1), 1, BRICK)
    w = (psf_taps[0] / jnp.sum(psf_taps[0], axis=1, keepdims=True)).reshape(-1)
    ids = jnp.stack([
        lax.axis_index("views"),
        row % 2,
        jnp.where(block == 0, 0, -DEEP),
        jnp.where(block == block_count - 1, y_cells, y_cells + DEEP),
        odd,
    ]).astype(jnp.int32)
    pieces = None
    for iteration in range(ITERS):
        if pieces is None:
            field = z_first(w, estimate, est_lo, est_hi)
            below = x_blur(w, ids, *y_blur(w, ids, field, False, TRIM))
            arrived, below = lax.optimization_barrier((arrived, below))
            moved, inner, outer = unpack(ids, arrived, peer_count, capacity, x_cells, y_cells)
            inner, outer = swap_rows(inner, outer)
            own = call(
                ratio_own_kernel, "ratio_own", [f32(2, x_cells, y_cells, BRICK)], (w, below, moved)
            )[0]
            middle = call(
                functools.partial(y_kernel, True, TILE), "y_blur",
                [f32(2, x_cells, y_cells - 2 * TILE, BRICK)], (w, ids, own), 2,
            )[0]
            fields = rim(w, ids, below, own, middle, inner, outer)
            obs = call(
                widen_kernel, "widen", [f32(2, x_cells, y_cells + 2 * DEEP, BRICK)],
                (ids, moved, inner, outer),
            )[0]
            sent = split(w, ids, view_count, *fields)
        else:
            y = pieces[0].shape[1] - 2 * TRIM
            field, inner, outer = swap_layers(*call(
                functools.partial(y_pieces_kernel, view_count), "y_blur_pieces",
                field_and_layers(x_cells, y),
                (w, ids, *(z for d in range(view_count) for z in z_piece(w, *pieces[2 * d : 2 * d + 2]))),
                2,
            ))
            field = call(
                ratio_kernel, "ratio", [f32(*field.shape)], (w, ids, field, inner, outer, obs), 2,
                scratch=[sides(field)],
            )[0]
            sent = split(w, ids, view_count, *y_blur(w, ids, field, True, TRIM))
        a0, b0, a1, b1, a2, b2, a3, b3 = sent
        pair = [f32(*a0.shape)] * 2
        ra, rb = turn(a2, 1, view_count), turn(b2, -1, view_count)
        near_b, near_a = turn(b1, 1, view_count), turn(a3, -1, view_count)
        a1, b3 = call(add_kernel, "add", pair, (a1, ra, b3, rb), 0)
        far_a, far_b = turn(a1, 1, view_count), turn(b3, -1, view_count)
        sums = (a0, near_a, far_a, b0, near_b, far_b)
        if pieces is None:
            own = call(
                functools.partial(update_first_kernel, view_count), "update_first", pair,
                (ids, estimate, est_lo, est_hi, *sums),
            )
        else:
            own = call(
                functools.partial(update_kernel, view_count), "update", pair,
                (*pieces[:2], *sums), 0,
            )
        prev_a, next_b = turn(own[0], 1, view_count), turn(own[1], -1, view_count)
        prev_b, next_a = turn(own[1], 1, view_count), turn(own[0], -1, view_count)
        far_a, far_b = turn(prev_a, 1, view_count), turn(next_b, -1, view_count)
        pieces = (*own, next_a, next_b, far_a, far_b, prev_a, prev_b)
    return call(
        functools.partial(join_kernel, view_count), "join", [f32(x_cells, y_cells, z_cells)],
        (ids, *pieces),
    )[0]


def solution(mesh):
    placed = (
        P("rows", "blocks", None),
        P("views", "rows", "blocks", None),
        P("views", "rows", "blocks", None),
        P("views", None, None),
        P("views"),
    )
    return jax.shard_map(
        per_device, mesh=mesh, in_specs=placed, out_specs=P("rows", "blocks", None), check_vma=False
    )
```

```python
import functools
import jax
import jax.numpy as jnp
from jax import lax
from jax.experimental import pallas as pl
from jax.experimental.pallas import tpu as pltpu
from jax.sharding import PartitionSpec as P

VMEM = pltpu.VMEM
BRICK = 128
HALO = 3
ITERS = 2
GROUP = 16
SPARE = 8
TAPS = 2 * HALO + 1
TILE = 8
TRIM = 4
DEEP = 16
ROWS = 32


def lane_sum(x):
    return jnp.sum(x, axis=1, keepdims=True)


def pack_kernel(geo, shift_ref, target_ref, views_ref, out_ref, rolled, pos_v, pos_s, sem):
    peers, cap, x_cells, y_cells, brick_cols, row_count, all_cols = geo
    groups = brick_cols * x_cells
    rows_per = cap + 1
    t = target_ref[...]
    bz = t % brick_cols
    column = t // brick_cols % all_cols
    line = t // (brick_cols * all_cols)
    dest = column // y_cells * row_count + line // x_cells
    slot = (bz * x_cells + line % x_cells) * y_cells + column % y_cells + 1
    high, low = slot // 64, slot % 64
    peer_id = lax.broadcasted_iota(jnp.int32, (peers, y_cells), 0)
    before = (
        lax.broadcasted_iota(jnp.int32, (y_cells, y_cells), 0)
        < lax.broadcasted_iota(jnp.int32, (y_cells, y_cells), 1)
    ).astype(jnp.bfloat16)
    kid = lax.broadcasted_iota(jnp.int32, (BRICK, y_cells), 0)
    carry = jnp.zeros((peers, 1), jnp.float32)
    listed = jnp.zeros((2 * peers, BRICK), jnp.float32)
    for g in range(groups):
        here = (g % x_cells, slice(g // x_cells, g // x_cells + 1))
        d = dest[here]
        hot = d == peer_id
        hot_f = hot.astype(jnp.float32)
        ahead = jnp.dot(hot_f.astype(jnp.bfloat16), before, preferred_element_type=jnp.float32)
        ranks = jnp.sum(hot_f * (ahead + carry), axis=0, keepdims=True)
        carry = carry + lane_sum(hot_f)
        rank_i = ranks.astype(jnp.int32)
        pos_v[g : g + 1, :] = d * rows_per + rank_i
        h = hot_f * high[here].astype(jnp.float32)
        l = hot_f * low[here].astype(jnp.float32)
        both = jnp.concatenate([h, l], axis=0).astype(jnp.bfloat16)
        at = (rank_i == kid).astype(jnp.float32).astype(jnp.bfloat16)
        listed = listed + lax.dot_general(
            both, at, (((1,), (1,)), ((), ())), preferred_element_type=jnp.float32
        )
    copy = pltpu.make_async_copy(pos_v, pos_s, sem)
    copy.start()
    entries = 64.0 * listed[:peers] + listed[peers:]
    for p in range(peers):
        out_ref[p * rows_per + cap] = entries[p : p + 1, :]
    shift = shift_ref[0]
    for bz_i in range(brick_cols):
        for x in range(x_cells):
            rolled[bz_i * x_cells + x] = pltpu.roll(
                views_ref[x, :, bz_i * BRICK : (bz_i + 1) * BRICK], shift, 1
            )
    copy.wait()

    def body(g, c):
        for base in range(0, y_cells, GROUP):
            places = [pos_s[g, base + i] for i in range(GROUP)]
            rows = [rolled[g, base + i : base + i + 1, :] for i in range(GROUP)]
            for place, row in zip(places, rows):
                out_ref[place] = row
        return c

    lax.fori_loop(0, groups, body, 0)


def pack(shift, target, views, geo):
    peers, cap, x_cells, y_cells, brick_cols, row_count, all_cols = geo
    groups = brick_cols * x_cells
    return pl.pallas_call(
        functools.partial(pack_kernel, geo),
        out_shape=jax.ShapeDtypeStruct((peers * (cap + 1), 1, BRICK), jnp.float32),
        in_specs=[
            pl.BlockSpec(memory_space=pltpu.SMEM),
            pl.BlockSpec(memory_space=pltpu.VMEM),
            pl.BlockSpec(memory_space=pltpu.VMEM),
        ],
        out_specs=pl.BlockSpec(memory_space=pltpu.VMEM),
        scratch_shapes=[
            pltpu.VMEM((groups, y_cells, BRICK), jnp.float32),
            pltpu.VMEM((groups, y_cells), jnp.int32),
            pltpu.SMEM((groups, y_cells), jnp.int32),
            pltpu.SemaphoreType.DMA,
        ],
        name="pack",
    )(shift, target, views)


def unpack_kernel(peers, cap, slots, id_ref, in_ref, out_ref, inner, outer, list_v, idx_v, idx_s, sem):
    rows_per = cap + 1
    for p in range(peers):
        list_v[p : p + 1, :] = in_ref[p * rows_per + cap]
    e = list_v[...].astype(jnp.int32)
    idx_v[...] = jnp.where(e > 0, e - 1, slots)
    copy = pltpu.make_async_copy(idx_v, idx_s, sem)
    copy.start()
    copy.wait()

    def per_peer(p, c):
        for base in range(0, cap, GROUP):
            places = [idx_s[p, base + i] for i in range(GROUP)]
            rows = [in_ref[p * rows_per + base + i] for i in range(GROUP)]
            for place, row in zip(places, rows):
                out_ref[pl.ds(place, 1), :] = row
        return c

    lax.fori_loop(0, peers, per_peer, 0)
    _, x_cells, deep, _ = inner.shape
    y_cells = slots // (2 * x_cells)
    odd = id_ref[4]
    for c in range(2):
        for x in range(x_cells):
            at = (c * x_cells + x) * y_cells
            near = pl.multiple_of(at + odd * (y_cells - deep), deep)
            far = pl.multiple_of(at + (1 - odd) * (y_cells - deep), deep)
            inner[c, x] = out_ref[pl.ds(far, deep), :]
            outer[c, x] = out_ref[pl.ds(near, deep), :]


def unpack(ids, arrived, peers, cap, x_cells, y_cells):
    slots = 2 * x_cells * y_cells
    edge = f32(2, x_cells, DEEP, BRICK)
    return call(
        functools.partial(unpack_kernel, peers, cap, slots), "unpack",
        [f32(slots + SPARE, BRICK), edge, edge], (ids, arrived),
        scratch=[
            pltpu.VMEM((peers, BRICK), jnp.float32),
            pltpu.VMEM((peers, BRICK), jnp.int32),
            pltpu.SMEM((peers, BRICK), jnp.int32),
            pltpu.SemaphoreType.DMA,
        ],
    )


def vmem():
    return pl.BlockSpec(memory_space=pltpu.VMEM)


def smem():
    return pl.BlockSpec(memory_space=pltpu.SMEM)


def f32(*shape):
    return jax.ShapeDtypeStruct(shape, jnp.float32)


def call(kernel, name, outs, args, scalars=1, scratch=(), work=1000):
    return pl.pallas_call(
        kernel,
        out_shape=outs,
        in_specs=[smem()] * scalars + [vmem()] * (len(args) - scalars),
        out_specs=[vmem()] * len(outs),
        scratch_shapes=list(scratch),
        cost_estimate=pl.CostEstimate(flops=work, bytes_accessed=work, transcendentals=0),
        compiler_params=pltpu.CompilerParams(vmem_limit_bytes=32 * 1024 * 1024),
        name=name,
    )(*args)


def taps_of(w_ref, dim, flip):
    return [w_ref[dim * TAPS + (TAPS - 1 - k if flip else k)] for k in range(TAPS)]


def blur_z(a, b, w):
    lane = lax.broadcasted_iota(jnp.int32, a.shape, 1)
    out_a, out_b = w[HALO] * a, w[HALO] * b
    for s in range(1, HALO + 1):
        keep = lane < BRICK - s
        ra, rb = pltpu.roll(a, BRICK - s, 1), pltpu.roll(b, BRICK - s, 1)
        out_a += w[HALO + s] * jnp.where(keep, ra, rb)
        out_b += w[HALO + s] * jnp.where(keep, rb, 0.0)
        fresh = lane < s
        la, lb = pltpu.roll(a, s, 1), pltpu.roll(b, s, 1)
        out_a += w[HALO - s] * jnp.where(fresh, 0.0, la)
        out_b += w[HALO - s] * jnp.where(fresh, la, lb)
    return out_a, out_b


def row_parts(rows):
    return [(y, min(ROWS, rows - y)) for y in range(0, rows, ROWS)]


def z_first_kernel(w_ref, est_ref, lo, hi, out_ref):
    x_cells, y_cells, _ = est_ref.shape
    w = taps_of(w_ref, 2, False)
    spans = [(lo, 0, 0, DEEP), (hi, 0, DEEP + y_cells, DEEP)]
    spans += [(est_ref, y, DEEP + y, n) for y, n in row_parts(y_cells)]

    def body(x, carry):
        for ref, y, to, n in spans:
            a, b = blur_z(ref[x, y : y + n, 0:BRICK], ref[x, y : y + n, BRICK : 2 * BRICK], w)
            out_ref[0, x, to : to + n, :] = a
            out_ref[1, x, to : to + n, :] = b
        return carry

    lax.fori_loop(0, x_cells, body, 0)


def z_first(w, estimate, lo, hi):
    x, y, _ = estimate.shape
    return call(z_first_kernel, "z_blur", [f32(2, x, y + 2 * DEEP, BRICK)], (w, estimate, lo, hi))[0]


def z_piece_kernel(w_ref, in_a, in_b, out_a, out_b):
    depth, y_cells, _ = in_a.shape
    w = taps_of(w_ref, 2, False)

    def body(i, carry):
        for y, n in row_parts(y_cells):
            at = pl.ds(y, n)
            out_a[i, at, :], out_b[i, at, :] = blur_z(in_a[i, at, :], in_b[i, at, :], w)
        return carry

    lax.fori_loop(0, depth, body, 0)


def z_piece(w, a, b):
    return call(z_piece_kernel, "z_piece", [f32(*a.shape)] * 2, (w, a, b))


def y_rows(ref, at, trim, w, y, n):
    total = w[0] * ref[(*at, pl.ds(trim - HALO + y, n))]
    for k in range(1, TAPS):
        total += w[k] * ref[(*at, pl.ds(trim - HALO + k + y, n))]
    return total


def put_layers(id_ref, field, inner, outer):
    x_cells = field.shape[1]
    odd = id_ref[1]
    for c in range(2):
        for i in range(HALO):
            inner[c, i] = field[c, (1 - odd) * (x_cells - HALO) + i]
            outer[c, i] = field[c, odd * (x_cells - HALO) + i]


def y_kernel(flip, trim, w_ref, id_ref, in_ref, out_ref, *layers):
    _, x_cells, y_cells, _ = out_ref.shape
    w = taps_of(w_ref, 1, flip)

    def body(x, carry):
        for c in range(2):
            for y, n in row_parts(y_cells):
                out_ref[c, x, pl.ds(y, n), :] = y_rows(in_ref, (c, x), trim, w, y, n)
        return carry

    lax.fori_loop(0, x_cells, body, 0)
    if layers:
        put_layers(id_ref, out_ref, *layers)


def y_pieces_kernel(views, w_ref, id_ref, *refs):
    pieces, (out_ref, inner, outer) = refs[: 2 * views], refs[2 * views :]
    depth = pieces[0].shape[0]
    w = taps_of(w_ref, 1, False)
    for d in range(views):
        base = lax.rem(id_ref[0] + d, views) * depth
        for c in range(2):
            for i in range(depth):
                for y, n in row_parts(out_ref.shape[2]):
                    out_ref[c, base + i, pl.ds(y, n), :] = y_rows(pieces[2 * d + c], (i,), TRIM, w, y, n)
    put_layers(id_ref, out_ref, inner, outer)


def swap_layers(field, inner, outer):
    count = lax.axis_size("rows")
    links = [(i, i + 1) for i in range(1, count - 1, 2)]
    outer = lax.ppermute(outer, "rows", links + [(j, i) for i, j in links])
    inner = lax.ppermute(inner, "rows", [(i, i ^ 1) for i in range(count)])
    return field, inner, outer


def swap_rows(inner, outer):
    count = lax.axis_size("blocks")
    links = [(i, i + 1) for i in range(1, count - 1, 2)]
    outer = lax.ppermute(outer, "blocks", links + [(j, i) for i, j in links])
    inner = lax.ppermute(inner, "blocks", [(i, i ^ 1) for i in range(count)])
    return inner, outer


def field_and_layers(x, y):
    return [f32(2, x, y, BRICK), f32(2, HALO, y, BRICK), f32(2, HALO, y, BRICK)]


def y_blur(w, ids, field, flip, trim):
    _, x, y, _ = field.shape
    return swap_layers(*call(
        functools.partial(y_kernel, flip, trim), "y_blur", field_and_layers(x, y - 2 * trim),
        (w, ids, field), 2,
    ))


def set_sides(id_ref, inner, outer, side):
    odd = id_ref[1]
    for c in range(2):
        for i in range(HALO):
            side[1 - odd, c, i] = inner[c, i]
            side[odd, c, i] = outer[c, i]


def sides(field):
    _, _, y, _ = field.shape
    return pltpu.VMEM((2, 2, HALO, y, BRICK), jnp.float32)


def x_layers(field, side, c, at):
    x_cells = field.shape[1]
    return (
        [side[0, c, i, at, :] for i in range(HALO)]
        + [field[c, i, at, :] for i in range(x_cells)]
        + [side[1, c, i, at, :] for i in range(HALO)]
    )


def weigh(layers, w):
    total = w[0] * layers[0]
    for k in range(1, TAPS):
        total += w[k] * layers[k]
    return total


def x_kernel(w_ref, id_ref, field, outer, inner, out_ref, side):
    _, x_cells, y_cells, _ = field.shape
    w = taps_of(w_ref, 0, False)
    set_sides(id_ref, inner, outer, side)

    def body(t, carry):
        at = pl.ds(pl.multiple_of(t * TILE, TILE), TILE)
        for c in range(2):
            layers = x_layers(field, side, c, at)
            for x in range(x_cells):
                out_ref[c, x, at, :] = weigh(layers[x : x + TAPS], w)
        return carry

    lax.fori_loop(0, y_cells // TILE, body, 0)


def x_blur(w, ids, field, inner, outer):
    return call(
        x_kernel, "x_blur", [f32(*field.shape)], (w, ids, field, outer, inner), 2,
        scratch=[sides(field)],
    )[0]


def inside(id_ref, y, shape):
    row = lax.broadcasted_iota(jnp.int32, shape, 0) + y
    return (row >= id_ref[2]) & (row < id_ref[3])


def ratio_own_kernel(w_ref, below, moved, out_ref):
    _, x_cells, own, _ = out_ref.shape
    u = taps_of(w_ref, 2, True)
    skip = (below.shape[2] - own) // 2

    def body(x, carry):
        for y, n in row_parts(own):
            rows = [
                moved[pl.ds(pl.multiple_of((c * x_cells + x) * own + y, TILE), n), :]
                / below[c, x, pl.ds(skip + y, n), :]
                for c in range(2)
            ]
            a, b = blur_z(*rows, u)
            out_ref[0, x, pl.ds(y, n), :] = a
            out_ref[1, x, pl.ds(y, n), :] = b
        return carry

    lax.fori_loop(0, x_cells, body, 0)


def rim_kernel(w_ref, id_ref, below, own_ref, middle, inner, outer, out_ref, *scratch):
    _, x_cells, own, _ = own_ref.shape
    layers_in, layers_out, halo, strip = scratch
    u = taps_of(w_ref, 2, True)
    w = taps_of(w_ref, 1, True)
    rows_out = out_ref.shape[2]
    skip = (below.shape[2] - own) // 2
    span = DEEP + 2 * TRIM
    odd = id_ref[4]
    for c in range(2):
        halo[1 - odd, c] = inner[c]
        halo[odd, c] = outer[c]
    sides = (
        (0, DEEP - skip, 0, -skip, 0, skip, 0),
        (1, 0, skip + own, own, skip, 0, own - skip),
    )

    def body(x, carry):
        for side, obs_at, below_at, row, here, there, rest in sides:
            ok = inside(id_ref, row, (skip, BRICK))
            rows = [
                jnp.where(
                    ok,
                    halo[side, c, x, obs_at : obs_at + skip, :]
                    / below[c, x, below_at : below_at + skip, :],
                    0.0,
                )
                for c in range(2)
            ]
            for c, value in enumerate(blur_z(*rows, u)):
                strip[c, here : here + skip, :] = value
                strip[c, there : there + skip, :] = own_ref[c, x, rest : rest + skip, :]
                at = side * (rows_out - DEEP)
                out_ref[c, x, at : at + DEEP, :] = y_rows(strip, (c,), TRIM, w, 0, DEEP)
        for c in range(2):
            out_ref[c, x, DEEP : rows_out - DEEP, :] = middle[c, x]
        return carry

    lax.fori_loop(0, x_cells, body, 0)
    put_layers(id_ref, out_ref, layers_in, layers_out)


def rim(w, ids, below, own, middle, inner, outer):
    _, x, y, _ = own.shape
    skip = (below.shape[2] - y) // 2
    return swap_layers(*call(
        rim_kernel, "rim", field_and_layers(x, middle.shape[2] + 2 * DEEP),
        (w, ids, below, own, middle, inner, outer), 2,
        scratch=[
            pltpu.VMEM((2, 2, x, DEEP, BRICK), jnp.float32),
            pltpu.VMEM((2, 2 * skip, BRICK), jnp.float32),
        ],
    ))


def widen_kernel(id_ref, moved, inner, outer, obs):
    _, x_cells, rows, _ = obs.shape
    own = rows - 2 * DEEP
    odd = id_ref[4]
    for c in range(2):
        for x in range(x_cells):
            at = (c * x_cells + x) * own
            obs[c, x, DEEP : DEEP + own, :] = moved[at : at + own, :]
            low = pl.multiple_of((1 - odd) * (DEEP + own), DEEP)
            high = pl.multiple_of(odd * (DEEP + own), DEEP)
            obs[c, x, pl.ds(low, DEEP), :] = inner[c, x]
            obs[c, x, pl.ds(high, DEEP), :] = outer[c, x]


def ratio_kernel(w_ref, id_ref, field, outer, inner, obs, out_ref, side):
    _, x_cells, y_cells, _ = field.shape
    skip = (obs.shape[2] - y_cells) // 2
    w = taps_of(w_ref, 0, False)
    u = taps_of(w_ref, 2, True)
    set_sides(id_ref, inner, outer, side)

    def body(t, carry):
        start = pl.multiple_of(t * TILE, TILE)
        at = pl.ds(start, TILE)
        ok = inside(id_ref, start + skip - DEEP, (TILE, BRICK))
        la, lb = x_layers(field, side, 0, at), x_layers(field, side, 1, at)
        for x in range(x_cells):
            rows = [
                jnp.where(ok, obs[c, x, pl.ds(start + skip, TILE), :] / weigh(l[x : x + TAPS], w), 0.0)
                for c, l in ((0, la), (1, lb))
            ]
            a, b = blur_z(*rows, u)
            out_ref[0, x, at, :] = a
            out_ref[1, x, at, :] = b
        return carry

    lax.fori_loop(0, y_cells // TILE, body, 0)


def split_kernel(views, w_ref, id_ref, field, outer, inner, *refs):
    outs, wide = refs[:-1], refs[-1]
    _, x_cells, y_cells, _ = field.shape
    depth = x_cells // views
    w = taps_of(w_ref, 0, True)
    odd = id_ref[1]
    for c in range(2):
        for i in range(HALO):
            wide[c, (1 - odd) * (HALO + x_cells) + i] = inner[c, i]
            wide[c, odd * (HALO + x_cells) + i] = outer[c, i]
        for i in range(x_cells):
            wide[c, HALO + i] = field[c, i]
    for r in range(views):
        base = lax.rem(id_ref[0] + r, views) * depth

        def body(t, carry, base=base, pair=outs[2 * r : 2 * r + 2]):
            at = pl.ds(pl.multiple_of(t * TILE, TILE), TILE)
            for c in range(2):
                layers = [wide[c, base + i, at, :] for i in range(depth + 2 * HALO)]
                for i in range(depth):
                    pair[c][i, at, :] = weigh(layers[i : i + TAPS], w)
            return carry

        lax.fori_loop(0, y_cells // TILE, body, 0, unroll=2)


def split(w, ids, views, field, inner, outer):
    _, x, y, _ = field.shape
    outs = [f32(x // views, y, BRICK)] * (2 * views)
    return call(
        functools.partial(split_kernel, views), "x_blur_split", outs,
        (w, ids, field, outer, inner), 2,
        scratch=[pltpu.VMEM((2, x + 2 * HALO, y, BRICK), jnp.float32)],
    )


def add_kernel(a, ra, b, rb, out_a, out_b):
    out_a[...] = a[...] + ra[...]
    out_b[...] = b[...] + rb[...]


def update_first_kernel(views, id_ref, est, lo, hi, a, a1, a2, b, b1, b2, out_a, out_b):
    depth, y_cells, _ = a.shape
    own = est.shape[1]
    side = (y_cells - own) // 2
    base = id_ref[0] * depth
    spans = ((lo, DEEP - side, 0, side), (est, 0, side, own), (hi, 0, side + own, side))
    for i in range(depth):
        for ref, y, to, n in spans:
            at = slice(to, to + n)
            row = ref[base + i, y : y + n, :]
            out_a[i, at, :] = row[:, 0:BRICK] * (a[i, at, :] + a1[i, at, :] + a2[i, at, :]) / views
            out_b[i, at, :] = (
                row[:, BRICK : 2 * BRICK] * (b[i, at, :] + b1[i, at, :] + b2[i, at, :]) / views
            )


def update_kernel(views, est_a, est_b, a, a1, a2, b, b1, b2, out_a, out_b):
    side = (est_a.shape[1] - a.shape[1]) // 2
    at = slice(side, side + a.shape[1])
    out_a[...] = est_a[:, at, :] * (a[...] + a1[...] + a2[...]) / views
    out_b[...] = est_b[:, at, :] * (b[...] + b1[...] + b2[...]) / views


def join_kernel(count, id_ref, *refs):
    pieces, out_ref = refs[: 2 * count], refs[-1]
    step = pl.program_id(0)
    for d in range(count):

        @pl.when(step == d)
        def _(d=d):
            out_ref[:, :, 0:BRICK] = pieces[2 * d][...]
            out_ref[:, :, BRICK : 2 * BRICK] = pieces[2 * d + 1][...]


def join(ids, steps, pieces, shape, into=None):
    count = len(steps)
    views = shape[0] // pieces[0].shape[0]
    depth = pieces[0].shape[0]

    def place(step, id_ref):
        at = steps[0]
        for d in range(1, count):
            at = jnp.where(step == d, steps[d], at)
        return (id_ref[0] + at) % views, 0, 0

    whole = [pl.BlockSpec(p.shape, lambda step, id_ref: (0, 0, 0)) for p in pieces]
    given = [] if into is None else [into]
    return pl.pallas_call(
        functools.partial(join_kernel, count),
        out_shape=f32(*shape),
        grid_spec=pltpu.PrefetchScalarGridSpec(
            num_scalar_prefetch=1,
            grid=(count,),
            in_specs=whole + [pl.BlockSpec(memory_space=pl.ANY)] * len(given),
            out_specs=pl.BlockSpec((depth, *shape[1:]), place),
        ),
        input_output_aliases={} if into is None else {1 + len(pieces): 0},
        cost_estimate=pl.CostEstimate(flops=1000, bytes_accessed=1000, transcendentals=0),
        name="join",
    )(ids, *pieces, *given)


def turn(value, step, count):
    return lax.ppermute(value, "views", [(i, (i + step) % count) for i in range(count)])


def per_device(estimate, views_data, target, psf_taps, shifts):
    x_cells, y_cells, z_cells = estimate.shape
    row_count = lax.axis_size("rows")
    block_count = lax.axis_size("blocks")
    peer_count = block_count * row_count
    view_count = lax.axis_size("views")
    brick_cols = z_cells // BRICK
    brick_count = x_cells * y_cells * brick_cols
    capacity = 2 * brick_count // peer_count
    geo = (peer_count, capacity, x_cells, y_cells, brick_cols, row_count, y_cells * block_count)
    block, row = lax.axis_index("blocks"), lax.axis_index("rows")
    odd = block % 2
    sent = [
        lax.dynamic_slice_in_dim(estimate, at * (y_cells - DEEP), DEEP, 1) for at in (1 - odd, odd)
    ]
    est_in, est_out = swap_rows(*sent)
    targets = target[0].transpose(0, 2, 1)
    outgoing = pack(shifts, targets, views_data[0], geo)
    outgoing, *first = lax.optimization_barrier((outgoing, est_in[:1, :1], est_out[:1, :1]))
    est_in = lax.dynamic_update_slice(est_in, first[0], (0, 0, 0))
    est_out = lax.dynamic_update_slice(est_out, first[1], (0, 0, 0))
    est_lo = jnp.where(odd == 1, est_in, est_out)
    est_hi = jnp.where(odd == 1, est_out, est_in)
    arrived = lax.all_to_all(
        outgoing.reshape(peer_count, capacity + 1, 1, BRICK),
        ("blocks", "rows"), split_axis=0, concat_axis=0, tiled=True,
    ).reshape(peer_count * (capacity + 1), 1, BRICK)
    w = (psf_taps[0] / jnp.sum(psf_taps[0], axis=1, keepdims=True)).reshape(-1)
    ids = jnp.stack([
        lax.axis_index("views"),
        row % 2,
        jnp.where(block == 0, 0, -DEEP),
        jnp.where(block == block_count - 1, y_cells, y_cells + DEEP),
        odd,
    ]).astype(jnp.int32)
    pieces = None
    for iteration in range(ITERS):
        if pieces is None:
            field = z_first(w, estimate, est_lo, est_hi)
            below = x_blur(w, ids, *y_blur(w, ids, field, False, TRIM))
            arrived, below = lax.optimization_barrier((arrived, below))
            moved, inner, outer = unpack(ids, arrived, peer_count, capacity, x_cells, y_cells)
            inner, outer = swap_rows(inner, outer)
            own = call(
                ratio_own_kernel, "ratio_own", [f32(2, x_cells, y_cells, BRICK)], (w, below, moved)
            )[0]
            middle = call(
                functools.partial(y_kernel, True, TILE), "y_blur",
                [f32(2, x_cells, y_cells - 2 * TILE, BRICK)], (w, ids, own), 2,
            )[0]
            fields = rim(w, ids, below, own, middle, inner, outer)
            obs = call(
                widen_kernel, "widen", [f32(2, x_cells, y_cells + 2 * DEEP, BRICK)],
                (ids, moved, inner, outer),
            )[0]
            sent = split(w, ids, view_count, *fields)
        else:
            y = pieces[0].shape[1] - 2 * TRIM
            field, inner, outer = swap_layers(*call(
                functools.partial(y_pieces_kernel, view_count), "y_blur_pieces",
                field_and_layers(x_cells, y),
                (w, ids, *(z for d in range(view_count) for z in z_piece(w, *pieces[2 * d : 2 * d + 2]))),
                2,
            ))
            field = call(
                ratio_kernel, "ratio", [f32(*field.shape)], (w, ids, field, outer, inner, obs), 2,
                scratch=[sides(field)],
            )[0]
            sent = split(w, ids, view_count, *y_blur(w, ids, field, True, TRIM))
        a0, b0, a1, b1, a2, b2, a3, b3 = sent
        pair = [f32(*a0.shape)] * 2
        ra, rb = turn(a2, 1, view_count), turn(b2, -1, view_count)
        near_b, near_a = turn(b1, 1, view_count), turn(a3, -1, view_count)
        a1, b3 = call(add_kernel, "add", pair, (a1, ra, b3, rb), 0)
        far_a, far_b = turn(a1, 1, view_count), turn(b3, -1, view_count)
        sums = (a0, near_a, far_a, b0, near_b, far_b)
        if pieces is None:
            own = call(
                functools.partial(update_first_kernel, view_count), "update_first", pair,
                (ids, estimate, est_lo, est_hi, *sums),
            )
        else:
            own = call(
                functools.partial(update_kernel, view_count), "update", pair,
                (*pieces[:2], *sums), 0,
            )
        prev_a, next_b = turn(own[0], 1, view_count), turn(own[1], -1, view_count)
        prev_b, next_a = turn(own[1], 1, view_count), turn(own[0], -1, view_count)
        far_a, far_b = turn(prev_a, 1, view_count), turn(next_b, -1, view_count)
        pieces = (*own, next_a, next_b, far_a, far_b, prev_a, prev_b)
    shape = (x_cells, y_cells, z_cells)
    near = join(ids, (0, 1, 3), pieces[:4] + pieces[6:], shape)
    return join(ids, (2,), pieces[4:6], shape, near)


def solution(mesh):
    placed = (
        P("rows", "blocks", None),
        P("views", "rows", "blocks", None),
        P("views", "rows", "blocks", None),
        P("views", None, None),
        P("views"),
    )
    return jax.shard_map(
        per_device, mesh=mesh, in_specs=placed, out_specs=P("rows", "blocks", None), check_vma=False
    )
```

```python
import functools
import jax
import jax.numpy as jnp
from jax import lax
from jax.experimental import pallas as pl
from jax.experimental.pallas import tpu as pltpu
from jax.sharding import PartitionSpec as P

VMEM = pltpu.VMEM
BRICK = 128
HALO = 3
ITERS = 2
GROUP = 16
SPARE = 8
TAPS = 2 * HALO + 1
TILE = 8
TRIM = 4


def lane_sum(x):
    return jnp.sum(x, axis=1, keepdims=True)


def pack_kernel(geo, shift_ref, target_ref, views_ref, out_ref, rolled, pos_v, pos_s, sem):
    peers, cap, x_cells, y_cells, brick_cols, row_count, all_cols, view_count = geo
    groups = brick_cols * x_cells
    rows_per = cap + 1
    t = target_ref[...]
    bz = t % brick_cols
    column = t // brick_cols % all_cols
    line = t // (brick_cols * all_cols)
    dest = column // y_cells * row_count + line // x_cells
    part = y_cells // view_count
    y = column % y_cells
    slot = ((y // part * brick_cols + bz) * x_cells + line % x_cells) * part + y % part + 1
    high, low = slot // 64, slot % 64
    peer_id = lax.broadcasted_iota(jnp.int32, (peers, y_cells), 0)
    before = (
        lax.broadcasted_iota(jnp.int32, (y_cells, y_cells), 0)
        < lax.broadcasted_iota(jnp.int32, (y_cells, y_cells), 1)
    ).astype(jnp.bfloat16)
    kid = lax.broadcasted_iota(jnp.int32, (BRICK, y_cells), 0)
    carry = jnp.zeros((peers, 1), jnp.float32)
    listed = jnp.zeros((2 * peers, BRICK), jnp.float32)
    for g in range(groups):
        here = (g % x_cells, slice(g // x_cells, g // x_cells + 1))
        d = dest[here]
        hot = d == peer_id
        hot_f = hot.astype(jnp.float32)
        ahead = jnp.dot(hot_f.astype(jnp.bfloat16), before, preferred_element_type=jnp.float32)
        ranks = jnp.sum(hot_f * (ahead + carry), axis=0, keepdims=True)
        carry = carry + lane_sum(hot_f)
        rank_i = ranks.astype(jnp.int32)
        pos_v[g : g + 1, :] = d * rows_per + rank_i
        h = hot_f * high[here].astype(jnp.float32)
        l = hot_f * low[here].astype(jnp.float32)
        both = jnp.concatenate([h, l], axis=0).astype(jnp.bfloat16)
        at = (rank_i == kid).astype(jnp.float32).astype(jnp.bfloat16)
        listed = listed + lax.dot_general(
            both, at, (((1,), (1,)), ((), ())), preferred_element_type=jnp.float32
        )
    copy = pltpu.make_async_copy(pos_v, pos_s, sem)
    copy.start()
    entries = 64.0 * listed[:peers] + listed[peers:]
    for p in range(peers):
        out_ref[p * rows_per + cap] = entries[p : p + 1, :]
    shift = shift_ref[0]
    for bz_i in range(brick_cols):
        for x in range(x_cells):
            rolled[bz_i * x_cells + x] = pltpu.roll(
                views_ref[x, :, bz_i * BRICK : (bz_i + 1) * BRICK], shift, 1
            )
    copy.wait()

    def body(g, c):
        for base in range(0, y_cells, GROUP):
            places = [pos_s[g, base + i] for i in range(GROUP)]
            rows = [rolled[g, base + i : base + i + 1, :] for i in range(GROUP)]
            for place, row in zip(places, rows):
                out_ref[place] = row
        return c

    lax.fori_loop(0, groups, body, 0)


def pack(shift, target, views, geo):
    peers, cap, x_cells, y_cells, brick_cols, row_count, all_cols, view_count = geo
    groups = brick_cols * x_cells
    return pl.pallas_call(
        functools.partial(pack_kernel, geo),
        out_shape=jax.ShapeDtypeStruct((peers * (cap + 1), 1, BRICK), jnp.float32),
        in_specs=[
            pl.BlockSpec(memory_space=pltpu.SMEM),
            pl.BlockSpec(memory_space=pltpu.VMEM),
            pl.BlockSpec(memory_space=pltpu.VMEM),
        ],
        out_specs=pl.BlockSpec(memory_space=pltpu.VMEM),
        scratch_shapes=[
            pltpu.VMEM((groups, y_cells, BRICK), jnp.float32),
            pltpu.VMEM((groups, y_cells), jnp.int32),
            pltpu.SMEM((groups, y_cells), jnp.int32),
            pltpu.SemaphoreType.DMA,
        ],
        name="pack",
    )(shift, target, views)


def unpack_kernel(peers, cap, slots, in_ref, out_ref, placed, list_v, idx_v, idx_s, sem):
    rows_per = cap + 1
    for p in range(peers):
        list_v[p : p + 1, :] = in_ref[p * rows_per + cap]
    e = list_v[...].astype(jnp.int32)
    idx_v[...] = jnp.where(e > 0, e - 1, slots)
    copy = pltpu.make_async_copy(idx_v, idx_s, sem)
    copy.start()
    copy.wait()

    def per_peer(p, c):
        for base in range(0, cap, GROUP):
            places = [idx_s[p, base + i] for i in range(GROUP)]
            rows = [in_ref[p * rows_per + base + i] for i in range(GROUP)]
            for place, row in zip(places, rows):
                placed[pl.ds(place, 1), :] = row
        return c

    lax.fori_loop(0, peers, per_peer, 0)
    out_ref[...] = placed[0:slots, :]


def unpack(arrived, peers, cap, slots):
    return call(
        functools.partial(unpack_kernel, peers, cap, slots), "unpack", [f32(slots, BRICK)],
        (arrived,), 0,
        scratch=[
            pltpu.VMEM((slots + SPARE, BRICK), jnp.float32),
            pltpu.VMEM((peers, BRICK), jnp.float32),
            pltpu.VMEM((peers, BRICK), jnp.int32),
            pltpu.SMEM((peers, BRICK), jnp.int32),
            pltpu.SemaphoreType.DMA,
        ],
    )[0]


def vmem():
    return pl.BlockSpec(memory_space=pltpu.VMEM)


def smem():
    return pl.BlockSpec(memory_space=pltpu.SMEM)


def f32(*shape):
    return jax.ShapeDtypeStruct(shape, jnp.float32)


def call(kernel, name, outs, args, scalars=1, scratch=(), work=1000):
    return pl.pallas_call(
        kernel,
        out_shape=outs,
        in_specs=[smem()] * scalars + [vmem()] * (len(args) - scalars),
        out_specs=[vmem()] * len(outs),
        scratch_shapes=list(scratch),
        cost_estimate=pl.CostEstimate(flops=work, bytes_accessed=work, transcendentals=0),
        compiler_params=pltpu.CompilerParams(vmem_limit_bytes=32 * 1024 * 1024),
        name=name,
    )(*args)


def taps_of(w_ref, view, dim, flip):
    base = (view * 3 + dim) * TAPS
    return [w_ref[base + (TAPS - 1 - k if flip else k)] for k in range(TAPS)]


def blur_z(a, b, w):
    lane = lax.broadcasted_iota(jnp.int32, a.shape, 1)
    out_a, out_b = w[HALO] * a, w[HALO] * b
    for s in range(1, HALO + 1):
        keep = lane < BRICK - s
        ra, rb = pltpu.roll(a, BRICK - s, 1), pltpu.roll(b, BRICK - s, 1)
        out_a += w[HALO + s] * jnp.where(keep, ra, rb)
        out_b += w[HALO + s] * jnp.where(keep, rb, 0.0)
        fresh = lane < s
        la, lb = pltpu.roll(a, s, 1), pltpu.roll(b, s, 1)
        out_a += w[HALO - s] * jnp.where(fresh, 0.0, la)
        out_b += w[HALO - s] * jnp.where(fresh, la, lb)
    return out_a, out_b


def y_rows(ref, at, w, n):
    total = w[0] * ref[(*at, pl.ds(TRIM - HALO, n))]
    for k in range(1, TAPS):
        total += w[k] * ref[(*at, pl.ds(TRIM - HALO + k, n))]
    return total


def weigh(layers, w):
    total = w[0] * layers[0]
    for k in range(1, TAPS):
        total += w[k] * layers[k]
    return total


def spread(layers, w, x):
    total = None
    for k in range(TAPS):
        i = x + k - HALO
        if 0 <= i < len(layers):
            term = w[k] * layers[i]
            total = term if total is None else total + term
    return total


def part_kernel(id_ref, est, outer, inner, out_ref, send_in, send_out, wide):
    x_cells, y_cells, _ = est.shape
    part = out_ref.shape[2] - 2 * TILE
    odd = id_ref[2]
    start = pl.multiple_of(id_ref[0] * part, part)
    far = TILE + y_cells
    at_in = pl.ds(pl.multiple_of((1 - odd) * far, TILE), TILE)
    at_out = pl.ds(pl.multiple_of(odd * far, TILE), TILE)

    def body(x, carry):
        for c in range(2):
            lanes = slice(c * BRICK, (c + 1) * BRICK)
            wide[c, TILE:far, :] = est[x, :, lanes]
            wide[c, at_in, :] = inner[x, :, lanes]
            wide[c, at_out, :] = outer[x, :, lanes]
            out_ref[c, x] = wide[c, pl.ds(start, part + 2 * TILE), :]
        return carry

    lax.fori_loop(0, x_cells, body, 0)
    base = x_cells - HALO
    for c in range(2):
        for i in range(HALO):
            send_in[c, i] = out_ref[c, (1 - id_ref[1]) * base + i]
            send_out[c, i] = out_ref[c, id_ref[1] * base + i]


def extend_kernel(id_ref, own, outer, inner, out_ref):
    x_cells = own.shape[1]
    odd = id_ref[1]
    rows = slice(TRIM, own.shape[2] - TRIM)
    base = x_cells + HALO
    for c in range(2):
        for i in range(x_cells):
            out_ref[c, HALO + i] = own[c, i, rows, :]
        for i in range(HALO):
            out_ref[c, (1 - odd) * base + i] = inner[c, i, rows, :]
            out_ref[c, odd * base + i] = outer[c, i, rows, :]


def forward_kernel(w_ref, est, out_ref, partial):
    views, _, x_cells, part, _ = out_ref.shape

    def per_view(u, carry):
        wx, wy, wz = (taps_of(w_ref, u, dim, False) for dim in range(3))

        def per_tile(t, carry):
            at = pl.ds(pl.multiple_of(t * TILE, TILE), TILE)
            for c in range(2):
                layers = [est[c, i, at, :] for i in range(x_cells + 2 * HALO)]
                for x in range(x_cells):
                    partial[c, x, at, :] = weigh(layers[x : x + TAPS], wx)
            return carry

        lax.fori_loop(0, (part + 2 * TRIM) // TILE, per_tile, 0)

        def per_layer(x, carry):
            rows = [y_rows(partial, (c, x), wy, part) for c in range(2)]
            out_ref[u, 0, x], out_ref[u, 1, x] = blur_z(*rows, wz)
            return carry

        lax.fori_loop(0, x_cells, per_layer, 0)
        return carry

    lax.fori_loop(0, views, per_view, 0)


def forward(w, est, views, x_cells):
    rows = est.shape[2]
    return call(
        forward_kernel, "forward", [f32(views, 2, x_cells, rows - 2 * TRIM, BRICK)], (w, est),
        scratch=[pltpu.VMEM((2, x_cells, rows, BRICK), jnp.float32)],
    )[0]


def backward_kernel(w_ref, id_ref, below, obs, out_ref, send_in, send_out, wide, partial):
    views, _, x_cells, part, _ = obs.shape
    layers_out, count = out_ref.shape[1], send_in.shape[1]
    zeros = jnp.zeros((TILE, BRICK), jnp.float32)
    for c in range(2):
        for x in range(x_cells):
            wide[c, x, 0:TILE, :] = zeros
            wide[c, x, TILE + part : 2 * TILE + part, :] = zeros
    out_ref[...] = jnp.zeros_like(out_ref)

    def per_view(u, carry):
        wx, wy, wz = (taps_of(w_ref, u, dim, True) for dim in range(3))

        def per_layer(x, carry):
            rows = blur_z(*(obs[u, c, x] / below[u, c, x] for c in range(2)), wz)
            for c in range(2):
                wide[c, x, TILE : TILE + part, :] = rows[c]
                partial[c, x] = y_rows(wide, (c, x), wy, part + 2 * TRIM)
            return carry

        lax.fori_loop(0, x_cells, per_layer, 0)

        def per_tile(t, carry):
            at = pl.ds(pl.multiple_of(t * TILE, TILE), TILE)
            for c in range(2):
                layers = [partial[c, x, at, :] for x in range(x_cells)]
                for i in range(layers_out):
                    out_ref[c, i, at, :] += spread(layers, wx, i - HALO)
            return carry

        lax.fori_loop(0, (part + 2 * TRIM) // TILE, per_tile, 0)
        return carry

    lax.fori_loop(0, views, per_view, 0)
    odd = id_ref[1]
    base = layers_out - count
    for c in range(2):
        for i in range(count):
            send_in[c, i] = out_ref[c, (1 - odd) * base + i]
            send_out[c, i] = out_ref[c, odd * base + i]


def backward(w, ids, below, obs, count):
    _, _, x, part, _ = obs.shape
    rows = part + 2 * TRIM
    outs = [f32(2, x + 2 * HALO, rows, BRICK)] + [f32(2, count, rows, BRICK)] * 2
    return call(
        backward_kernel, "backward", outs, (w, ids, below, obs), 2,
        scratch=[
            pltpu.VMEM((2, x, part + 2 * TILE, BRICK), jnp.float32),
            pltpu.VMEM((2, x, rows, BRICK), jnp.float32),
        ],
    )


def merge_kernel(id_ref, total, outer, inner, out_ref, send_in, send_out):
    layers, rows = out_ref.shape[1:3]
    count = inner.shape[1]
    skip = (total.shape[1] - layers) // 2
    odd, odd_part = id_ref[1], lax.rem(id_ref[0], 2)
    base = layers - count
    at_in = pl.ds(pl.multiple_of((1 - odd_part) * (rows - TILE), TILE), TILE)
    at_out = pl.ds(pl.multiple_of(odd_part * (rows - TILE), TILE), TILE)
    for c in range(2):
        for i in range(layers):
            out_ref[c, i] = total[c, skip + i]
        for i in range(count):
            out_ref[c, (1 - odd) * base + i] += inner[c, i]
            out_ref[c, odd * base + i] += outer[c, i]
        for i in range(layers):
            send_in[c, i] = out_ref[c, i, at_in, :]
            send_out[c, i] = out_ref[c, i, at_out, :]


def merge(ids, total, outer, inner, layers):
    rows = total.shape[2]
    outs = [f32(2, layers, rows, BRICK)] + [f32(2, layers, TILE, BRICK)] * 2
    return call(merge_kernel, "merge", outs, (ids, total, outer, inner))


def update_kernel(views, id_ref, total, outer, inner, est, out_ref):
    layers, rows = out_ref.shape[1:3]
    odd = lax.rem(id_ref[0], 2)
    at_in = pl.ds(pl.multiple_of((1 - odd) * (rows - TILE), TILE), TILE)
    at_out = pl.ds(pl.multiple_of(odd * (rows - TILE), TILE), TILE)
    for c in range(2):
        for i in range(layers):
            out_ref[c, i] = est[c, i] * total[c, i] / views
            for at, more in ((at_in, inner), (at_out, outer)):
                out_ref[c, i, at, :] = est[c, i, at, :] * (total[c, i, at, :] + more[c, i]) / views


def finish_kernel(views, id_ref, total, outer, inner, est, out_a, out_b, wide):
    layers, rows = total.shape[1:3]
    odd = lax.rem(id_ref[0], 2)
    at_in = pl.ds(pl.multiple_of((1 - odd) * (rows - TILE), TILE), TILE)
    at_out = pl.ds(pl.multiple_of(odd * (rows - TILE), TILE), TILE)
    own = slice(TRIM, rows - TRIM)
    for c, out in ((0, out_a), (1, out_b)):
        for i in range(layers):
            wide[...] = total[c, i]
            wide[at_in, :] += inner[c, i]
            wide[at_out, :] += outer[c, i]
            out[i] = est[c, HALO + i, own, :] * wide[own, :] / views


def join_kernel(views, id_ref, *refs):
    pieces, out_ref = refs[: 2 * views], refs[2 * views]
    part = pieces[0].shape[1]
    for d in range(views):
        at = pl.ds(pl.multiple_of(lax.rem(id_ref[0] + d, views) * part, part), part)
        out_ref[:, at, 0:BRICK] = pieces[2 * d][...]
        out_ref[:, at, BRICK : 2 * BRICK] = pieces[2 * d + 1][...]


def swap(inner, outer, axes):
    count = lax.axis_size(axes)
    links = [(i, i + 1) for i in range(1, count - 1, 2)]
    outer = lax.ppermute(outer, axes, links + [(j, i) for i, j in links])
    inner = lax.ppermute(inner, axes, [(i, i ^ 1) for i in range(count)])
    return outer, inner


def turn(value, step, count):
    return lax.ppermute(value, "views", [(i, (i + step) % count) for i in range(count)])


def per_device(estimate, views_data, target, psf_taps, shifts):
    x_cells, y_cells, z_cells = estimate.shape
    row_count = lax.axis_size("rows")
    block_count = lax.axis_size("blocks")
    peer_count = block_count * row_count
    view_count = lax.axis_size("views")
    brick_cols = z_cells // BRICK
    brick_count = x_cells * y_cells * brick_cols
    capacity = 2 * brick_count // peer_count
    part = y_cells // view_count
    all_cols = y_cells * block_count
    geo = (peer_count, capacity, x_cells, y_cells, brick_cols, row_count, all_cols, view_count)
    block, row, place = (lax.axis_index(name) for name in ("blocks", "rows", "views"))
    odd = block % 2
    est_out, est_in = swap(*(
        lax.dynamic_slice_in_dim(estimate, at * (y_cells - TILE), TILE, 1) for at in (1 - odd, odd)
    ), "blocks")
    outgoing = pack(shifts, target[0].transpose(0, 2, 1), views_data[0], geo)
    outgoing, est_out, est_in = lax.optimization_barrier((outgoing, est_out, est_in))
    arrived = lax.all_to_all(
        outgoing.reshape(peer_count, capacity + 1, 1, BRICK),
        ("blocks", "rows"), split_axis=0, concat_axis=0, tiled=True,
    ).reshape(peer_count * (capacity + 1), 1, BRICK)
    taps = lax.all_gather(psf_taps, "views", axis=0, tiled=True)
    w = (taps / jnp.sum(taps, axis=2, keepdims=True)).reshape(-1)
    ids = jnp.stack([place, row % 2, odd]).astype(jnp.int32)
    halo = f32(2, HALO, part + 2 * TILE, BRICK)
    own, *sent = call(
        part_kernel, "part", [f32(2, x_cells, part + 2 * TILE, BRICK), halo, halo],
        (ids, estimate, est_out, est_in), scratch=[pltpu.VMEM((2, y_cells + 2 * TILE, BRICK), jnp.float32)],
    )
    wide = [f32(2, x_cells + 2 * HALO, part + 2 * TRIM, BRICK)]
    est = call(extend_kernel, "extend", wide, (ids, own, *swap(*sent, "rows")))[0]
    below = forward(w, est, view_count, x_cells)
    arrived, below = lax.optimization_barrier((arrived, below))
    moved = unpack(arrived, peer_count, capacity, brick_count)
    obs = lax.all_to_all(
        moved.reshape(view_count, brick_count // view_count, BRICK),
        "views", split_axis=0, concat_axis=0, tiled=True,
    ).reshape(view_count, brick_cols, x_cells, part, BRICK)
    for iteration in range(ITERS):
        if iteration > 0:
            below = forward(w, est, view_count, x_cells)
        more = iteration < ITERS - 1
        total, *sent = backward(w, ids, below, obs, (2 if more else 1) * HALO)
        layers = x_cells + (2 * HALO if more else 0)
        total, *sent = merge(ids, total, *swap(*sent, "rows"), layers)
        args = (ids, total, *swap(*sent, ("blocks", "views")), est)
        if more:
            est = call(functools.partial(update_kernel, view_count), "update", wide, args)[0]
    own = call(
        functools.partial(finish_kernel, view_count), "finish",
        [f32(x_cells, part, BRICK)] * 2, args,
        scratch=[pltpu.VMEM((part + 2 * TRIM, BRICK), jnp.float32)],
    )
    prev_a, next_b = turn(own[0], 1, view_count), turn(own[1], -1, view_count)
    prev_b, next_a = turn(own[1], 1, view_count), turn(own[0], -1, view_count)
    far_a, far_b = turn(prev_a, 1, view_count), turn(next_b, -1, view_count)
    pieces = (*own, next_a, next_b, far_a, far_b, prev_a, prev_b)
    return call(
        functools.partial(join_kernel, view_count), "join", [f32(x_cells, y_cells, z_cells)],
        (ids, *pieces),
    )[0]


def solution(mesh):
    placed = (
        P("rows", "blocks", None),
        P("views", "rows", "blocks", None),
        P("views", "rows", "blocks", None),
        P("views", None, None),
        P("views"),
    )
    return jax.shard_map(
        per_device, mesh=mesh, in_specs=placed, out_specs=P("rows", "blocks", None), check_vma=False
    )
```

```python
import functools
import jax
import jax.numpy as jnp
from jax import lax
from jax.experimental import pallas as pl
from jax.experimental.pallas import tpu as pltpu
from jax.sharding import PartitionSpec as P

VMEM = pltpu.VMEM
BRICK = 128
HALO = 3
ITERS = 2
GROUP = 16
SPARE = 8
TAPS = 2 * HALO + 1
TILE = 8
TRIM = 4


def lane_sum(x):
    return jnp.sum(x, axis=1, keepdims=True)


def pack_kernel(geo, shift_ref, target_ref, views_ref, out_ref, rolled, pos_v, pos_s, sem):
    peers, cap, x_cells, y_cells, brick_cols, row_count, all_cols, view_count = geo
    groups = brick_cols * x_cells
    rows_per = cap + 1
    t = target_ref[...]
    bz = t % brick_cols
    column = t // brick_cols % all_cols
    line = t // (brick_cols * all_cols)
    dest = column // y_cells * row_count + line // x_cells
    part = y_cells // view_count
    y = column % y_cells
    slot = ((y // part * brick_cols + bz) * x_cells + line % x_cells) * part + y % part + 1
    high, low = slot // 64, slot % 64
    peer_id = lax.broadcasted_iota(jnp.int32, (peers, y_cells), 0)
    before = (
        lax.broadcasted_iota(jnp.int32, (y_cells, y_cells), 0)
        < lax.broadcasted_iota(jnp.int32, (y_cells, y_cells), 1)
    ).astype(jnp.bfloat16)
    kid = lax.broadcasted_iota(jnp.int32, (BRICK, y_cells), 0)
    carry = jnp.zeros((peers, 1), jnp.float32)
    listed = jnp.zeros((2 * peers, BRICK), jnp.float32)
    for g in range(groups):
        here = (g % x_cells, slice(g // x_cells, g // x_cells + 1))
        d = dest[here]
        hot = d == peer_id
        hot_f = hot.astype(jnp.float32)
        ahead = jnp.dot(hot_f.astype(jnp.bfloat16), before, preferred_element_type=jnp.float32)
        ranks = jnp.sum(hot_f * (ahead + carry), axis=0, keepdims=True)
        carry = carry + lane_sum(hot_f)
        rank_i = ranks.astype(jnp.int32)
        pos_v[g : g + 1, :] = d * rows_per + rank_i
        h = hot_f * high[here].astype(jnp.float32)
        l = hot_f * low[here].astype(jnp.float32)
        both = jnp.concatenate([h, l], axis=0).astype(jnp.bfloat16)
        at = (rank_i == kid).astype(jnp.float32).astype(jnp.bfloat16)
        listed = listed + lax.dot_general(
            both, at, (((1,), (1,)), ((), ())), preferred_element_type=jnp.float32
        )
    copy = pltpu.make_async_copy(pos_v, pos_s, sem)
    copy.start()
    entries = 64.0 * listed[:peers] + listed[peers:]
    for p in range(peers):
        out_ref[p * rows_per + cap] = entries[p : p + 1, :]
    shift = shift_ref[0]
    for bz_i in range(brick_cols):
        for x in range(x_cells):
            rolled[bz_i * x_cells + x] = pltpu.roll(
                views_ref[x, :, bz_i * BRICK : (bz_i + 1) * BRICK], shift, 1
            )
    copy.wait()

    def body(g, c):
        for base in range(0, y_cells, GROUP):
            places = [pos_s[g, base + i] for i in range(GROUP)]
            rows = [rolled[g, base + i : base + i + 1, :] for i in range(GROUP)]
            for place, row in zip(places, rows):
                out_ref[place] = row
        return c

    lax.fori_loop(0, groups, body, 0)


def pack(shift, target, views, geo):
    peers, cap, x_cells, y_cells, brick_cols, row_count, all_cols, view_count = geo
    groups = brick_cols * x_cells
    return pl.pallas_call(
        functools.partial(pack_kernel, geo),
        out_shape=jax.ShapeDtypeStruct((peers * (cap + 1), 1, BRICK), jnp.float32),
        in_specs=[
            pl.BlockSpec(memory_space=pltpu.SMEM),
            pl.BlockSpec(memory_space=pltpu.VMEM),
            pl.BlockSpec(memory_space=pltpu.VMEM),
        ],
        out_specs=pl.BlockSpec(memory_space=pltpu.VMEM),
        scratch_shapes=[
            pltpu.VMEM((groups, y_cells, BRICK), jnp.float32),
            pltpu.VMEM((groups, y_cells), jnp.int32),
            pltpu.SMEM((groups, y_cells), jnp.int32),
            pltpu.SemaphoreType.DMA,
        ],
        name="pack",
    )(shift, target, views)


def unpack_kernel(peers, cap, slots, id_ref, in_ref, *refs):
    outs, (placed, list_v, idx_v, idx_s, sem) = refs[:-5], refs[-5:]
    rows_per = cap + 1
    for p in range(peers):
        list_v[p : p + 1, :] = in_ref[p * rows_per + cap]
    e = list_v[...].astype(jnp.int32)
    idx_v[...] = jnp.where(e > 0, e - 1, slots)
    copy = pltpu.make_async_copy(idx_v, idx_s, sem)
    copy.start()
    copy.wait()

    def per_peer(p, c):
        for base in range(0, cap, GROUP):
            places = [idx_s[p, base + i] for i in range(GROUP)]
            rows = [in_ref[p * rows_per + base + i] for i in range(GROUP)]
            for place, row in zip(places, rows):
                placed[pl.ds(place, 1), :] = row
        return c

    lax.fori_loop(0, peers, per_peer, 0)
    views, size = len(outs), slots // len(outs)
    for d, out in enumerate(outs):
        base = pl.multiple_of(lax.rem(id_ref[0] + d, views) * size, size)
        out[...] = placed[pl.ds(base, size), :]


def unpack(ids, arrived, peers, cap, slots, views):
    return call(
        functools.partial(unpack_kernel, peers, cap, slots), "unpack",
        [f32(slots // views, BRICK)] * views, (ids, arrived),
        scratch=[
            pltpu.VMEM((slots + SPARE, BRICK), jnp.float32),
            pltpu.VMEM((peers, BRICK), jnp.float32),
            pltpu.VMEM((peers, BRICK), jnp.int32),
            pltpu.SMEM((peers, BRICK), jnp.int32),
            pltpu.SemaphoreType.DMA,
        ],
    )


def vmem():
    return pl.BlockSpec(memory_space=pltpu.VMEM)


def smem():
    return pl.BlockSpec(memory_space=pltpu.SMEM)


def f32(*shape):
    return jax.ShapeDtypeStruct(shape, jnp.float32)


def call(kernel, name, outs, args, scalars=1, scratch=(), work=1000):
    return pl.pallas_call(
        kernel,
        out_shape=outs,
        in_specs=[smem()] * scalars + [vmem()] * (len(args) - scalars),
        out_specs=[vmem()] * len(outs),
        scratch_shapes=list(scratch),
        cost_estimate=pl.CostEstimate(flops=work, bytes_accessed=work, transcendentals=0),
        compiler_params=pltpu.CompilerParams(vmem_limit_bytes=32 * 1024 * 1024),
        name=name,
    )(*args)


def taps_of(w_ref, view, dim, flip):
    base = (view * 3 + dim) * TAPS
    return [w_ref[base + (TAPS - 1 - k if flip else k)] for k in range(TAPS)]


def blur_z(a, b, w):
    lane = lax.broadcasted_iota(jnp.int32, a.shape, 1)
    out_a, out_b = w[HALO] * a, w[HALO] * b
    for s in range(1, HALO + 1):
        keep = lane < BRICK - s
        ra, rb = pltpu.roll(a, BRICK - s, 1), pltpu.roll(b, BRICK - s, 1)
        out_a += w[HALO + s] * jnp.where(keep, ra, rb)
        out_b += w[HALO + s] * jnp.where(keep, rb, 0.0)
        fresh = lane < s
        la, lb = pltpu.roll(a, s, 1), pltpu.roll(b, s, 1)
        out_a += w[HALO - s] * jnp.where(fresh, 0.0, la)
        out_b += w[HALO - s] * jnp.where(fresh, la, lb)
    return out_a, out_b


def y_rows(ref, at, w, n):
    total = w[0] * ref[(*at, pl.ds(TRIM - HALO, n))]
    for k in range(1, TAPS):
        total += w[k] * ref[(*at, pl.ds(TRIM - HALO + k, n))]
    return total


def weigh(layers, w):
    total = w[0] * layers[0]
    for k in range(1, TAPS):
        total += w[k] * layers[k]
    return total


def spread(layers, w, x):
    total = None
    for k in range(TAPS):
        i = x + k - HALO
        if 0 <= i < len(layers):
            term = w[k] * layers[i]
            total = term if total is None else total + term
    return total


def part_kernel(id_ref, est, edge, out_ref, send_in, send_out, wide):
    x_cells, y_cells, _ = est.shape
    part = out_ref.shape[2] - 2 * TILE
    start = pl.multiple_of(id_ref[0] * part, part)
    far = TILE + y_cells

    def body(x, carry):
        for c in range(2):
            lanes = slice(c * BRICK, (c + 1) * BRICK)
            wide[c, TILE:far, :] = est[x, :, lanes]
            wide[c, 0:TILE, :] = edge[x, :, lanes]
            wide[c, far : far + TILE, :] = edge[x, :, lanes]
            out_ref[c, x] = wide[c, pl.ds(start, part + 2 * TILE), :]
        return carry

    lax.fori_loop(0, x_cells, body, 0)
    base = x_cells - HALO
    for c in range(2):
        for i in range(HALO):
            send_in[c, i] = out_ref[c, (1 - id_ref[1]) * base + i]
            send_out[c, i] = out_ref[c, id_ref[1] * base + i]


def extend_kernel(id_ref, own, outer, inner, out_ref):
    x_cells = own.shape[1]
    odd = id_ref[1]
    rows = slice(TRIM, own.shape[2] - TRIM)
    base = x_cells + HALO
    for c in range(2):
        for i in range(x_cells):
            out_ref[c, HALO + i] = own[c, i, rows, :]
        for i in range(HALO):
            out_ref[c, (1 - odd) * base + i] = inner[c, i, rows, :]
            out_ref[c, odd * base + i] = outer[c, i, rows, :]


def forward_kernel(w_ref, est, out_ref, partial):
    views, _, x_cells, part, _ = out_ref.shape

    def per_view(u, carry):
        wx, wy, wz = (taps_of(w_ref, u, dim, False) for dim in range(3))

        def per_tile(t, carry):
            at = pl.ds(pl.multiple_of(t * TILE, TILE), TILE)
            for c in range(2):
                layers = [est[c, i, at, :] for i in range(x_cells + 2 * HALO)]
                for x in range(x_cells):
                    partial[c, x, at, :] = weigh(layers[x : x + TAPS], wx)
            return carry

        lax.fori_loop(0, (part + 2 * TRIM) // TILE, per_tile, 0)

        def per_layer(x, carry):
            rows = [y_rows(partial, (c, x), wy, part) for c in range(2)]
            out_ref[u, 0, x], out_ref[u, 1, x] = blur_z(*rows, wz)
            return carry

        lax.fori_loop(0, x_cells, per_layer, 0)
        return carry

    lax.fori_loop(0, views, per_view, 0)


def forward(w, est, views, x_cells):
    rows = est.shape[2]
    return call(
        forward_kernel, "forward", [f32(views, 2, x_cells, rows - 2 * TRIM, BRICK)], (w, est),
        scratch=[pltpu.VMEM((2, x_cells, rows, BRICK), jnp.float32)],
    )[0]


def blur_x_tile(est, at, wx, out, c, x_cells, rows):
    layers = [est[c, i, at, :] for i in range(x_cells + 2 * HALO)]
    for x in range(x_cells):
        out[c, x, rows, :] = weigh(layers[x : x + TAPS], wx)


def middle_kernel(w_ref, est, total, out_ref, part_ref, fresh):
    views, _, x_cells, part, _ = out_ref.shape
    tall = part_ref.shape[3]
    rows = slice(TILE, TILE + tall)
    for c in range(2):
        for i in range(x_cells + 2 * HALO):
            fresh[c, i] = est[c, i, rows, :] * total[c, i, rows, :] / views

    def per_view(u, carry):
        wx, wy, wz = (taps_of(w_ref, u, dim, False) for dim in range(3))

        def per_tile(t, carry):
            at = pl.ds(pl.multiple_of(t * TILE, TILE), TILE)
            for c in range(2):
                blur_x_tile(fresh, at, wx, part_ref.at[u], c, x_cells, at)
            return carry

        lax.fori_loop(0, tall // TILE, per_tile, 0)

        def per_layer(x, carry):
            rows = [y_rows(part_ref, (u, c, x), wy, part) for c in range(2)]
            out_ref[u, 0, x], out_ref[u, 1, x] = blur_z(*rows, wz)
            return carry

        lax.fori_loop(0, x_cells, per_layer, 0)
        return carry

    lax.fori_loop(0, views, per_view, 0)


def middle(w, est, total, views, x_cells):
    tall = est.shape[2] - 2 * TILE
    return call(
        middle_kernel, "middle",
        [f32(views, 2, x_cells, tall - TILE, BRICK), f32(views, 2, x_cells, tall, BRICK)],
        (w, est, total), scratch=[pltpu.VMEM((2, x_cells + 2 * HALO, tall, BRICK), jnp.float32)],
    )


def ends_kernel(w_ref, est, mid, part_ref, out_ref, strip):
    views, _, x_cells, part, _ = out_ref.shape
    tall = part_ref.shape[3]
    sides = ((0, 0, 0, TILE, 0), (tall + TILE, TILE, tall - TILE, 0, part - TILE))

    def per_view(u, carry):
        wx, wy, wz = (taps_of(w_ref, u, dim, False) for dim in range(3))
        for s, (at, here, kept, there, to) in enumerate(sides):
            for c in range(2):
                blur_x_tile(est, slice(at, at + TILE), wx, strip.at[s], c, x_cells, slice(here, here + TILE))

        def per_layer(x, carry):
            for s, (at, here, kept, there, to) in enumerate(sides):
                for c in range(2):
                    strip[s, c, x, there : there + TILE, :] = part_ref[u, c, x, kept : kept + TILE, :]
                rows = blur_z(*(y_rows(strip, (s, c, x), wy, TILE) for c in range(2)), wz)
                for c in range(2):
                    out_ref[u, c, x, to : to + TILE, :] = rows[c]
            for c in range(2):
                out_ref[u, c, x, TILE : part - TILE, :] = mid[u, c, x]
            return carry

        lax.fori_loop(0, x_cells, per_layer, 0)
        return carry

    lax.fori_loop(0, views, per_view, 0)


def ends(w, est, mid, partial):
    views, _, x, tall, _ = partial.shape
    return call(
        ends_kernel, "ends", [f32(views, 2, x, tall + TILE, BRICK)], (w, est, mid, partial),
        scratch=[pltpu.VMEM((2, 2, x, 2 * TILE, BRICK), jnp.float32)],
    )[0]


def backward_kernel(views, rels, add, w_ref, id_ref, below, *refs):
    observed, refs = refs[: len(rels)], refs[len(rels) :]
    before, refs = (refs[0], refs[1:]) if add else (None, refs)
    out_ref, *sends = refs[:-2]
    wide, partial = refs[-2:]
    x_cells, part = below.shape[2:4]
    layers_out = out_ref.shape[1]
    zeros = jnp.zeros((TILE, BRICK), jnp.float32)
    for c in range(2):
        for x in range(x_cells):
            wide[c, x, 0:TILE, :] = zeros
            wide[c, x, TILE + part : 2 * TILE + part, :] = zeros
    for d, obs in zip(rels, observed):
        u = lax.rem(id_ref[0] + d, views)
        wx, wy, wz = (taps_of(w_ref, u, dim, True) for dim in range(3))

        def per_layer(x, carry, u=u, obs=obs, wy=wy, wz=wz):
            rows = blur_z(*(obs[c, x] / below[u, c, x] for c in range(2)), wz)
            for c in range(2):
                wide[c, x, TILE : TILE + part, :] = rows[c]
                partial[c, x] = y_rows(wide, (c, x), wy, part + 2 * TRIM)
            return carry

        lax.fori_loop(0, x_cells, per_layer, 0)

        def per_tile(t, carry, wx=wx, source=before):
            at = pl.ds(pl.multiple_of(t * TILE, TILE), TILE)
            for c in range(2):
                layers = [partial[c, x, at, :] for x in range(x_cells)]
                for i in range(layers_out):
                    value = spread(layers, wx, i - HALO)
                    out_ref[c, i, at, :] = value if source is None else value + source[c, i, at, :]
            return carry

        lax.fori_loop(0, (part + 2 * TRIM) // TILE, per_tile, 0)
        before = out_ref
    odd = id_ref[1]
    for slot, send in enumerate(sends):
        base = layers_out - send.shape[1]
        for c in range(2):
            for i in range(send.shape[1]):
                send[c, i] = out_ref[c, (odd if slot else 1 - odd) * base + i]


def backward(w, ids, below, rels, observed, before, count):
    views, _, x, part, _ = below.shape
    rows = part + 2 * TRIM
    outs = [f32(2, x + 2 * HALO, rows, BRICK)] + [f32(2, count, rows, BRICK)] * (2 if count else 0)
    given = () if before is None else (before,)
    return call(
        functools.partial(backward_kernel, views, rels, before is not None), "backward", outs,
        (w, ids, below, *observed, *given), 2,
        scratch=[
            pltpu.VMEM((2, x, part + 2 * TILE, BRICK), jnp.float32),
            pltpu.VMEM((2, x, rows, BRICK), jnp.float32),
        ],
    )


def merge_kernel(id_ref, total, outer, inner, out_ref, send_in, send_out):
    layers, rows = out_ref.shape[1:3]
    count = inner.shape[1]
    skip = (total.shape[1] - layers) // 2
    odd, odd_part = id_ref[1], lax.rem(id_ref[0], 2)
    base = layers - count
    at_in = pl.ds(pl.multiple_of((1 - odd_part) * (rows - TILE), TILE), TILE)
    at_out = pl.ds(pl.multiple_of(odd_part * (rows - TILE), TILE), TILE)
    for c in range(2):
        for i in range(layers):
            out_ref[c, i] = total[c, skip + i]
        for i in range(count):
            out_ref[c, (1 - odd) * base + i] += inner[c, i]
            out_ref[c, odd * base + i] += outer[c, i]
        for i in range(layers):
            send_in[c, i] = out_ref[c, i, at_in, :]
            send_out[c, i] = out_ref[c, i, at_out, :]


def merge(ids, total, outer, inner, layers):
    rows = total.shape[2]
    outs = [f32(2, layers, rows, BRICK)] + [f32(2, layers, TILE, BRICK)] * 2
    return call(merge_kernel, "merge", outs, (ids, total, outer, inner))


def update_kernel(views, id_ref, total, outer, inner, est, out_ref):
    layers, rows = out_ref.shape[1:3]
    odd = lax.rem(id_ref[0], 2)
    at_in = pl.ds(pl.multiple_of((1 - odd) * (rows - TILE), TILE), TILE)
    at_out = pl.ds(pl.multiple_of(odd * (rows - TILE), TILE), TILE)
    for c in range(2):
        for i in range(layers):
            out_ref[c, i] = est[c, i] * total[c, i] / views
            for at, more in ((at_in, inner), (at_out, outer)):
                out_ref[c, i, at, :] = est[c, i, at, :] * (total[c, i, at, :] + more[c, i]) / views


def finish_kernel(views, id_ref, total, outer, inner, est, out_a, out_b, wide):
    layers, rows = total.shape[1:3]
    odd = lax.rem(id_ref[0], 2)
    at_in = pl.ds(pl.multiple_of((1 - odd) * (rows - TILE), TILE), TILE)
    at_out = pl.ds(pl.multiple_of(odd * (rows - TILE), TILE), TILE)
    own = slice(TRIM, rows - TRIM)
    for c, out in ((0, out_a), (1, out_b)):
        for i in range(layers):
            wide[...] = total[c, i]
            wide[at_in, :] += inner[c, i]
            wide[at_out, :] += outer[c, i]
            out[i] = est[c, HALO + i, own, :] * wide[own, :] / views


def join_kernel(views, id_ref, *refs):
    pieces, out_ref = refs[: 2 * views], refs[2 * views]
    part = pieces[0].shape[1]
    for d in range(views):
        at = pl.ds(pl.multiple_of(lax.rem(id_ref[0] + d, views) * part, part), part)
        out_ref[:, at, 0:BRICK] = pieces[2 * d][...]
        out_ref[:, at, BRICK : 2 * BRICK] = pieces[2 * d + 1][...]


def swap(inner, outer, axes):
    count = lax.axis_size(axes)
    links = [(i, i + 1) for i in range(1, count - 1, 2)]
    outer = lax.ppermute(outer, axes, links + [(j, i) for i, j in links])
    inner = lax.ppermute(inner, axes, [(i, i ^ 1) for i in range(count)])
    return outer, inner


def turn(value, step, count):
    return lax.ppermute(value, "views", [(i, (i + step) % count) for i in range(count)])


def per_device(estimate, views_data, target, psf_taps, shifts):
    x_cells, y_cells, z_cells = estimate.shape
    row_count = lax.axis_size("rows")
    block_count = lax.axis_size("blocks")
    peer_count = block_count * row_count
    view_count = lax.axis_size("views")
    brick_cols = z_cells // BRICK
    brick_count = x_cells * y_cells * brick_cols
    capacity = 2 * brick_count // peer_count
    part = y_cells // view_count
    all_cols = y_cells * block_count
    geo = (peer_count, capacity, x_cells, y_cells, brick_cols, row_count, all_cols, view_count)
    row, place = lax.axis_index("rows"), lax.axis_index("views")
    chain = [(block * view_count - 1, block * view_count) for block in range(1, block_count)]
    edge_at = jnp.where(place == 0, 0, y_cells - TILE)
    edge = lax.ppermute(
        lax.dynamic_slice_in_dim(estimate, edge_at, TILE, 1),
        ("blocks", "views"), chain + [(j, i) for i, j in chain],
    )
    outgoing = pack(shifts, target[0].transpose(0, 2, 1), views_data[0], geo)
    outgoing, edge = lax.optimization_barrier((outgoing, edge))
    arrived = lax.all_to_all(
        outgoing.reshape(peer_count, capacity + 1, 1, BRICK),
        ("blocks", "rows"), split_axis=0, concat_axis=0, tiled=True,
    ).reshape(peer_count * (capacity + 1), 1, BRICK)
    taps = lax.all_gather(psf_taps, "views", axis=0, tiled=True)
    w = (taps / jnp.sum(taps, axis=2, keepdims=True)).reshape(-1)
    ids = jnp.stack([place, row % 2]).astype(jnp.int32)
    halo = f32(2, HALO, part + 2 * TILE, BRICK)
    own, *sent = call(
        part_kernel, "part", [f32(2, x_cells, part + 2 * TILE, BRICK), halo, halo],
        (ids, estimate, edge),
        scratch=[pltpu.VMEM((2, y_cells + 2 * TILE, BRICK), jnp.float32)],
    )
    wide = [f32(2, x_cells + 2 * HALO, part + 2 * TRIM, BRICK)]
    est = call(extend_kernel, "extend", wide, (ids, own, *swap(*sent, "rows")))[0]
    below = forward(w, est, view_count, x_cells)
    arrived, below = lax.optimization_barrier((arrived, below))
    moved = unpack(ids, arrived, peer_count, capacity, brick_count, view_count)
    moved = [m.reshape(brick_cols, x_cells, part, BRICK) for m in moved]
    behind, ahead = turn(moved[1], 1, view_count), turn(moved[3], -1, view_count)
    across = turn(moved[2], 2, view_count)
    total = backward(w, ids, below, (0,), moved[:1], None, 0)[0]
    total = backward(w, ids, below, (3, 1), (behind, ahead), total, 0)[0]
    total, *sent = backward(w, ids, below, (2,), (across,), total, 2 * HALO)
    total, *sent = merge(ids, total, *swap(*sent, "rows"), x_cells + 2 * HALO)
    mid, partial = middle(w, est, total, view_count, x_cells)
    args = (ids, total, *swap(*sent, ("blocks", "views")), est)
    est = call(functools.partial(update_kernel, view_count), "update", wide, args)[0]
    below = ends(w, est, mid, partial)
    observed = (moved[0], ahead, across, behind)
    total, *sent = backward(w, ids, below, (0, 1, 2, 3), observed, None, HALO)
    total, *sent = merge(ids, total, *swap(*sent, "rows"), x_cells)
    args = (ids, total, *swap(*sent, ("blocks", "views")), est)
    own = call(
        functools.partial(finish_kernel, view_count), "finish",
        [f32(x_cells, part, BRICK)] * 2, args,
        scratch=[pltpu.VMEM((part + 2 * TRIM, BRICK), jnp.float32)],
    )
    prev_a, next_b = turn(own[0], 1, view_count), turn(own[1], -1, view_count)
    prev_b, next_a = turn(own[1], 1, view_count), turn(own[0], -1, view_count)
    far_a, far_b = turn(prev_a, 1, view_count), turn(next_b, -1, view_count)
    pieces = (*own, next_a, next_b, far_a, far_b, prev_a, prev_b)
    return call(
        functools.partial(join_kernel, view_count), "join", [f32(x_cells, y_cells, z_cells)],
        (ids, *pieces),
    )[0]


def solution(mesh):
    placed = (
        P("rows", "blocks", None),
        P("views", "rows", "blocks", None),
        P("views", "rows", "blocks", None),
        P("views", None, None),
        P("views"),
    )
    return jax.shard_map(
        per_device, mesh=mesh, in_specs=placed, out_specs=P("rows", "blocks", None), check_vma=False
    )
```

```python
import functools
import jax
import jax.numpy as jnp
from jax import lax
from jax.experimental import pallas as pl
from jax.experimental.pallas import tpu as pltpu
from jax.sharding import PartitionSpec as P

VMEM = pltpu.VMEM
BRICK = 128
HALO = 3
ITERS = 2
GROUP = 16
SPARE = 8
TAPS = 2 * HALO + 1
TILE = 8
TRIM = 4


def lane_sum(x):
    return jnp.sum(x, axis=1, keepdims=True)


def pack_kernel(geo, shift_ref, id_ref, target_ref, views_ref, out_ref, rolled, pos_v, pos_s, sem):
    peers, cap, x_cells, y_cells, brick_cols, row_count, all_cols, view_count = geo
    groups = brick_cols * x_cells
    rows_per = cap + 1
    t = target_ref[...]
    bz = t % brick_cols
    column = t // brick_cols % all_cols
    line = t // (brick_cols * all_cols)
    dest = column // y_cells * row_count + line // x_cells
    part = y_cells // view_count
    y = column % y_cells
    turned = (y // part + view_count - id_ref[0]) % view_count
    slot = ((turned * brick_cols + bz) * x_cells + line % x_cells) * part + y % part + 1
    high, low = slot // 64, slot % 64
    peer_id = lax.broadcasted_iota(jnp.int32, (peers, y_cells), 0)
    before = (
        lax.broadcasted_iota(jnp.int32, (y_cells, y_cells), 0)
        < lax.broadcasted_iota(jnp.int32, (y_cells, y_cells), 1)
    ).astype(jnp.bfloat16)
    kid = lax.broadcasted_iota(jnp.int32, (BRICK, y_cells), 0)
    carry = jnp.zeros((peers, 1), jnp.float32)
    listed = jnp.zeros((2 * peers, BRICK), jnp.float32)
    for g in range(groups):
        here = (g % x_cells, slice(g // x_cells, g // x_cells + 1))
        d = dest[here]
        hot = d == peer_id
        hot_f = hot.astype(jnp.float32)
        ahead = jnp.dot(hot_f.astype(jnp.bfloat16), before, preferred_element_type=jnp.float32)
        ranks = jnp.sum(hot_f * (ahead + carry), axis=0, keepdims=True)
        carry = carry + lane_sum(hot_f)
        rank_i = ranks.astype(jnp.int32)
        pos_v[g : g + 1, :] = d * rows_per + rank_i
        h = hot_f * high[here].astype(jnp.float32)
        l = hot_f * low[here].astype(jnp.float32)
        both = jnp.concatenate([h, l], axis=0).astype(jnp.bfloat16)
        at = (rank_i == kid).astype(jnp.float32).astype(jnp.bfloat16)
        listed = listed + lax.dot_general(
            both, at, (((1,), (1,)), ((), ())), preferred_element_type=jnp.float32
        )
    copy = pltpu.make_async_copy(pos_v, pos_s, sem)
    copy.start()
    entries = 64.0 * listed[:peers] + listed[peers:]
    for p in range(peers):
        out_ref[p * rows_per + cap] = entries[p : p + 1, :]
    shift = shift_ref[0]
    for bz_i in range(brick_cols):
        for x in range(x_cells):
            rolled[bz_i * x_cells + x] = pltpu.roll(
                views_ref[x, :, bz_i * BRICK : (bz_i + 1) * BRICK], shift, 1
            )
    copy.wait()

    def body(g, c):
        for base in range(0, y_cells, GROUP):
            places = [pos_s[g, base + i] for i in range(GROUP)]
            rows = [rolled[g, base + i : base + i + 1, :] for i in range(GROUP)]
            for place, row in zip(places, rows):
                out_ref[place] = row
        return c

    lax.fori_loop(0, groups, body, 0)


def pack(shift, ids, target, views, geo):
    peers, cap, x_cells, y_cells, brick_cols, row_count, all_cols, view_count = geo
    groups = brick_cols * x_cells
    return pl.pallas_call(
        functools.partial(pack_kernel, geo),
        out_shape=jax.ShapeDtypeStruct((peers * (cap + 1), 1, BRICK), jnp.float32),
        in_specs=[
            pl.BlockSpec(memory_space=pltpu.SMEM),
            pl.BlockSpec(memory_space=pltpu.SMEM),
            pl.BlockSpec(memory_space=pltpu.VMEM),
            pl.BlockSpec(memory_space=pltpu.VMEM),
        ],
        out_specs=pl.BlockSpec(memory_space=pltpu.VMEM),
        scratch_shapes=[
            pltpu.VMEM((groups, y_cells, BRICK), jnp.float32),
            pltpu.VMEM((groups, y_cells), jnp.int32),
            pltpu.SMEM((groups, y_cells), jnp.int32),
            pltpu.SemaphoreType.DMA,
        ],
        name="pack",
    )(shift, ids, target, views)


def unpack_kernel(peers, cap, slots, in_ref, *refs):
    outs, (placed, list_v, idx_v, idx_s, sem) = refs[:-5], refs[-5:]
    rows_per = cap + 1
    for p in range(peers):
        list_v[p : p + 1, :] = in_ref[p * rows_per + cap]
    e = list_v[...].astype(jnp.int32)
    idx_v[...] = jnp.where(e > 0, e - 1, slots)
    copy = pltpu.make_async_copy(idx_v, idx_s, sem)
    copy.start()
    copy.wait()

    def per_peer(p, c):
        for base in range(0, cap, GROUP):
            places = [idx_s[p, base + i] for i in range(GROUP)]
            rows = [in_ref[p * rows_per + base + i] for i in range(GROUP)]
            for place, row in zip(places, rows):
                placed[pl.ds(place, 1), :] = row
        return c

    lax.fori_loop(0, peers, per_peer, 0)
    views, size = len(outs), slots // len(outs)
    for d, out in enumerate(outs):
        out[...] = placed[d * size : (d + 1) * size, :]


def unpack(arrived, peers, cap, slots, views):
    return call(
        functools.partial(unpack_kernel, peers, cap, slots), "unpack",
        [f32(slots // views, BRICK)] * views, (arrived,), 0,
        scratch=[
            pltpu.VMEM((slots + SPARE, BRICK), jnp.float32),
            pltpu.VMEM((peers, BRICK), jnp.float32),
            pltpu.VMEM((peers, BRICK), jnp.int32),
            pltpu.SMEM((peers, BRICK), jnp.int32),
            pltpu.SemaphoreType.DMA,
        ],
    )


def vmem():
    return pl.BlockSpec(memory_space=pltpu.VMEM)


def smem():
    return pl.BlockSpec(memory_space=pltpu.SMEM)


def f32(*shape):
    return jax.ShapeDtypeStruct(shape, jnp.float32)


def call(kernel, name, outs, args, scalars=1, scratch=(), work=1000):
    return pl.pallas_call(
        kernel,
        out_shape=outs,
        in_specs=[smem()] * scalars + [vmem()] * (len(args) - scalars),
        out_specs=[vmem()] * len(outs),
        scratch_shapes=list(scratch),
        cost_estimate=pl.CostEstimate(flops=work, bytes_accessed=work, transcendentals=0),
        compiler_params=pltpu.CompilerParams(vmem_limit_bytes=32 * 1024 * 1024),
        name=name,
    )(*args)


def taps_of(w_ref, view, dim, flip):
    base = (view * 3 + dim) * TAPS
    return [w_ref[base + (TAPS - 1 - k if flip else k)] for k in range(TAPS)]


def blur_z(a, b, w):
    lane = lax.broadcasted_iota(jnp.int32, a.shape, 1)
    out_a, out_b = w[HALO] * a, w[HALO] * b
    for s in range(1, HALO + 1):
        keep = lane < BRICK - s
        ra, rb = pltpu.roll(a, BRICK - s, 1), pltpu.roll(b, BRICK - s, 1)
        out_a += w[HALO + s] * jnp.where(keep, ra, rb)
        out_b += w[HALO + s] * jnp.where(keep, rb, 0.0)
        fresh = lane < s
        la, lb = pltpu.roll(a, s, 1), pltpu.roll(b, s, 1)
        out_a += w[HALO - s] * jnp.where(fresh, 0.0, la)
        out_b += w[HALO - s] * jnp.where(fresh, la, lb)
    return out_a, out_b


def y_rows(ref, at, w, n):
    total = w[0] * ref[(*at, pl.ds(TRIM - HALO, n))]
    for k in range(1, TAPS):
        total += w[k] * ref[(*at, pl.ds(TRIM - HALO + k, n))]
    return total


def weigh(layers, w):
    total = w[0] * layers[0]
    for k in range(1, TAPS):
        total += w[k] * layers[k]
    return total


def spread(layers, w, x):
    total = None
    for k in range(TAPS):
        i = x + k - HALO
        if 0 <= i < len(layers):
            term = w[k] * layers[i]
            total = term if total is None else total + term
    return total


def part_kernel(id_ref, est, edge, out_ref, send_in, send_out, wide):
    x_cells, y_cells, _ = est.shape
    part = out_ref.shape[2] - 2 * TILE
    start = pl.multiple_of(id_ref[0] * part, part)
    far = TILE + y_cells

    def body(x, carry):
        for c in range(2):
            lanes = slice(c * BRICK, (c + 1) * BRICK)
            wide[c, TILE:far, :] = est[x, :, lanes]
            wide[c, 0:TILE, :] = edge[x, :, lanes]
            wide[c, far : far + TILE, :] = edge[x, :, lanes]
            out_ref[c, x] = wide[c, pl.ds(start, part + 2 * TILE), :]
        return carry

    lax.fori_loop(0, x_cells, body, 0)
    base = x_cells - HALO
    for c in range(2):
        for i in range(HALO):
            send_in[c, i] = out_ref[c, (1 - id_ref[1]) * base + i]
            send_out[c, i] = out_ref[c, id_ref[1] * base + i]


def extend_kernel(id_ref, own, outer, inner, out_ref):
    x_cells = own.shape[1]
    odd = id_ref[1]
    rows = slice(TRIM, own.shape[2] - TRIM)
    base = x_cells + HALO
    for c in range(2):
        for i in range(x_cells):
            out_ref[c, HALO + i] = own[c, i, rows, :]
        for i in range(HALO):
            out_ref[c, (1 - odd) * base + i] = inner[c, i, rows, :]
            out_ref[c, odd * base + i] = outer[c, i, rows, :]


def forward_kernel(w_ref, est, out_ref, partial):
    views, _, x_cells, part, _ = out_ref.shape

    def per_view(u, carry):
        wx, wy, wz = (taps_of(w_ref, u, dim, False) for dim in range(3))

        def per_tile(t, carry):
            at = pl.ds(pl.multiple_of(t * TILE, TILE), TILE)
            for c in range(2):
                layers = [est[c, i, at, :] for i in range(x_cells + 2 * HALO)]
                for x in range(x_cells):
                    partial[c, x, at, :] = weigh(layers[x : x + TAPS], wx)
            return carry

        lax.fori_loop(0, (part + 2 * TRIM) // TILE, per_tile, 0, unroll=True)

        def per_layer(x, carry):
            rows = [y_rows(partial, (c, x), wy, part) for c in range(2)]
            out_ref[u, 0, x], out_ref[u, 1, x] = blur_z(*rows, wz)
            return carry

        lax.fori_loop(0, x_cells, per_layer, 0, unroll=True)
        return carry

    lax.fori_loop(0, views, per_view, 0)


def forward(w, est, views, x_cells):
    rows = est.shape[2]
    return call(
        forward_kernel, "forward", [f32(views, 2, x_cells, rows - 2 * TRIM, BRICK)], (w, est),
        scratch=[pltpu.VMEM((2, x_cells, rows, BRICK), jnp.float32)],
    )[0]


def backward_kernel(views, rels, add, w_ref, id_ref, below, *refs):
    observed, refs = refs[: len(rels)], refs[len(rels) :]
    before, refs = (refs[0], refs[1:]) if add else (None, refs)
    out_ref, *sends = refs[:-2]
    wide, partial = refs[-2:]
    x_cells, part = below.shape[2:4]
    layers_out = out_ref.shape[1]
    zeros = jnp.zeros((TILE, BRICK), jnp.float32)
    for c in range(2):
        for x in range(x_cells):
            wide[c, x, 0:TILE, :] = zeros
            wide[c, x, TILE + part : 2 * TILE + part, :] = zeros
    for d, obs in zip(rels, observed):
        u = lax.rem(id_ref[0] + d, views)
        wx, wy, wz = (taps_of(w_ref, u, dim, True) for dim in range(3))

        def per_layer(x, carry, u=u, obs=obs, wy=wy, wz=wz):
            rows = blur_z(*(obs[c, x] / below[u, c, x] for c in range(2)), wz)
            for c in range(2):
                wide[c, x, TILE : TILE + part, :] = rows[c]
                partial[c, x] = y_rows(wide, (c, x), wy, part + 2 * TRIM)
            return carry

        lax.fori_loop(0, x_cells, per_layer, 0, unroll=True)

        def per_tile(t, carry, wx=wx, source=before):
            at = pl.ds(pl.multiple_of(t * TILE, TILE), TILE)
            for c in range(2):
                layers = [partial[c, x, at, :] for x in range(x_cells)]
                for i in range(layers_out):
                    value = spread(layers, wx, i - HALO)
                    out_ref[c, i, at, :] = value if source is None else value + source[c, i, at, :]
            return carry

        lax.fori_loop(0, (part + 2 * TRIM) // TILE, per_tile, 0, unroll=True)
        before = out_ref
    odd = id_ref[1]
    for slot, send in enumerate(sends):
        base = layers_out - send.shape[1]
        for c in range(2):
            for i in range(send.shape[1]):
                send[c, i] = out_ref[c, (odd if slot else 1 - odd) * base + i]


def backward(w, ids, below, rels, observed, before, count):
    views, _, x, part, _ = below.shape
    rows = part + 2 * TRIM
    outs = [f32(2, x + 2 * HALO, rows, BRICK)] + [f32(2, count, rows, BRICK)] * (2 if count else 0)
    given = () if before is None else (before,)
    return call(
        functools.partial(backward_kernel, views, rels, before is not None), "backward", outs,
        (w, ids, below, *observed, *given), 2,
        scratch=[
            pltpu.VMEM((2, x, part + 2 * TILE, BRICK), jnp.float32),
            pltpu.VMEM((2, x, rows, BRICK), jnp.float32),
        ],
    )


def merge_kernel(id_ref, total, outer, inner, out_ref, send_in, send_out):
    layers, rows = out_ref.shape[1:3]
    count = inner.shape[1]
    skip = (total.shape[1] - layers) // 2
    odd, odd_part = id_ref[1], lax.rem(id_ref[0], 2)
    base = layers - count
    at_in = pl.ds(pl.multiple_of((1 - odd_part) * (rows - TILE), TILE), TILE)
    at_out = pl.ds(pl.multiple_of(odd_part * (rows - TILE), TILE), TILE)
    for c in range(2):
        for i in range(layers):
            out_ref[c, i] = total[c, skip + i]
        for i in range(count):
            out_ref[c, (1 - odd) * base + i] += inner[c, i]
            out_ref[c, odd * base + i] += outer[c, i]
        for i in range(layers):
            send_in[c, i] = out_ref[c, i, at_in, :]
            send_out[c, i] = out_ref[c, i, at_out, :]


def merge(ids, total, outer, inner, layers):
    rows = total.shape[2]
    outs = [f32(2, layers, rows, BRICK)] + [f32(2, layers, TILE, BRICK)] * 2
    return call(merge_kernel, "merge", outs, (ids, total, outer, inner))


def update_kernel(views, id_ref, total, outer, inner, est, out_ref):
    layers, rows = out_ref.shape[1:3]
    odd = lax.rem(id_ref[0], 2)
    at_in = pl.ds(pl.multiple_of((1 - odd) * (rows - TILE), TILE), TILE)
    at_out = pl.ds(pl.multiple_of(odd * (rows - TILE), TILE), TILE)
    for c in range(2):
        for i in range(layers):
            out_ref[c, i] = est[c, i] * total[c, i] / views
            for at, more in ((at_in, inner), (at_out, outer)):
                out_ref[c, i, at, :] = est[c, i, at, :] * (total[c, i, at, :] + more[c, i]) / views


def finish_kernel(views, id_ref, total, outer, inner, est, out_a, out_b, wide):
    layers, rows = total.shape[1:3]
    odd = lax.rem(id_ref[0], 2)
    at_in = pl.ds(pl.multiple_of((1 - odd) * (rows - TILE), TILE), TILE)
    at_out = pl.ds(pl.multiple_of(odd * (rows - TILE), TILE), TILE)
    own = slice(TRIM, rows - TRIM)
    for c, out in ((0, out_a), (1, out_b)):
        for i in range(layers):
            wide[...] = total[c, i]
            wide[at_in, :] += inner[c, i]
            wide[at_out, :] += outer[c, i]
            out[i] = est[c, HALO + i, own, :] * wide[own, :] / views


def join_kernel(views, id_ref, *refs):
    pieces, out_ref = refs[: 2 * views], refs[2 * views]
    part = pieces[0].shape[1]
    for d in range(views):
        at = pl.ds(pl.multiple_of(lax.rem(id_ref[0] + d, views) * part, part), part)
        out_ref[:, at, 0:BRICK] = pieces[2 * d][...]
        out_ref[:, at, BRICK : 2 * BRICK] = pieces[2 * d + 1][...]


def swap(inner, outer, axes):
    count = lax.axis_size(axes)
    links = [(i, i + 1) for i in range(1, count - 1, 2)]
    outer = lax.ppermute(outer, axes, links + [(j, i) for i, j in links])
    inner = lax.ppermute(inner, axes, [(i, i ^ 1) for i in range(count)])
    return outer, inner


def turn(value, step, count):
    return lax.ppermute(value, "views", [(i, (i + step) % count) for i in range(count)])


def per_device(estimate, views_data, target, psf_taps, shifts):
    x_cells, y_cells, z_cells = estimate.shape
    row_count = lax.axis_size("rows")
    block_count = lax.axis_size("blocks")
    peer_count = block_count * row_count
    view_count = lax.axis_size("views")
    brick_cols = z_cells // BRICK
    brick_count = x_cells * y_cells * brick_cols
    capacity = 2 * brick_count // peer_count
    part = y_cells // view_count
    all_cols = y_cells * block_count
    geo = (peer_count, capacity, x_cells, y_cells, brick_cols, row_count, all_cols, view_count)
    row, place = lax.axis_index("rows"), lax.axis_index("views")
    ids = jnp.stack([place, row % 2]).astype(jnp.int32)
    chain = [(block * view_count - 1, block * view_count) for block in range(1, block_count)]
    edge_at = jnp.where(place == 0, 0, y_cells - TILE)
    edge = lax.ppermute(
        lax.dynamic_slice_in_dim(estimate, edge_at, TILE, 1),
        ("blocks", "views"), chain + [(j, i) for i, j in chain],
    )
    outgoing = pack(shifts, ids, target[0].transpose(0, 2, 1), views_data[0], geo)
    outgoing, edge = lax.optimization_barrier((outgoing, edge))
    arrived = lax.all_to_all(
        outgoing.reshape(peer_count, capacity + 1, 1, BRICK),
        ("blocks", "rows"), split_axis=0, concat_axis=0, tiled=True,
    ).reshape(peer_count * (capacity + 1), 1, BRICK)
    taps = lax.all_gather(psf_taps, "views", axis=0, tiled=True)
    w = (taps / jnp.sum(taps, axis=2, keepdims=True)).reshape(-1)
    halo = f32(2, HALO, part + 2 * TILE, BRICK)
    own, *sent = call(
        part_kernel, "part", [f32(2, x_cells, part + 2 * TILE, BRICK), halo, halo],
        (ids, estimate, edge),
        scratch=[pltpu.VMEM((2, y_cells + 2 * TILE, BRICK), jnp.float32)],
    )
    wide = [f32(2, x_cells + 2 * HALO, part + 2 * TRIM, BRICK)]
    est = call(extend_kernel, "extend", wide, (ids, own, *swap(*sent, "rows")))[0]
    below = forward(w, est, view_count, x_cells)
    arrived, below = lax.optimization_barrier((arrived, below))
    moved = unpack(arrived, peer_count, capacity, brick_count, view_count)
    moved = [m.reshape(brick_cols, x_cells, part, BRICK) for m in moved]
    behind, ahead = turn(moved[1], 1, view_count), turn(moved[3], -1, view_count)
    across = turn(moved[2], 2, view_count)
    total = backward(w, ids, below, (0,), moved[:1], None, 0)[0]
    total = backward(w, ids, below, (3, 1), (behind, ahead), total, 0)[0]
    total, *sent = backward(w, ids, below, (2,), (across,), total, 2 * HALO)
    total, *sent = merge(ids, total, *swap(*sent, "rows"), x_cells + 2 * HALO)
    args = (ids, total, *swap(*sent, ("blocks", "views")), est)
    est = call(functools.partial(update_kernel, view_count), "update", wide, args)[0]
    below = forward(w, est, view_count, x_cells)
    observed = (moved[0], ahead, across, behind)
    total, *sent = backward(w, ids, below, (0, 1, 2, 3), observed, None, HALO)
    total, *sent = merge(ids, total, *swap(*sent, "rows"), x_cells)
    args = (ids, total, *swap(*sent, ("blocks", "views")), est)
    own = call(
        functools.partial(finish_kernel, view_count), "finish",
        [f32(x_cells, part, BRICK)] * 2, args,
        scratch=[pltpu.VMEM((part + 2 * TRIM, BRICK), jnp.float32)],
    )
    prev_a, next_b = turn(own[0], 1, view_count), turn(own[1], -1, view_count)
    prev_b, next_a = turn(own[1], 1, view_count), turn(own[0], -1, view_count)
    far_a, far_b = turn(prev_a, 1, view_count), turn(next_b, -1, view_count)
    pieces = (*own, next_a, next_b, far_a, far_b, prev_a, prev_b)
    return call(
        functools.partial(join_kernel, view_count), "join", [f32(x_cells, y_cells, z_cells)],
        (ids, *pieces),
    )[0]


def solution(mesh):
    placed = (
        P("rows", "blocks", None),
        P("views", "rows", "blocks", None),
        P("views", "rows", "blocks", None),
        P("views", None, None),
        P("views"),
    )
    return jax.shard_map(
        per_device, mesh=mesh, in_specs=placed, out_specs=P("rows", "blocks", None), check_vma=False
    )
```

```python
import functools
import jax
import jax.numpy as jnp
from jax import lax
from jax.experimental import pallas as pl
from jax.experimental.pallas import tpu as pltpu
from jax.sharding import PartitionSpec as P

VMEM = pltpu.VMEM
BRICK = 128
HALO = 3
ITERS = 2
GROUP = 16
SPARE = 8
TAPS = 2 * HALO + 1
TILE = 8
TRIM = 4


def div_mod(x, n):
    if n & (n - 1):
        return x // n, x % n
    return lax.shift_right_logical(x, n.bit_length() - 1), x & (n - 1)


def lane_sum(x):
    return jnp.sum(x, axis=1, keepdims=True)


def pack_kernel(geo, shift_ref, target_ref, views_ref, out_ref, rolled, pos_v, pos_s, sem):
    peers, cap, x_cells, y_cells, brick_cols, row_count, all_cols, view_count = geo
    groups = brick_cols * x_cells
    rows_per = cap + 1
    t = target_ref[...]
    t, bz = div_mod(t, brick_cols)
    line, column = div_mod(t, all_cols)
    block, y = div_mod(column, y_cells)
    row, x = div_mod(line, x_cells)
    dest = block * row_count + row
    quarter, y = div_mod(y, y_cells // view_count)
    quarter = jnp.where(block % 2 == 1, view_count - 1 - quarter, quarter)
    slot = ((quarter * brick_cols + bz) * x_cells + x) * (y_cells // view_count) + y + 1
    high, low = div_mod(slot, 64)
    peer_id = lax.broadcasted_iota(jnp.int32, (peers, y_cells), 0)
    before = (
        lax.broadcasted_iota(jnp.int32, (y_cells, y_cells), 0)
        < lax.broadcasted_iota(jnp.int32, (y_cells, y_cells), 1)
    ).astype(jnp.bfloat16)
    kid = lax.broadcasted_iota(jnp.int32, (BRICK, y_cells), 0)
    carry = jnp.zeros((peers, 1), jnp.float32)
    listed = jnp.zeros((2 * peers, BRICK), jnp.float32)
    for g in range(groups):
        here = (g % x_cells, slice(g // x_cells, g // x_cells + 1))
        d = dest[here]
        hot = d == peer_id
        hot_f = hot.astype(jnp.float32)
        ahead = jnp.dot(hot_f.astype(jnp.bfloat16), before, preferred_element_type=jnp.float32)
        ranks = jnp.sum(hot_f * (ahead + carry), axis=0, keepdims=True)
        carry = carry + lane_sum(hot_f)
        rank_i = ranks.astype(jnp.int32)
        pos_v[g : g + 1, :] = d * rows_per + rank_i
        h = hot_f * high[here].astype(jnp.float32)
        l = hot_f * low[here].astype(jnp.float32)
        both = jnp.concatenate([h, l], axis=0).astype(jnp.bfloat16)
        at = (rank_i == kid).astype(jnp.float32).astype(jnp.bfloat16)
        listed = listed + lax.dot_general(
            both, at, (((1,), (1,)), ((), ())), preferred_element_type=jnp.float32
        )
    copy = pltpu.make_async_copy(pos_v, pos_s, sem)
    copy.start()
    entries = 64.0 * listed[:peers] + listed[peers:]
    for p in range(peers):
        out_ref[p * rows_per + cap] = entries[p : p + 1, :]
    shift = shift_ref[0]
    for bz_i in range(brick_cols):
        for x in range(x_cells):
            rolled[bz_i * x_cells + x] = pltpu.roll(
                views_ref[x, :, bz_i * BRICK : (bz_i + 1) * BRICK], shift, 1
            )
    copy.wait()

    def body(g, c):
        for base in range(0, y_cells, GROUP):
            places = [pos_s[g, base + i] for i in range(GROUP)]
            rows = [rolled[g, base + i : base + i + 1, :] for i in range(GROUP)]
            for place, row in zip(places, rows):
                out_ref[place] = row
        return c

    lax.fori_loop(0, groups, body, 0)


def pack(shift, target, views, geo):
    peers, cap, x_cells, y_cells, brick_cols, row_count, all_cols, view_count = geo
    groups = brick_cols * x_cells
    return pl.pallas_call(
        functools.partial(pack_kernel, geo),
        out_shape=jax.ShapeDtypeStruct((peers * (cap + 1), 1, BRICK), jnp.float32),
        in_specs=[
            pl.BlockSpec(memory_space=pltpu.SMEM),
            pl.BlockSpec(memory_space=pltpu.VMEM),
            pl.BlockSpec(memory_space=pltpu.VMEM),
        ],
        out_specs=pl.BlockSpec(memory_space=pltpu.VMEM),
        scratch_shapes=[
            pltpu.VMEM((groups, y_cells, BRICK), jnp.float32),
            pltpu.VMEM((groups, y_cells), jnp.int32),
            pltpu.SMEM((groups, y_cells), jnp.int32),
            pltpu.SemaphoreType.DMA,
        ],
        name="pack",
    )(shift, target, views)


def unpack_kernel(peers, cap, slots, id_ref, in_ref, *refs):
    outs, (placed, list_v, idx_v, idx_s, sem) = refs[:-5], refs[-5:]
    rows_per = cap + 1
    for p in range(peers):
        list_v[p : p + 1, :] = in_ref[p * rows_per + cap]
    e = list_v[...].astype(jnp.int32)
    views, size = len(outs), slots // len(outs)
    quarter, rest = div_mod(jnp.maximum(e - 1, 0), size)
    turned = quarter - id_ref[0]
    turned = jnp.where(turned < 0, turned + views, turned)
    idx_v[...] = jnp.where(e > 0, turned * size + rest, slots)
    copy = pltpu.make_async_copy(idx_v, idx_s, sem)
    copy.start()
    copy.wait()

    def per_peer(p, c):
        for base in range(0, cap, GROUP):
            places = [idx_s[p, base + i] for i in range(GROUP)]
            rows = [in_ref[p * rows_per + base + i] for i in range(GROUP)]
            for place, row in zip(places, rows):
                placed[pl.ds(place, 1), :] = row
        return c

    lax.fori_loop(0, peers, per_peer, 0)
    for d, out in enumerate(outs):
        out[...] = placed[d * size : (d + 1) * size, :]


def unpack(ids, arrived, peers, cap, slots, views):
    return call(
        functools.partial(unpack_kernel, peers, cap, slots), "unpack",
        [f32(slots // views, BRICK)] * views, (ids, arrived),
        scratch=[
            pltpu.VMEM((slots + SPARE, BRICK), jnp.float32),
            pltpu.VMEM((peers, BRICK), jnp.float32),
            pltpu.VMEM((peers, BRICK), jnp.int32),
            pltpu.SMEM((peers, BRICK), jnp.int32),
            pltpu.SemaphoreType.DMA,
        ],
    )


def vmem():
    return pl.BlockSpec(memory_space=pltpu.VMEM)


def smem():
    return pl.BlockSpec(memory_space=pltpu.SMEM)


def f32(*shape):
    return jax.ShapeDtypeStruct(shape, jnp.float32)


def call(kernel, name, outs, args, scalars=1, scratch=(), work=1000):
    return pl.pallas_call(
        kernel,
        out_shape=outs,
        in_specs=[smem()] * scalars + [vmem()] * (len(args) - scalars),
        out_specs=[vmem()] * len(outs),
        scratch_shapes=list(scratch),
        cost_estimate=pl.CostEstimate(flops=work, bytes_accessed=work, transcendentals=0),
        compiler_params=pltpu.CompilerParams(vmem_limit_bytes=32 * 1024 * 1024),
        name=name,
    )(*args)


def taps_of(w_ref, view, dim, flip):
    base = (view * 3 + dim) * TAPS
    return [w_ref[base + (TAPS - 1 - k if flip else k)] for k in range(TAPS)]


def blur_z(a, b, w):
    lane = lax.broadcasted_iota(jnp.int32, a.shape, 1)
    out_a, out_b = w[HALO] * a, w[HALO] * b
    for s in range(1, HALO + 1):
        keep = lane < BRICK - s
        ra, rb = pltpu.roll(a, BRICK - s, 1), pltpu.roll(b, BRICK - s, 1)
        out_a += w[HALO + s] * jnp.where(keep, ra, rb)
        out_b += w[HALO + s] * jnp.where(keep, rb, 0.0)
        fresh = lane < s
        la, lb = pltpu.roll(a, s, 1), pltpu.roll(b, s, 1)
        out_a += w[HALO - s] * jnp.where(fresh, 0.0, la)
        out_b += w[HALO - s] * jnp.where(fresh, la, lb)
    return out_a, out_b


def y_rows(ref, at, w, n):
    total = w[0] * ref[(*at, pl.ds(TRIM - HALO, n))]
    for k in range(1, TAPS):
        total += w[k] * ref[(*at, pl.ds(TRIM - HALO + k, n))]
    return total


def weigh(layers, w):
    total = w[0] * layers[0]
    for k in range(1, TAPS):
        total += w[k] * layers[k]
    return total


def spread(layers, w, x):
    total = None
    for k in range(TAPS):
        i = x + k - HALO
        if 0 <= i < len(layers):
            term = w[k] * layers[i]
            total = term if total is None else total + term
    return total


def part_kernel(id_ref, est, edge, out_ref, send_in, send_out, wide):
    x_cells, y_cells, _ = est.shape
    part = out_ref.shape[2] - 2 * TILE
    start = pl.multiple_of(id_ref[2] * part, part)
    far = TILE + y_cells

    def body(x, carry):
        for c in range(2):
            lanes = slice(c * BRICK, (c + 1) * BRICK)
            wide[c, TILE:far, :] = est[x, :, lanes]
            wide[c, 0:TILE, :] = edge[x, :, lanes]
            wide[c, far : far + TILE, :] = edge[x, :, lanes]
            out_ref[c, x] = wide[c, pl.ds(start, part + 2 * TILE), :]
        return carry

    lax.fori_loop(0, x_cells, body, 0)
    base = x_cells - HALO
    for c in range(2):
        for i in range(HALO):
            send_in[c, i] = out_ref[c, (1 - id_ref[1]) * base + i]
            send_out[c, i] = out_ref[c, id_ref[1] * base + i]


def extend_kernel(id_ref, own, outer, inner, out_ref):
    x_cells = own.shape[1]
    odd = id_ref[1]
    rows = slice(TRIM, own.shape[2] - TRIM)
    base = x_cells + HALO
    for c in range(2):
        for i in range(x_cells):
            out_ref[c, HALO + i] = own[c, i, rows, :]
        for i in range(HALO):
            out_ref[c, (1 - odd) * base + i] = inner[c, i, rows, :]
            out_ref[c, odd * base + i] = outer[c, i, rows, :]


def forward_kernel(w_ref, est, out_ref, partial):
    views, _, x_cells, part, _ = out_ref.shape

    def per_view(u, carry):
        wx, wy, wz = (taps_of(w_ref, u, dim, False) for dim in range(3))

        def per_tile(t, carry):
            at = pl.ds(pl.multiple_of(t * TILE, TILE), TILE)
            for c in range(2):
                layers = [est[c, i, at, :] for i in range(x_cells + 2 * HALO)]
                for x in range(x_cells):
                    partial[c, x, at, :] = weigh(layers[x : x + TAPS], wx)
            return carry

        lax.fori_loop(0, (part + 2 * TRIM) // TILE, per_tile, 0, unroll=True)

        def per_layer(x, carry):
            rows = [y_rows(partial, (c, x), wy, part) for c in range(2)]
            out_ref[u, 0, x], out_ref[u, 1, x] = blur_z(*rows, wz)
            return carry

        lax.fori_loop(0, x_cells, per_layer, 0, unroll=True)
        return carry

    lax.fori_loop(0, views, per_view, 0)


def forward(w, est, views, x_cells):
    rows = est.shape[2]
    return call(
        forward_kernel, "forward", [f32(views, 2, x_cells, rows - 2 * TRIM, BRICK)], (w, est),
        scratch=[pltpu.VMEM((2, x_cells, rows, BRICK), jnp.float32)],
    )[0]


def backward_kernel(views, rels, add, w_ref, id_ref, below, *refs):
    observed, refs = refs[: len(rels)], refs[len(rels) :]
    before, refs = (refs[0], refs[1:]) if add else (None, refs)
    out_ref, *sends = refs[:-2]
    wide, partial = refs[-2:]
    x_cells, part = below.shape[2:4]
    layers_out = out_ref.shape[1]
    zeros = jnp.zeros((TILE, BRICK), jnp.float32)
    for c in range(2):
        for x in range(x_cells):
            wide[c, x, 0:TILE, :] = zeros
            wide[c, x, TILE + part : 2 * TILE + part, :] = zeros
    for d, obs in zip(rels, observed):
        u = lax.rem(id_ref[0] + d, views)
        wx, wy, wz = (taps_of(w_ref, u, dim, True) for dim in range(3))

        def per_layer(x, carry, u=u, obs=obs, wy=wy, wz=wz):
            rows = blur_z(*(obs[c, x] / below[u, c, x] for c in range(2)), wz)
            for c in range(2):
                wide[c, x, TILE : TILE + part, :] = rows[c]
                partial[c, x] = y_rows(wide, (c, x), wy, part + 2 * TRIM)
            return carry

        lax.fori_loop(0, x_cells, per_layer, 0, unroll=True)

        def per_tile(t, carry, wx=wx, source=before):
            at = pl.ds(pl.multiple_of(t * TILE, TILE), TILE)
            for c in range(2):
                layers = [partial[c, x, at, :] for x in range(x_cells)]
                for i in range(layers_out):
                    value = spread(layers, wx, i - HALO)
                    out_ref[c, i, at, :] = value if source is None else value + source[c, i, at, :]
            return carry

        lax.fori_loop(0, (part + 2 * TRIM) // TILE, per_tile, 0, unroll=True)
        before = out_ref
    odd = id_ref[1]
    for slot, send in enumerate(sends):
        base = layers_out - send.shape[1]
        for c in range(2):
            for i in range(send.shape[1]):
                send[c, i] = out_ref[c, (odd if slot else 1 - odd) * base + i]


def backward(w, ids, below, rels, observed, before, count):
    views, _, x, part, _ = below.shape
    rows = part + 2 * TRIM
    outs = [f32(2, x + 2 * HALO, rows, BRICK)] + [f32(2, count, rows, BRICK)] * (2 if count else 0)
    given = () if before is None else (before,)
    return call(
        functools.partial(backward_kernel, views, rels, before is not None), "backward", outs,
        (w, ids, below, *observed, *given), 2,
        scratch=[
            pltpu.VMEM((2, x, part + 2 * TILE, BRICK), jnp.float32),
            pltpu.VMEM((2, x, rows, BRICK), jnp.float32),
        ],
    )


def merge_kernel(id_ref, total, outer, inner, out_ref, send_in, send_out):
    layers, rows = out_ref.shape[1:3]
    count = inner.shape[1]
    skip = (total.shape[1] - layers) // 2
    odd, odd_part = id_ref[1], lax.rem(id_ref[2], 2)
    base = layers - count
    at_in = pl.ds(pl.multiple_of((1 - odd_part) * (rows - TILE), TILE), TILE)
    at_out = pl.ds(pl.multiple_of(odd_part * (rows - TILE), TILE), TILE)
    for c in range(2):
        for i in range(layers):
            out_ref[c, i] = total[c, skip + i]
        for i in range(count):
            out_ref[c, (1 - odd) * base + i] += inner[c, i]
            out_ref[c, odd * base + i] += outer[c, i]
        for i in range(layers):
            send_in[c, i] = out_ref[c, i, at_in, :]
            send_out[c, i] = out_ref[c, i, at_out, :]


def merge(ids, total, outer, inner, layers):
    rows = total.shape[2]
    outs = [f32(2, layers, rows, BRICK)] + [f32(2, layers, TILE, BRICK)] * 2
    return call(merge_kernel, "merge", outs, (ids, total, outer, inner))


def update_kernel(views, id_ref, total, outer, inner, est, out_ref):
    layers, rows = out_ref.shape[1:3]
    odd = lax.rem(id_ref[2], 2)
    at_in = pl.ds(pl.multiple_of((1 - odd) * (rows - TILE), TILE), TILE)
    at_out = pl.ds(pl.multiple_of(odd * (rows - TILE), TILE), TILE)
    for c in range(2):
        for i in range(layers):
            out_ref[c, i] = est[c, i] * total[c, i] / views
            for at, more in ((at_in, inner), (at_out, outer)):
                out_ref[c, i, at, :] = est[c, i, at, :] * (total[c, i, at, :] + more[c, i]) / views


def finish_kernel(views, id_ref, total, outer, inner, est, out_a, out_b, wide):
    layers, rows = total.shape[1:3]
    odd = lax.rem(id_ref[2], 2)
    at_in = pl.ds(pl.multiple_of((1 - odd) * (rows - TILE), TILE), TILE)
    at_out = pl.ds(pl.multiple_of(odd * (rows - TILE), TILE), TILE)
    own = slice(TRIM, rows - TRIM)
    for c, out in ((0, out_a), (1, out_b)):
        for i in range(layers):
            wide[...] = total[c, i]
            wide[at_in, :] += inner[c, i]
            wide[at_out, :] += outer[c, i]
            out[i] = est[c, HALO + i, own, :] * wide[own, :] / views


def join_kernel(views, id_ref, *refs):
    pieces, out_ref = refs[: 2 * views], refs[2 * views]
    part = pieces[0].shape[1]
    for d in range(views):
        place = lax.rem(id_ref[0] + d, views)
        place = jnp.where(id_ref[3] == 1, views - 1 - place, place)
        at = pl.ds(pl.multiple_of(place * part, part), part)
        out_ref[:, at, 0:BRICK] = pieces[2 * d][...]
        out_ref[:, at, BRICK : 2 * BRICK] = pieces[2 * d + 1][...]


def snake(at, views):
    block, quarter = divmod(at, views)
    return block * views + (views - 1 - quarter if block % 2 else quarter)


def both_ways(links):
    return links + [(j, i) for i, j in links]


def swap_layers(inner, outer):
    count = lax.axis_size("rows")
    outer = lax.ppermute(outer, "rows", both_ways([(i, i + 1) for i in range(1, count - 1, 2)]))
    inner = lax.ppermute(inner, "rows", both_ways([(i, i + 1) for i in range(0, count, 2)]))
    return outer, inner


def swap_rows(inner, outer):
    axes, views = ("blocks", "views"), lax.axis_size("views")
    chain = [snake(i, views) for i in range(lax.axis_size(axes))]
    outer = lax.ppermute(outer, axes, both_ways(list(zip(chain[1:-1:2], chain[2::2]))))
    inner = lax.ppermute(inner, axes, both_ways(list(zip(chain[::2], chain[1::2]))))
    return outer, inner


def turn(value, step, count):
    return lax.ppermute(value, "views", [(i, (i + step) % count) for i in range(count)])


def per_device(estimate, views_data, target, psf_taps, shifts):
    x_cells, y_cells, z_cells = estimate.shape
    row_count = lax.axis_size("rows")
    block_count = lax.axis_size("blocks")
    peer_count = block_count * row_count
    view_count = lax.axis_size("views")
    brick_cols = z_cells // BRICK
    brick_count = x_cells * y_cells * brick_cols
    capacity = 2 * brick_count // peer_count
    part = y_cells // view_count
    all_cols = y_cells * block_count
    geo = (peer_count, capacity, x_cells, y_cells, brick_cols, row_count, all_cols, view_count)
    row, place = lax.axis_index("rows"), lax.axis_index("views")
    turned = lax.axis_index("blocks") % 2
    quarter = jnp.where(turned == 1, view_count - 1 - place, place)
    borders = [
        (snake(b * view_count - 1, view_count), snake(b * view_count, view_count))
        for b in range(1, block_count)
    ]
    edge_at = jnp.where(quarter == 0, 0, y_cells - TILE)
    edge = lax.ppermute(
        lax.dynamic_slice_in_dim(estimate, edge_at, TILE, 1), ("blocks", "views"), both_ways(borders)
    )
    outgoing = pack(shifts, target[0].transpose(0, 2, 1), views_data[0], geo)
    outgoing, edge = lax.optimization_barrier((outgoing, edge))
    arrived = lax.all_to_all(
        outgoing.reshape(peer_count, capacity + 1, 1, BRICK),
        ("blocks", "rows"), split_axis=0, concat_axis=0, tiled=True,
    ).reshape(peer_count * (capacity + 1), 1, BRICK)
    ids = jnp.stack([place, row % 2, quarter, turned]).astype(jnp.int32)
    taps = lax.all_gather(psf_taps, "views", axis=0, tiled=True)
    w = (taps / jnp.sum(taps, axis=2, keepdims=True)).reshape(-1)
    halo = f32(2, HALO, part + 2 * TILE, BRICK)
    own, *sent = call(
        part_kernel, "part", [f32(2, x_cells, part + 2 * TILE, BRICK), halo, halo],
        (ids, estimate, edge),
        scratch=[pltpu.VMEM((2, y_cells + 2 * TILE, BRICK), jnp.float32)],
    )
    wide = [f32(2, x_cells + 2 * HALO, part + 2 * TRIM, BRICK)]
    est = call(extend_kernel, "extend", wide, (ids, own, *swap_layers(*sent)))[0]
    below = forward(w, est, view_count, x_cells)
    arrived, below = lax.optimization_barrier((arrived, below))
    moved = unpack(ids, arrived, peer_count, capacity, brick_count, view_count)
    moved = [m.reshape(brick_cols, x_cells, part, BRICK) for m in moved]
    behind, ahead = turn(moved[1], 1, view_count), turn(moved[3], -1, view_count)
    across = turn(moved[2], 2, view_count)
    total = backward(w, ids, below, (0,), moved[:1], None, 0)[0]
    total = backward(w, ids, below, (3, 1), (behind, ahead), total, 0)[0]
    total, *sent = backward(w, ids, below, (2,), (across,), total, 2 * HALO)
    total, *sent = merge(ids, total, *swap_layers(*sent), x_cells + 2 * HALO)
    args = (ids, total, *swap_rows(*sent), est)
    est = call(functools.partial(update_kernel, view_count), "update", wide, args)[0]
    below = forward(w, est, view_count, x_cells)
    observed = (moved[0], ahead, across, behind)
    total, *sent = backward(w, ids, below, (0, 1, 2, 3), observed, None, HALO)
    total, *sent = merge(ids, total, *swap_layers(*sent), x_cells)
    args = (ids, total, *swap_rows(*sent), est)
    own = call(
        functools.partial(finish_kernel, view_count), "finish",
        [f32(x_cells, part, BRICK)] * 2, args,
        scratch=[pltpu.VMEM((part + 2 * TRIM, BRICK), jnp.float32)],
    )
    prev_a, next_b = turn(own[0], 1, view_count), turn(own[1], -1, view_count)
    prev_b, next_a = turn(own[1], 1, view_count), turn(own[0], -1, view_count)
    far_a, far_b = turn(prev_a, 1, view_count), turn(next_b, -1, view_count)
    pieces = (*own, next_a, next_b, far_a, far_b, prev_a, prev_b)
    return call(
        functools.partial(join_kernel, view_count), "join", [f32(x_cells, y_cells, z_cells)],
        (ids, *pieces),
    )[0]


def solution(mesh):
    placed = (
        P("rows", "blocks", None),
        P("views", "rows", "blocks", None),
        P("views", "rows", "blocks", None),
        P("views", None, None),
        P("views"),
    )
    return jax.shard_map(
        per_device, mesh=mesh, in_specs=placed, out_specs=P("rows", "blocks", None), check_vma=False
    )
```

```python
import functools
import jax
import jax.numpy as jnp
from jax import lax
from jax.experimental import pallas as pl
from jax.experimental.pallas import tpu as pltpu
from jax.sharding import PartitionSpec as P

VMEM = pltpu.VMEM
BRICK = 128
HALO = 3
ITERS = 2
GROUP = 16
SPARE = 8
TAPS = 2 * HALO + 1
TILE = 8
TRIM = 4


def div_mod(x, n):
    if n & (n - 1):
        return x // n, x % n
    return lax.shift_right_logical(x, n.bit_length() - 1), x & (n - 1)


def lane_sum(x):
    return jnp.sum(x, axis=1, keepdims=True)


def pack_kernel(geo, shift_ref, target_ref, views_ref, out_ref, rolled, pos_v, pos_s, sem):
    peers, cap, x_cells, y_cells, brick_cols, row_count, all_cols, view_count = geo
    groups = brick_cols * x_cells
    rows_per = cap + 1
    t = target_ref[...]
    t, bz = div_mod(t, brick_cols)
    line, column = div_mod(t, all_cols)
    block, y = div_mod(column, y_cells)
    row, x = div_mod(line, x_cells)
    dest = block * row_count + row
    quarter, y = div_mod(y, y_cells // view_count)
    quarter = jnp.where(block % 2 == 1, view_count - 1 - quarter, quarter)
    slot = ((quarter * brick_cols + bz) * x_cells + x) * (y_cells // view_count) + y + 1
    high, low = div_mod(slot, 64)
    peer_id = lax.broadcasted_iota(jnp.int32, (peers, y_cells), 0)
    before = (
        lax.broadcasted_iota(jnp.int32, (y_cells, y_cells), 0)
        < lax.broadcasted_iota(jnp.int32, (y_cells, y_cells), 1)
    ).astype(jnp.bfloat16)
    kid = lax.broadcasted_iota(jnp.int32, (BRICK, y_cells), 0)
    carry = jnp.zeros((peers, 1), jnp.float32)
    listed = jnp.zeros((2 * peers, BRICK), jnp.float32)
    for g in range(groups):
        here = (g % x_cells, slice(g // x_cells, g // x_cells + 1))
        d = dest[here]
        hot = d == peer_id
        hot_f = hot.astype(jnp.float32)
        ahead = jnp.dot(hot_f.astype(jnp.bfloat16), before, preferred_element_type=jnp.float32)
        ranks = jnp.sum(hot_f * (ahead + carry), axis=0, keepdims=True)
        carry = carry + lane_sum(hot_f)
        rank_i = ranks.astype(jnp.int32)
        pos_v[g : g + 1, :] = d * rows_per + rank_i
        h = hot_f * high[here].astype(jnp.float32)
        l = hot_f * low[here].astype(jnp.float32)
        both = jnp.concatenate([h, l], axis=0).astype(jnp.bfloat16)
        at = (rank_i == kid).astype(jnp.float32).astype(jnp.bfloat16)
        listed = listed + lax.dot_general(
            both, at, (((1,), (1,)), ((), ())), preferred_element_type=jnp.float32
        )
    copy = pltpu.make_async_copy(pos_v, pos_s, sem)
    copy.start()
    entries = 64.0 * listed[:peers] + listed[peers:]
    for p in range(peers):
        out_ref[p * rows_per + cap] = entries[p : p + 1, :]
    shift = shift_ref[0]
    for bz_i in range(brick_cols):
        for x in range(x_cells):
            rolled[bz_i * x_cells + x] = pltpu.roll(
                views_ref[x, :, bz_i * BRICK : (bz_i + 1) * BRICK], shift, 1
            )
    copy.wait()

    def body(g, c):
        for base in range(0, y_cells, GROUP):
            places = [pos_s[g, base + i] for i in range(GROUP)]
            rows = [rolled[g, base + i : base + i + 1, :] for i in range(GROUP)]
            for place, row in zip(places, rows):
                out_ref[place] = row
        return c

    lax.fori_loop(0, groups, body, 0)


def pack(shift, target, views, geo):
    peers, cap, x_cells, y_cells, brick_cols, row_count, all_cols, view_count = geo
    groups = brick_cols * x_cells
    return pl.pallas_call(
        functools.partial(pack_kernel, geo),
        out_shape=jax.ShapeDtypeStruct((peers * (cap + 1), 1, BRICK), jnp.float32),
        in_specs=[
            pl.BlockSpec(memory_space=pltpu.SMEM),
            pl.BlockSpec(memory_space=pltpu.VMEM),
            pl.BlockSpec(memory_space=pltpu.VMEM),
        ],
        out_specs=pl.BlockSpec(memory_space=pltpu.VMEM),
        scratch_shapes=[
            pltpu.VMEM((groups, y_cells, BRICK), jnp.float32),
            pltpu.VMEM((groups, y_cells), jnp.int32),
            pltpu.SMEM((groups, y_cells), jnp.int32),
            pltpu.SemaphoreType.DMA,
        ],
        name="pack",
    )(shift, target, views)


def unpack_kernel(peers, cap, slots, id_ref, in_ref, *refs):
    outs, (placed, list_v, idx_v, idx_s, sem) = refs[:-5], refs[-5:]
    rows_per = cap + 1
    for p in range(peers):
        list_v[p : p + 1, :] = in_ref[p * rows_per + cap]
    e = list_v[...].astype(jnp.int32)
    views = len(outs) - 1
    size = slots // views
    quarter, rest = div_mod(jnp.maximum(e - 1, 0), size)
    turned = quarter - id_ref[0]
    turned = jnp.where(turned < 0, turned + views, turned)
    idx_v[...] = jnp.where(e > 0, turned * size + rest, slots)
    copy = pltpu.make_async_copy(idx_v, idx_s, sem)
    copy.start()
    copy.wait()

    def per_peer(p, c):
        for base in range(0, cap, GROUP):
            places = [idx_s[p, base + i] for i in range(GROUP)]
            rows = [in_ref[p * rows_per + base + i] for i in range(GROUP)]
            for place, row in zip(places, rows):
                placed[pl.ds(place, 1), :] = row
        return c

    lax.fori_loop(0, peers, per_peer, 0)
    at = 0
    for out in outs:
        out[...] = placed[at : at + out.shape[0], :]
        at += out.shape[0]


def unpack(ids, arrived, peers, cap, slots, views):
    size = slots // views
    return call(
        functools.partial(unpack_kernel, peers, cap, slots), "unpack",
        [f32(n, BRICK) for n in (size, size, size // 2, size // 2, size)], (ids, arrived),
        scratch=[
            pltpu.VMEM((slots + SPARE, BRICK), jnp.float32),
            pltpu.VMEM((peers, BRICK), jnp.float32),
            pltpu.VMEM((peers, BRICK), jnp.int32),
            pltpu.SMEM((peers, BRICK), jnp.int32),
            pltpu.SemaphoreType.DMA,
        ],
    )


def vmem():
    return pl.BlockSpec(memory_space=pltpu.VMEM)


def smem():
    return pl.BlockSpec(memory_space=pltpu.SMEM)


def f32(*shape):
    return jax.ShapeDtypeStruct(shape, jnp.float32)


def call(kernel, name, outs, args, scalars=1, scratch=(), work=1000):
    return pl.pallas_call(
        kernel,
        out_shape=outs,
        in_specs=[smem()] * scalars + [vmem()] * (len(args) - scalars),
        out_specs=[vmem()] * len(outs),
        scratch_shapes=list(scratch),
        cost_estimate=pl.CostEstimate(flops=work, bytes_accessed=work, transcendentals=0),
        compiler_params=pltpu.CompilerParams(vmem_limit_bytes=32 * 1024 * 1024),
        name=name,
    )(*args)


def taps_of(w_ref, view, dim, flip):
    base = (view * 3 + dim) * TAPS
    return [w_ref[base + (TAPS - 1 - k if flip else k)] for k in range(TAPS)]


def blur_z(a, b, w):
    lane = lax.broadcasted_iota(jnp.int32, a.shape, 1)
    out_a, out_b = w[HALO] * a, w[HALO] * b
    for s in range(1, HALO + 1):
        keep = lane < BRICK - s
        ra, rb = pltpu.roll(a, BRICK - s, 1), pltpu.roll(b, BRICK - s, 1)
        out_a += w[HALO + s] * jnp.where(keep, ra, rb)
        out_b += w[HALO + s] * jnp.where(keep, rb, 0.0)
        fresh = lane < s
        la, lb = pltpu.roll(a, s, 1), pltpu.roll(b, s, 1)
        out_a += w[HALO - s] * jnp.where(fresh, 0.0, la)
        out_b += w[HALO - s] * jnp.where(fresh, la, lb)
    return out_a, out_b


def y_rows(ref, at, w, n):
    total = w[0] * ref[(*at, pl.ds(TRIM - HALO, n))]
    for k in range(1, TAPS):
        total += w[k] * ref[(*at, pl.ds(TRIM - HALO + k, n))]
    return total


def weigh(layers, w):
    total = w[0] * layers[0]
    for k in range(1, TAPS):
        total += w[k] * layers[k]
    return total


def spread(layers, w, x):
    total = None
    for k in range(TAPS):
        i = x + k - HALO
        if 0 <= i < len(layers):
            term = w[k] * layers[i]
            total = term if total is None else total + term
    return total


def part_kernel(id_ref, est, edge, out_ref, send_in, send_out, wide):
    x_cells, y_cells, _ = est.shape
    part = out_ref.shape[2] - 2 * TILE
    start = pl.multiple_of(id_ref[2] * part, part)
    far = TILE + y_cells

    def body(x, carry):
        for c in range(2):
            lanes = slice(c * BRICK, (c + 1) * BRICK)
            wide[c, TILE:far, :] = est[x, :, lanes]
            wide[c, 0:TILE, :] = edge[x, :, lanes]
            wide[c, far : far + TILE, :] = edge[x, :, lanes]
            out_ref[c, x] = wide[c, pl.ds(start, part + 2 * TILE), :]
        return carry

    lax.fori_loop(0, x_cells, body, 0)
    base = x_cells - HALO
    for c in range(2):
        for i in range(HALO):
            send_in[c, i] = out_ref[c, (1 - id_ref[1]) * base + i]
            send_out[c, i] = out_ref[c, id_ref[1] * base + i]


def extend_kernel(id_ref, own, outer, inner, out_ref):
    x_cells = own.shape[1]
    odd = id_ref[1]
    rows = slice(TRIM, own.shape[2] - TRIM)
    base = x_cells + HALO
    for c in range(2):
        for i in range(x_cells):
            out_ref[c, HALO + i] = own[c, i, rows, :]
        for i in range(HALO):
            out_ref[c, (1 - odd) * base + i] = inner[c, i, rows, :]
            out_ref[c, odd * base + i] = outer[c, i, rows, :]


def forward_kernel(w_ref, est, out_ref, partial):
    views, _, x_cells, part, _ = out_ref.shape

    def per_view(u, carry):
        wx, wy, wz = (taps_of(w_ref, u, dim, False) for dim in range(3))

        def per_tile(t, carry):
            at = pl.ds(pl.multiple_of(t * TILE, TILE), TILE)
            for c in range(2):
                layers = [est[c, i, at, :] for i in range(x_cells + 2 * HALO)]
                for x in range(x_cells):
                    partial[c, x, at, :] = weigh(layers[x : x + TAPS], wx)
            return carry

        lax.fori_loop(0, (part + 2 * TRIM) // TILE, per_tile, 0, unroll=True)

        def per_layer(x, carry):
            rows = [y_rows(partial, (c, x), wy, part) for c in range(2)]
            out_ref[u, 0, x], out_ref[u, 1, x] = blur_z(*rows, wz)
            return carry

        lax.fori_loop(0, x_cells, per_layer, 0, unroll=True)
        return carry

    lax.fori_loop(0, views, per_view, 0)


def forward(w, est, views, x_cells):
    rows = est.shape[2]
    return call(
        forward_kernel, "forward", [f32(views, 2, x_cells, rows - 2 * TRIM, BRICK)], (w, est),
        scratch=[pltpu.VMEM((2, x_cells, rows, BRICK), jnp.float32)],
    )[0]


def backward_kernel(views, rels, add, w_ref, id_ref, below, *refs):
    observed = []
    for d in rels:
        count = 2 if 2 * d == views else 1
        observed.append(refs[:count])
        refs = refs[count:]
    before, refs = (refs[0], refs[1:]) if add else (None, refs)
    out_ref, *sends = refs[:-2]
    wide, partial = refs[-2:]
    x_cells, part = below.shape[2:4]
    layers_out = out_ref.shape[1]
    zeros = jnp.zeros((TILE, BRICK), jnp.float32)
    for c in range(2):
        for x in range(x_cells):
            wide[c, x, 0:TILE, :] = zeros
            wide[c, x, TILE + part : 2 * TILE + part, :] = zeros
    for d, obs in zip(rels, observed):
        u = lax.rem(id_ref[0] + d, views)
        wx, wy, wz = (taps_of(w_ref, u, dim, True) for dim in range(3))

        def per_layer(x, carry, u=u, obs=obs, wy=wy, wz=wz):
            seen = (obs[0][0, x], obs[-1][obs[-1].shape[0] - 1, x])
            rows = blur_z(*(seen[c] / below[u, c, x] for c in range(2)), wz)
            for c in range(2):
                wide[c, x, TILE : TILE + part, :] = rows[c]
                partial[c, x] = y_rows(wide, (c, x), wy, part + 2 * TRIM)
            return carry

        lax.fori_loop(0, x_cells, per_layer, 0, unroll=True)

        def per_tile(t, carry, wx=wx, source=before):
            at = pl.ds(pl.multiple_of(t * TILE, TILE), TILE)
            for c in range(2):
                layers = [partial[c, x, at, :] for x in range(x_cells)]
                for i in range(layers_out):
                    value = spread(layers, wx, i - HALO)
                    out_ref[c, i, at, :] = value if source is None else value + source[c, i, at, :]
            return carry

        lax.fori_loop(0, (part + 2 * TRIM) // TILE, per_tile, 0, unroll=True)
        before = out_ref
    odd = id_ref[1]
    for slot, send in enumerate(sends):
        base = layers_out - send.shape[1]
        for c in range(2):
            for i in range(send.shape[1]):
                send[c, i] = out_ref[c, (odd if slot else 1 - odd) * base + i]


def backward(w, ids, below, rels, observed, before, count):
    views, _, x, part, _ = below.shape
    rows = part + 2 * TRIM
    outs = [f32(2, x + 2 * HALO, rows, BRICK)] + [f32(2, count, rows, BRICK)] * (2 if count else 0)
    given = () if before is None else (before,)
    return call(
        functools.partial(backward_kernel, views, rels, before is not None), "backward", outs,
        (w, ids, below, *(o for pair in observed for o in pair), *given), 2,
        scratch=[
            pltpu.VMEM((2, x, part + 2 * TILE, BRICK), jnp.float32),
            pltpu.VMEM((2, x, rows, BRICK), jnp.float32),
        ],
    )


def merge_kernel(id_ref, total, outer, inner, out_ref, send_in, send_out):
    layers, rows = out_ref.shape[1:3]
    count = inner.shape[1]
    skip = (total.shape[1] - layers) // 2
    odd, odd_part = id_ref[1], lax.rem(id_ref[2], 2)
    base = layers - count
    at_in = pl.ds(pl.multiple_of((1 - odd_part) * (rows - TILE), TILE), TILE)
    at_out = pl.ds(pl.multiple_of(odd_part * (rows - TILE), TILE), TILE)
    for c in range(2):
        for i in range(layers):
            out_ref[c, i] = total[c, skip + i]
        for i in range(count):
            out_ref[c, (1 - odd) * base + i] += inner[c, i]
            out_ref[c, odd * base + i] += outer[c, i]
        for i in range(layers):
            send_in[c, i] = out_ref[c, i, at_in, :]
            send_out[c, i] = out_ref[c, i, at_out, :]


def merge(ids, total, outer, inner, layers):
    rows = total.shape[2]
    outs = [f32(2, layers, rows, BRICK)] + [f32(2, layers, TILE, BRICK)] * 2
    return call(merge_kernel, "merge", outs, (ids, total, outer, inner))


def update_kernel(views, id_ref, total, outer, inner, est, out_ref):
    layers, rows = out_ref.shape[1:3]
    odd = lax.rem(id_ref[2], 2)
    at_in = pl.ds(pl.multiple_of((1 - odd) * (rows - TILE), TILE), TILE)
    at_out = pl.ds(pl.multiple_of(odd * (rows - TILE), TILE), TILE)
    for c in range(2):
        for i in range(layers):
            out_ref[c, i] = est[c, i] * total[c, i] / views
            for at, more in ((at_in, inner), (at_out, outer)):
                out_ref[c, i, at, :] = est[c, i, at, :] * (total[c, i, at, :] + more[c, i]) / views


def finish_kernel(views, id_ref, total, outer, inner, est, out_a, out_b, wide):
    layers, rows = total.shape[1:3]
    odd = lax.rem(id_ref[2], 2)
    at_in = pl.ds(pl.multiple_of((1 - odd) * (rows - TILE), TILE), TILE)
    at_out = pl.ds(pl.multiple_of(odd * (rows - TILE), TILE), TILE)
    own = slice(TRIM, rows - TRIM)
    for c, out in ((0, out_a), (1, out_b)):
        for i in range(layers):
            wide[...] = total[c, i]
            wide[at_in, :] += inner[c, i]
            wide[at_out, :] += outer[c, i]
            out[i] = est[c, HALO + i, own, :] * wide[own, :] / views


def join_kernel(views, id_ref, *refs):
    pieces, (out_ref, wide, sems) = refs[: 2 * views], refs[2 * views :]
    layers, part, _ = pieces[0].shape
    places = []
    for d in range(views):
        place = lax.rem(id_ref[0] + d, views)
        place = jnp.where(id_ref[3] == 1, views - 1 - place, place)
        places.append(pl.ds(pl.multiple_of(place * part, part), part))
    copies = []
    for i in range(layers):
        for d, at in enumerate(places):
            wide[i, at, 0:BRICK] = pieces[2 * d][i]
            wide[i, at, BRICK : 2 * BRICK] = pieces[2 * d + 1][i]
        copies.append(pltpu.make_async_copy(wide.at[i], out_ref.at[i], sems.at[i]))
        copies[-1].start()
    for copy in copies:
        copy.wait()


def join(ids, pieces, shape):
    return pl.pallas_call(
        functools.partial(join_kernel, len(pieces) // 2),
        out_shape=f32(*shape),
        in_specs=[smem()] + [vmem()] * len(pieces),
        out_specs=pl.BlockSpec(memory_space=pl.ANY),
        scratch_shapes=[pltpu.VMEM(shape, jnp.float32), pltpu.SemaphoreType.DMA((shape[0],))],
        cost_estimate=pl.CostEstimate(flops=1000, bytes_accessed=1000, transcendentals=0),
        name="join",
    )(ids, *pieces)


def snake(at, views):
    block, quarter = divmod(at, views)
    return block * views + (views - 1 - quarter if block % 2 else quarter)


def both_ways(links):
    return links + [(j, i) for i, j in links]


def swap_layers(inner, outer):
    count = lax.axis_size("rows")
    outer = lax.ppermute(outer, "rows", both_ways([(i, i + 1) for i in range(1, count - 1, 2)]))
    inner = lax.ppermute(inner, "rows", both_ways([(i, i + 1) for i in range(0, count, 2)]))
    return outer, inner


def swap_rows(inner, outer):
    axes, views = ("blocks", "views"), lax.axis_size("views")
    chain = [snake(i, views) for i in range(lax.axis_size(axes))]
    outer = lax.ppermute(outer, axes, both_ways(list(zip(chain[1:-1:2], chain[2::2]))))
    inner = lax.ppermute(inner, axes, both_ways(list(zip(chain[::2], chain[1::2]))))
    return outer, inner


def turn(value, step, count):
    return lax.ppermute(value, "views", [(i, (i + step) % count) for i in range(count)])


def per_device(estimate, views_data, target, psf_taps, shifts):
    x_cells, y_cells, z_cells = estimate.shape
    row_count = lax.axis_size("rows")
    block_count = lax.axis_size("blocks")
    peer_count = block_count * row_count
    view_count = lax.axis_size("views")
    brick_cols = z_cells // BRICK
    brick_count = x_cells * y_cells * brick_cols
    capacity = 2 * brick_count // peer_count
    part = y_cells // view_count
    all_cols = y_cells * block_count
    geo = (peer_count, capacity, x_cells, y_cells, brick_cols, row_count, all_cols, view_count)
    row, place = lax.axis_index("rows"), lax.axis_index("views")
    turned = lax.axis_index("blocks") % 2
    quarter = jnp.where(turned == 1, view_count - 1 - place, place)
    borders = [
        (snake(b * view_count - 1, view_count), snake(b * view_count, view_count))
        for b in range(1, block_count)
    ]
    edge_at = jnp.where(quarter == 0, 0, y_cells - TILE)
    edge = lax.ppermute(
        lax.dynamic_slice_in_dim(estimate, edge_at, TILE, 1), ("blocks", "views"), both_ways(borders)
    )
    outgoing = pack(shifts, target[0].transpose(0, 2, 1), views_data[0], geo)
    outgoing, edge = lax.optimization_barrier((outgoing, edge))
    arrived = lax.all_to_all(
        outgoing.reshape(peer_count, capacity + 1, 1, BRICK),
        ("blocks", "rows"), split_axis=0, concat_axis=0, tiled=True,
    ).reshape(peer_count * (capacity + 1), 1, BRICK)
    ids = jnp.stack([place, row % 2, quarter, turned]).astype(jnp.int32)
    taps = lax.all_gather(psf_taps, "views", axis=0, tiled=True)
    w = (taps / jnp.sum(taps, axis=2, keepdims=True)).reshape(-1)
    halo = f32(2, HALO, part + 2 * TILE, BRICK)
    own, *sent = call(
        part_kernel, "part", [f32(2, x_cells, part + 2 * TILE, BRICK), halo, halo],
        (ids, estimate, edge),
        scratch=[pltpu.VMEM((2, y_cells + 2 * TILE, BRICK), jnp.float32)],
    )
    wide = [f32(2, x_cells + 2 * HALO, part + 2 * TRIM, BRICK)]
    est = call(extend_kernel, "extend", wide, (ids, own, *swap_layers(*sent)))[0]
    below = forward(w, est, view_count, x_cells)
    arrived, below = lax.optimization_barrier((arrived, below))
    moved = unpack(ids, arrived, peer_count, capacity, brick_count, view_count)
    moved = [m.reshape(-1, x_cells, part, BRICK) for m in moved]
    hop_a, hop_b = turn(moved[2], 1, view_count), turn(moved[3], -1, view_count)
    behind, ahead = turn(moved[1], 1, view_count), turn(moved[4], -1, view_count)
    across = (turn(hop_a, 1, view_count), turn(hop_b, -1, view_count))
    total = backward(w, ids, below, (0,), [(moved[0],)], None, 0)[0]
    total = backward(w, ids, below, (3, 1), [(behind,), (ahead,)], total, 0)[0]
    total, *sent = backward(w, ids, below, (2,), [across], total, 2 * HALO)
    total, *sent = merge(ids, total, *swap_layers(*sent), x_cells + 2 * HALO)
    args = (ids, total, *swap_rows(*sent), est)
    est = call(functools.partial(update_kernel, view_count), "update", wide, args)[0]
    below = forward(w, est, view_count, x_cells)
    observed = [(moved[0],), (ahead,), across, (behind,)]
    total, *sent = backward(w, ids, below, (0, 1, 2, 3), observed, None, HALO)
    total, *sent = merge(ids, total, *swap_layers(*sent), x_cells)
    args = (ids, total, *swap_rows(*sent), est)
    own = call(
        functools.partial(finish_kernel, view_count), "finish",
        [f32(x_cells, part, BRICK)] * 2, args,
        scratch=[pltpu.VMEM((part + 2 * TRIM, BRICK), jnp.float32)],
    )
    prev_a, next_b = turn(own[0], 1, view_count), turn(own[1], -1, view_count)
    prev_b, next_a = turn(own[1], 1, view_count), turn(own[0], -1, view_count)
    far_a, far_b = turn(prev_a, 1, view_count), turn(next_b, -1, view_count)
    pieces = (*own, next_a, next_b, far_a, far_b, prev_a, prev_b)
    return join(ids, pieces, (x_cells, y_cells, z_cells))


def solution(mesh):
    placed = (
        P("rows", "blocks", None),
        P("views", "rows", "blocks", None),
        P("views", "rows", "blocks", None),
        P("views", None, None),
        P("views"),
    )
    return jax.shard_map(
        per_device, mesh=mesh, in_specs=placed, out_specs=P("rows", "blocks", None), check_vma=False
    )
```

```python
import functools
import jax
import jax.numpy as jnp
from jax import lax
from jax.experimental import pallas as pl
from jax.experimental.pallas import tpu as pltpu
from jax.sharding import PartitionSpec as P

VMEM = pltpu.VMEM
BRICK = 128
HALO = 3
ITERS = 2
GROUP = 16
SPARE = 8
TAPS = 2 * HALO + 1
TILE = 8
TRIM = 4


def div_mod(x, n):
    if n & (n - 1):
        return x // n, x % n
    return lax.shift_right_logical(x, n.bit_length() - 1), x & (n - 1)


def lane_sum(x):
    return jnp.sum(x, axis=1, keepdims=True)


def pack_kernel(geo, shift_ref, target_ref, views_ref, out_ref, rolled, pos_v, pos_s, sem):
    peers, cap, x_cells, y_cells, brick_cols, row_count, all_cols, view_count = geo
    groups = brick_cols * x_cells
    rows_per = cap + 1
    t = target_ref[...]
    t, bz = div_mod(t, brick_cols)
    line, column = div_mod(t, all_cols)
    block, y = div_mod(column, y_cells)
    row, x = div_mod(line, x_cells)
    dest = block * row_count + row
    quarter, y = div_mod(y, y_cells // view_count)
    quarter = jnp.where(block % 2 == 1, view_count - 1 - quarter, quarter)
    slot = ((quarter * brick_cols + bz) * x_cells + x) * (y_cells // view_count) + y + 1
    high, low = div_mod(slot, 64)
    peer_id = lax.broadcasted_iota(jnp.int32, (peers, y_cells), 0)
    before = (
        lax.broadcasted_iota(jnp.int32, (y_cells, y_cells), 0)
        < lax.broadcasted_iota(jnp.int32, (y_cells, y_cells), 1)
    ).astype(jnp.bfloat16)
    kid = lax.broadcasted_iota(jnp.int32, (BRICK, y_cells), 0)
    carry = jnp.zeros((peers, 1), jnp.float32)
    listed = jnp.zeros((2 * peers, BRICK), jnp.float32)
    for g in range(groups):
        here = (g % x_cells, slice(g // x_cells, g // x_cells + 1))
        d = dest[here]
        hot = d == peer_id
        hot_f = hot.astype(jnp.float32)
        ahead = jnp.dot(hot_f.astype(jnp.bfloat16), before, preferred_element_type=jnp.float32)
        ranks = jnp.sum(hot_f * (ahead + carry), axis=0, keepdims=True)
        carry = carry + lane_sum(hot_f)
        rank_i = ranks.astype(jnp.int32)
        pos_v[g : g + 1, :] = d * rows_per + rank_i
        h = hot_f * high[here].astype(jnp.float32)
        l = hot_f * low[here].astype(jnp.float32)
        both = jnp.concatenate([h, l], axis=0).astype(jnp.bfloat16)
        at = (rank_i == kid).astype(jnp.float32).astype(jnp.bfloat16)
        listed = listed + lax.dot_general(
            both, at, (((1,), (1,)), ((), ())), preferred_element_type=jnp.float32
        )
    copy = pltpu.make_async_copy(pos_v, pos_s, sem)
    copy.start()
    entries = 64.0 * listed[:peers] + listed[peers:]
    for p in range(peers):
        out_ref[p * rows_per + cap] = entries[p : p + 1, :]
    shift = shift_ref[0]
    for bz_i in range(brick_cols):
        for x in range(x_cells):
            rolled[bz_i * x_cells + x] = pltpu.roll(
                views_ref[x, :, bz_i * BRICK : (bz_i + 1) * BRICK], shift, 1
            )
    copy.wait()

    def body(g, c):
        for base in range(0, y_cells, GROUP):
            places = [pos_s[g, base + i] for i in range(GROUP)]
            rows = [rolled[g, base + i : base + i + 1, :] for i in range(GROUP)]
            for place, row in zip(places, rows):
                out_ref[place] = row
        return c

    lax.fori_loop(0, groups, body, 0)


def pack(shift, target, views, geo):
    peers, cap, x_cells, y_cells, brick_cols, row_count, all_cols, view_count = geo
    groups = brick_cols * x_cells
    return pl.pallas_call(
        functools.partial(pack_kernel, geo),
        out_shape=jax.ShapeDtypeStruct((peers * (cap + 1), 1, BRICK), jnp.float32),
        in_specs=[
            pl.BlockSpec(memory_space=pltpu.SMEM),
            pl.BlockSpec(memory_space=pltpu.VMEM),
            pl.BlockSpec(memory_space=pltpu.VMEM),
        ],
        out_specs=pl.BlockSpec(memory_space=pltpu.VMEM),
        scratch_shapes=[
            pltpu.VMEM((groups, y_cells, BRICK), jnp.float32),
            pltpu.VMEM((groups, y_cells), jnp.int32),
            pltpu.SMEM((groups, y_cells), jnp.int32),
            pltpu.SemaphoreType.DMA,
        ],
        name="pack",
    )(shift, target, views)


def unpack_kernel(peers, cap, slots, id_ref, in_ref, *refs):
    outs, (placed, list_v, idx_v, idx_s, sem) = refs[:-5], refs[-5:]
    rows_per = cap + 1
    for p in range(peers):
        list_v[p : p + 1, :] = in_ref[p * rows_per + cap]
    e = list_v[...].astype(jnp.int32)
    views, size = len(outs), slots // len(outs)
    quarter, rest = div_mod(jnp.maximum(e - 1, 0), size)
    turned = quarter - id_ref[0]
    turned = jnp.where(turned < 0, turned + views, turned)
    idx_v[...] = jnp.where(e > 0, turned * size + rest, slots)
    copy = pltpu.make_async_copy(idx_v, idx_s, sem)
    copy.start()
    copy.wait()

    def per_peer(p, c):
        for base in range(0, cap, GROUP):
            places = [idx_s[p, base + i] for i in range(GROUP)]
            rows = [in_ref[p * rows_per + base + i] for i in range(GROUP)]
            for place, row in zip(places, rows):
                placed[pl.ds(place, 1), :] = row
        return c

    lax.fori_loop(0, peers, per_peer, 0)
    for d, out in enumerate(outs):
        out[...] = placed[d * size : (d + 1) * size, :]


def unpack(ids, arrived, peers, cap, slots, views):
    return call(
        functools.partial(unpack_kernel, peers, cap, slots), "unpack",
        [f32(slots // views, BRICK)] * views, (ids, arrived),
        scratch=[
            pltpu.VMEM((slots + SPARE, BRICK), jnp.float32),
            pltpu.VMEM((peers, BRICK), jnp.float32),
            pltpu.VMEM((peers, BRICK), jnp.int32),
            pltpu.SMEM((peers, BRICK), jnp.int32),
            pltpu.SemaphoreType.DMA,
        ],
    )


def vmem():
    return pl.BlockSpec(memory_space=pltpu.VMEM)


def smem():
    return pl.BlockSpec(memory_space=pltpu.SMEM)


def f32(*shape):
    return jax.ShapeDtypeStruct(shape, jnp.float32)


def call(kernel, name, outs, args, scalars=1, scratch=(), work=1000):
    return pl.pallas_call(
        kernel,
        out_shape=outs,
        in_specs=[smem()] * scalars + [vmem()] * (len(args) - scalars),
        out_specs=[vmem()] * len(outs),
        scratch_shapes=list(scratch),
        cost_estimate=pl.CostEstimate(flops=work, bytes_accessed=work, transcendentals=0),
        compiler_params=pltpu.CompilerParams(vmem_limit_bytes=32 * 1024 * 1024),
        name=name,
    )(*args)


def taps_of(w_ref, view, dim, flip):
    base = (view * 3 + dim) * TAPS
    return [w_ref[base + (TAPS - 1 - k if flip else k)] for k in range(TAPS)]


def blur_z(a, b, w):
    lane = lax.broadcasted_iota(jnp.int32, a.shape, 1)
    out_a, out_b = w[HALO] * a, w[HALO] * b
    for s in range(1, HALO + 1):
        keep = lane < BRICK - s
        ra, rb = pltpu.roll(a, BRICK - s, 1), pltpu.roll(b, BRICK - s, 1)
        out_a += w[HALO + s] * jnp.where(keep, ra, rb)
        out_b += w[HALO + s] * jnp.where(keep, rb, 0.0)
        fresh = lane < s
        la, lb = pltpu.roll(a, s, 1), pltpu.roll(b, s, 1)
        out_a += w[HALO - s] * jnp.where(fresh, 0.0, la)
        out_b += w[HALO - s] * jnp.where(fresh, la, lb)
    return out_a, out_b


def y_rows(ref, at, w, n):
    total = w[0] * ref[(*at, pl.ds(TRIM - HALO, n))]
    for k in range(1, TAPS):
        total += w[k] * ref[(*at, pl.ds(TRIM - HALO + k, n))]
    return total


def weigh(layers, w):
    total = w[0] * layers[0]
    for k in range(1, TAPS):
        total += w[k] * layers[k]
    return total


def spread(layers, w, x):
    total = None
    for k in range(TAPS):
        i = x + k - HALO
        if 0 <= i < len(layers):
            term = w[k] * layers[i]
            total = term if total is None else total + term
    return total


def part_kernel(id_ref, est, edge, out_ref, send_in, send_out, wide):
    x_cells, y_cells, _ = est.shape
    part = out_ref.shape[2] - 2 * TILE
    start = pl.multiple_of(id_ref[2] * part, part)
    far = TILE + y_cells

    def body(x, carry):
        for c in range(2):
            lanes = slice(c * BRICK, (c + 1) * BRICK)
            wide[c, TILE:far, :] = est[x, :, lanes]
            wide[c, 0:TILE, :] = edge[x, :, lanes]
            wide[c, far : far + TILE, :] = edge[x, :, lanes]
            out_ref[c, x] = wide[c, pl.ds(start, part + 2 * TILE), :]
        return carry

    lax.fori_loop(0, x_cells, body, 0)
    base = x_cells - HALO
    for c in range(2):
        for i in range(HALO):
            send_in[c, i] = out_ref[c, (1 - id_ref[1]) * base + i]
            send_out[c, i] = out_ref[c, id_ref[1] * base + i]


def extend_kernel(id_ref, own, outer, inner, out_ref):
    x_cells = own.shape[1]
    odd = id_ref[1]
    rows = slice(TRIM, own.shape[2] - TRIM)
    base = x_cells + HALO
    for c in range(2):
        for i in range(x_cells):
            out_ref[c, HALO + i] = own[c, i, rows, :]
        for i in range(HALO):
            out_ref[c, (1 - odd) * base + i] = inner[c, i, rows, :]
            out_ref[c, odd * base + i] = outer[c, i, rows, :]


def forward_kernel(w_ref, est, out_ref, partial):
    views, _, x_cells, part, _ = out_ref.shape

    def per_view(u, carry):
        wx, wy, wz = (taps_of(w_ref, u, dim, False) for dim in range(3))

        def per_tile(t, carry):
            at = pl.ds(pl.multiple_of(t * TILE, TILE), TILE)
            for c in range(2):
                layers = [est[c, i, at, :] for i in range(x_cells + 2 * HALO)]
                for x in range(x_cells):
                    partial[c, x, at, :] = weigh(layers[x : x + TAPS], wx)
            return carry

        lax.fori_loop(0, (part + 2 * TRIM) // TILE, per_tile, 0, unroll=True)

        def per_layer(x, carry):
            rows = [y_rows(partial, (c, x), wy, part) for c in range(2)]
            out_ref[u, 0, x], out_ref[u, 1, x] = blur_z(*rows, wz)
            return carry

        lax.fori_loop(0, x_cells, per_layer, 0, unroll=True)
        return carry

    lax.fori_loop(0, views, per_view, 0)


def forward(w, est, views, x_cells):
    rows = est.shape[2]
    return call(
        forward_kernel, "forward", [f32(views, 2, x_cells, rows - 2 * TRIM, BRICK)], (w, est),
        scratch=[pltpu.VMEM((2, x_cells, rows, BRICK), jnp.float32)],
    )[0]


def blur_x_tile(est, at, wx, out, c, x_cells, rows):
    layers = [est[c, i, at, :] for i in range(x_cells + 2 * HALO)]
    for x in range(x_cells):
        out[c, x, rows, :] = weigh(layers[x : x + TAPS], wx)


def middle_kernel(w_ref, est, total, out_ref, part_ref, fresh):
    views, _, x_cells, part, _ = out_ref.shape
    tall = part_ref.shape[3]
    rows = slice(TILE, TILE + tall)
    for c in range(2):
        for i in range(x_cells + 2 * HALO):
            fresh[c, i] = est[c, i, rows, :] * total[c, i, rows, :] / views

    def per_view(u, carry):
        wx, wy, wz = (taps_of(w_ref, u, dim, False) for dim in range(3))

        def per_tile(t, carry):
            at = pl.ds(pl.multiple_of(t * TILE, TILE), TILE)
            for c in range(2):
                blur_x_tile(fresh, at, wx, part_ref.at[u], c, x_cells, at)
            return carry

        lax.fori_loop(0, tall // TILE, per_tile, 0, unroll=True)

        def per_layer(x, carry):
            rows = [y_rows(part_ref, (u, c, x), wy, part) for c in range(2)]
            out_ref[u, 0, x], out_ref[u, 1, x] = blur_z(*rows, wz)
            return carry

        lax.fori_loop(0, x_cells, per_layer, 0, unroll=True)
        return carry

    lax.fori_loop(0, views, per_view, 0)


def middle(w, est, total, views, x_cells):
    tall = est.shape[2] - 2 * TILE
    return call(
        middle_kernel, "middle",
        [f32(views, 2, x_cells, tall - TILE, BRICK), f32(views, 2, x_cells, tall, BRICK)],
        (w, est, total), scratch=[pltpu.VMEM((2, x_cells + 2 * HALO, tall, BRICK), jnp.float32)],
    )


def renew(views, id_ref, total, outer, inner, est, out_ref):
    layers, rows = out_ref.shape[1:3]
    odd = lax.rem(id_ref[2], 2)
    at_in = pl.ds(pl.multiple_of((1 - odd) * (rows - TILE), TILE), TILE)
    at_out = pl.ds(pl.multiple_of(odd * (rows - TILE), TILE), TILE)
    for c in range(2):
        for i in range(layers):
            out_ref[c, i] = est[c, i] * total[c, i] / views
            for at, more in ((at_in, inner), (at_out, outer)):
                out_ref[c, i, at, :] = est[c, i, at, :] * (total[c, i, at, :] + more[c, i]) / views


def ends_kernel(w_ref, id_ref, total, outer, inner, est, mid, part_ref, new, out_ref, strip):
    views, _, x_cells, part, _ = out_ref.shape
    tall = part_ref.shape[3]
    renew(views, id_ref, total, outer, inner, est, new)
    sides = ((0, 0, 0, TILE, 0), (tall + TILE, TILE, tall - TILE, 0, part - TILE))

    def per_view(u, carry):
        wx, wy, wz = (taps_of(w_ref, u, dim, False) for dim in range(3))
        for s, (at, here, kept, there, to) in enumerate(sides):
            for c in range(2):
                blur_x_tile(new, slice(at, at + TILE), wx, strip.at[s], c, x_cells, slice(here, here + TILE))
        for x in range(x_cells):
            for s, (at, here, kept, there, to) in enumerate(sides):
                for c in range(2):
                    strip[s, c, x, there : there + TILE, :] = part_ref[u, c, x, kept : kept + TILE, :]
                rows = blur_z(*(y_rows(strip, (s, c, x), wy, TILE) for c in range(2)), wz)
                for c in range(2):
                    out_ref[u, c, x, to : to + TILE, :] = rows[c]
            for c in range(2):
                out_ref[u, c, x, TILE : part - TILE, :] = mid[u, c, x]
        return carry

    lax.fori_loop(0, views, per_view, 0)


def ends(w, args, mid, partial):
    views, _, x, tall, _ = partial.shape
    rows = tall + 2 * TILE
    return call(
        ends_kernel, "ends", [f32(2, x + 2 * HALO, rows, BRICK), f32(views, 2, x, tall + TILE, BRICK)],
        (w, *args, mid, partial), 2, scratch=[pltpu.VMEM((2, 2, x, 2 * TILE, BRICK), jnp.float32)],
    )


def backward_kernel(views, rels, add, w_ref, id_ref, below, *refs):
    observed, refs = refs[: len(rels)], refs[len(rels) :]
    before, refs = (refs[0], refs[1:]) if add else (None, refs)
    out_ref, *sends = refs[:-2]
    wide, partial = refs[-2:]
    x_cells, part = below.shape[2:4]
    layers_out = out_ref.shape[1]
    zeros = jnp.zeros((TILE, BRICK), jnp.float32)
    for c in range(2):
        for x in range(x_cells):
            wide[c, x, 0:TILE, :] = zeros
            wide[c, x, TILE + part : 2 * TILE + part, :] = zeros
    for d, obs in zip(rels, observed):
        u = lax.rem(id_ref[0] + d, views)
        wx, wy, wz = (taps_of(w_ref, u, dim, True) for dim in range(3))

        def per_layer(x, carry, u=u, obs=obs, wy=wy, wz=wz):
            rows = blur_z(*(obs[c, x] / below[u, c, x] for c in range(2)), wz)
            for c in range(2):
                wide[c, x, TILE : TILE + part, :] = rows[c]
                partial[c, x] = y_rows(wide, (c, x), wy, part + 2 * TRIM)
            return carry

        lax.fori_loop(0, x_cells, per_layer, 0, unroll=True)

        def per_tile(t, carry, wx=wx, source=before):
            at = pl.ds(pl.multiple_of(t * TILE, TILE), TILE)
            for c in range(2):
                layers = [partial[c, x, at, :] for x in range(x_cells)]
                for i in range(layers_out):
                    value = spread(layers, wx, i - HALO)
                    out_ref[c, i, at, :] = value if source is None else value + source[c, i, at, :]
            return carry

        lax.fori_loop(0, (part + 2 * TRIM) // TILE, per_tile, 0, unroll=True)
        before = out_ref
    odd = id_ref[1]
    for slot, send in enumerate(sends):
        base = layers_out - send.shape[1]
        for c in range(2):
            for i in range(send.shape[1]):
                send[c, i] = out_ref[c, (odd if slot else 1 - odd) * base + i]


def backward(w, ids, below, rels, observed, before, count):
    views, _, x, part, _ = below.shape
    rows = part + 2 * TRIM
    outs = [f32(2, x + 2 * HALO, rows, BRICK)] + [f32(2, count, rows, BRICK)] * (2 if count else 0)
    given = () if before is None else (before,)
    return call(
        functools.partial(backward_kernel, views, rels, before is not None), "backward", outs,
        (w, ids, below, *observed, *given), 2,
        scratch=[
            pltpu.VMEM((2, x, part + 2 * TILE, BRICK), jnp.float32),
            pltpu.VMEM((2, x, rows, BRICK), jnp.float32),
        ],
    )


def merge_kernel(id_ref, total, outer, inner, out_ref, send_in, send_out):
    layers, rows = out_ref.shape[1:3]
    count = inner.shape[1]
    skip = (total.shape[1] - layers) // 2
    odd, odd_part = id_ref[1], lax.rem(id_ref[2], 2)
    base = layers - count
    at_in = pl.ds(pl.multiple_of((1 - odd_part) * (rows - TILE), TILE), TILE)
    at_out = pl.ds(pl.multiple_of(odd_part * (rows - TILE), TILE), TILE)
    for c in range(2):
        for i in range(layers):
            out_ref[c, i] = total[c, skip + i]
        for i in range(count):
            out_ref[c, (1 - odd) * base + i] += inner[c, i]
            out_ref[c, odd * base + i] += outer[c, i]
        for i in range(layers):
            send_in[c, i] = out_ref[c, i, at_in, :]
            send_out[c, i] = out_ref[c, i, at_out, :]


def merge(ids, total, outer, inner, layers):
    rows = total.shape[2]
    outs = [f32(2, layers, rows, BRICK)] + [f32(2, layers, TILE, BRICK)] * 2
    return call(merge_kernel, "merge", outs, (ids, total, outer, inner))


def finish_kernel(views, id_ref, total, outer, inner, est, out_a, out_b, wide):
    layers, rows = total.shape[1:3]
    odd = lax.rem(id_ref[2], 2)
    at_in = pl.ds(pl.multiple_of((1 - odd) * (rows - TILE), TILE), TILE)
    at_out = pl.ds(pl.multiple_of(odd * (rows - TILE), TILE), TILE)
    own = slice(TRIM, rows - TRIM)
    for c, out in ((0, out_a), (1, out_b)):
        for i in range(layers):
            wide[...] = total[c, i]
            wide[at_in, :] += inner[c, i]
            wide[at_out, :] += outer[c, i]
            out[i] = est[c, HALO + i, own, :] * wide[own, :] / views


def join_kernel(views, id_ref, *refs):
    pieces, out_ref = refs[: 2 * views], refs[2 * views]
    part = pieces[0].shape[1]
    for d in range(views):
        place = lax.rem(id_ref[0] + d, views)
        place = jnp.where(id_ref[3] == 1, views - 1 - place, place)
        at = pl.ds(pl.multiple_of(place * part, part), part)
        out_ref[:, at, 0:BRICK] = pieces[2 * d][...]
        out_ref[:, at, BRICK : 2 * BRICK] = pieces[2 * d + 1][...]


def snake(at, views):
    block, quarter = divmod(at, views)
    return block * views + (views - 1 - quarter if block % 2 else quarter)


def both_ways(links):
    return links + [(j, i) for i, j in links]


def swap_layers(inner, outer):
    count = lax.axis_size("rows")
    outer = lax.ppermute(outer, "rows", both_ways([(i, i + 1) for i in range(1, count - 1, 2)]))
    inner = lax.ppermute(inner, "rows", both_ways([(i, i + 1) for i in range(0, count, 2)]))
    return outer, inner


def swap_rows(inner, outer):
    axes, views = ("blocks", "views"), lax.axis_size("views")
    chain = [snake(i, views) for i in range(lax.axis_size(axes))]
    outer = lax.ppermute(outer, axes, both_ways(list(zip(chain[1:-1:2], chain[2::2]))))
    inner = lax.ppermute(inner, axes, both_ways(list(zip(chain[::2], chain[1::2]))))
    return outer, inner


def turn(value, step, count):
    return lax.ppermute(value, "views", [(i, (i + step) % count) for i in range(count)])


def per_device(estimate, views_data, target, psf_taps, shifts):
    x_cells, y_cells, z_cells = estimate.shape
    row_count = lax.axis_size("rows")
    block_count = lax.axis_size("blocks")
    peer_count = block_count * row_count
    view_count = lax.axis_size("views")
    brick_cols = z_cells // BRICK
    brick_count = x_cells * y_cells * brick_cols
    capacity = 2 * brick_count // peer_count
    part = y_cells // view_count
    all_cols = y_cells * block_count
    geo = (peer_count, capacity, x_cells, y_cells, brick_cols, row_count, all_cols, view_count)
    row, place = lax.axis_index("rows"), lax.axis_index("views")
    turned = lax.axis_index("blocks") % 2
    quarter = jnp.where(turned == 1, view_count - 1 - place, place)
    borders = [
        (snake(b * view_count - 1, view_count), snake(b * view_count, view_count))
        for b in range(1, block_count)
    ]
    edge_at = jnp.where(quarter == 0, 0, y_cells - TILE)
    edge = lax.ppermute(
        lax.dynamic_slice_in_dim(estimate, edge_at, TILE, 1), ("blocks", "views"), both_ways(borders)
    )
    outgoing = pack(shifts, target[0].transpose(0, 2, 1), views_data[0], geo)
    outgoing, edge = lax.optimization_barrier((outgoing, edge))
    arrived = lax.all_to_all(
        outgoing.reshape(peer_count, capacity + 1, 1, BRICK),
        ("blocks", "rows"), split_axis=0, concat_axis=0, tiled=True,
    ).reshape(peer_count * (capacity + 1), 1, BRICK)
    ids = jnp.stack([place, row % 2, quarter, turned]).astype(jnp.int32)
    taps = lax.all_gather(psf_taps, "views", axis=0, tiled=True)
    w = (taps / jnp.sum(taps, axis=2, keepdims=True)).reshape(-1)
    halo = f32(2, HALO, part + 2 * TILE, BRICK)
    own, *sent = call(
        part_kernel, "part", [f32(2, x_cells, part + 2 * TILE, BRICK), halo, halo],
        (ids, estimate, edge),
        scratch=[pltpu.VMEM((2, y_cells + 2 * TILE, BRICK), jnp.float32)],
    )
    wide = f32(2, x_cells + 2 * HALO, part + 2 * TRIM, BRICK)
    est = call(extend_kernel, "extend", [wide], (ids, own, *swap_layers(*sent)))[0]
    below = forward(w, est, view_count, x_cells)
    arrived, below = lax.optimization_barrier((arrived, below))
    moved = unpack(ids, arrived, peer_count, capacity, brick_count, view_count)
    moved = [m.reshape(brick_cols, x_cells, part, BRICK) for m in moved]
    behind, ahead = turn(moved[1], 1, view_count), turn(moved[3], -1, view_count)
    across = turn(moved[2], 2, view_count)
    total = backward(w, ids, below, (0,), moved[:1], None, 0)[0]
    total = backward(w, ids, below, (3, 1), (behind, ahead), total, 0)[0]
    total, *sent = backward(w, ids, below, (2,), (across,), total, 2 * HALO)
    total, *sent = merge(ids, total, *swap_layers(*sent), x_cells + 2 * HALO)
    mid, partial = middle(w, est, total, view_count, x_cells)
    est, below = ends(w, (ids, total, *swap_rows(*sent), est), mid, partial)
    observed = (moved[0], ahead, across, behind)
    total, *sent = backward(w, ids, below, (0, 1, 2, 3), observed, None, HALO)
    total, *sent = merge(ids, total, *swap_layers(*sent), x_cells)
    args = (ids, total, *swap_rows(*sent), est)
    own = call(
        functools.partial(finish_kernel, view_count), "finish",
        [f32(x_cells, part, BRICK)] * 2, args,
        scratch=[pltpu.VMEM((part + 2 * TRIM, BRICK), jnp.float32)],
    )
    prev_a, next_b = turn(own[0], 1, view_count), turn(own[1], -1, view_count)
    prev_b, next_a = turn(own[1], 1, view_count), turn(own[0], -1, view_count)
    far_a, far_b = turn(prev_a, 1, view_count), turn(next_b, -1, view_count)
    pieces = (*own, next_a, next_b, far_a, far_b, prev_a, prev_b)
    return call(
        functools.partial(join_kernel, view_count), "join", [f32(x_cells, y_cells, z_cells)],
        (ids, *pieces),
    )[0]


def solution(mesh):
    placed = (
        P("rows", "blocks", None),
        P("views", "rows", "blocks", None),
        P("views", "rows", "blocks", None),
        P("views", None, None),
        P("views"),
    )
    return jax.shard_map(
        per_device, mesh=mesh, in_specs=placed, out_specs=P("rows", "blocks", None), check_vma=False
    )
```

```python
import functools
import jax
import jax.numpy as jnp
from jax import lax
from jax.experimental import pallas as pl
from jax.experimental.pallas import tpu as pltpu
from jax.sharding import PartitionSpec as P

VMEM = pltpu.VMEM
BRICK = 128
HALO = 3
ITERS = 2
GROUP = 16
SPARE = 8
TAPS = 2 * HALO + 1
TILE = 8
TRIM = 4


def div_mod(x, n):
    if n & (n - 1):
        return x // n, x % n
    return lax.shift_right_logical(x, n.bit_length() - 1), x & (n - 1)


def lane_sum(x):
    return jnp.sum(x, axis=1, keepdims=True)


def pack_kernel(geo, shift_ref, target_ref, views_ref, out_ref, rolled, pos_v, pos_s, sem):
    peers, cap, x_cells, y_cells, brick_cols, row_count, all_cols, view_count = geo
    groups = brick_cols * x_cells
    rows_per = cap + 1
    t = target_ref[...]
    t, bz = div_mod(t, brick_cols)
    line, column = div_mod(t, all_cols)
    block, y = div_mod(column, y_cells)
    row, x = div_mod(line, x_cells)
    dest = block * row_count + row
    quarter, y = div_mod(y, y_cells // view_count)
    quarter = jnp.where(block % 2 == 1, view_count - 1 - quarter, quarter)
    slot = ((quarter * brick_cols + bz) * x_cells + x) * (y_cells // view_count) + y + 1
    high, low = div_mod(slot, 64)
    peer_id = lax.broadcasted_iota(jnp.int32, (peers, y_cells), 0)
    before = (
        lax.broadcasted_iota(jnp.int32, (y_cells, y_cells), 0)
        < lax.broadcasted_iota(jnp.int32, (y_cells, y_cells), 1)
    ).astype(jnp.bfloat16)
    kid = lax.broadcasted_iota(jnp.int32, (BRICK, y_cells), 0)
    carry = jnp.zeros((peers, 1), jnp.float32)
    listed = jnp.zeros((2 * peers, BRICK), jnp.float32)
    for g in range(groups):
        here = (g % x_cells, slice(g // x_cells, g // x_cells + 1))
        d = dest[here]
        hot = d == peer_id
        hot_f = hot.astype(jnp.float32)
        ahead = jnp.dot(hot_f.astype(jnp.bfloat16), before, preferred_element_type=jnp.float32)
        ranks = jnp.sum(hot_f * (ahead + carry), axis=0, keepdims=True)
        carry = carry + lane_sum(hot_f)
        rank_i = ranks.astype(jnp.int32)
        pos_v[g : g + 1, :] = d * rows_per + rank_i
        h = hot_f * high[here].astype(jnp.float32)
        l = hot_f * low[here].astype(jnp.float32)
        both = jnp.concatenate([h, l], axis=0).astype(jnp.bfloat16)
        at = (rank_i == kid).astype(jnp.float32).astype(jnp.bfloat16)
        listed = listed + lax.dot_general(
            both, at, (((1,), (1,)), ((), ())), preferred_element_type=jnp.float32
        )
    copy = pltpu.make_async_copy(pos_v, pos_s, sem)
    copy.start()
    entries = 64.0 * listed[:peers] + listed[peers:]
    for p in range(peers):
        out_ref[p * rows_per + cap] = entries[p : p + 1, :]
    shift = shift_ref[0]
    for bz_i in range(brick_cols):
        for x in range(x_cells):
            rolled[bz_i * x_cells + x] = pltpu.roll(
                views_ref[x, :, bz_i * BRICK : (bz_i + 1) * BRICK], shift, 1
            )
    copy.wait()

    def body(g, c):
        for base in range(0, y_cells, GROUP):
            places = [pos_s[g, base + i] for i in range(GROUP)]
            rows = [rolled[g, base + i : base + i + 1, :] for i in range(GROUP)]
            for place, row in zip(places, rows):
                out_ref[place] = row
        return c

    lax.fori_loop(0, groups, body, 0, unroll=2)


def pack(shift, target, views, geo):
    peers, cap, x_cells, y_cells, brick_cols, row_count, all_cols, view_count = geo
    groups = brick_cols * x_cells
    return pl.pallas_call(
        functools.partial(pack_kernel, geo),
        out_shape=jax.ShapeDtypeStruct((peers * (cap + 1), 1, BRICK), jnp.float32),
        in_specs=[
            pl.BlockSpec(memory_space=pltpu.SMEM),
            pl.BlockSpec(memory_space=pltpu.VMEM),
            pl.BlockSpec(memory_space=pltpu.VMEM),
        ],
        out_specs=pl.BlockSpec(memory_space=pltpu.VMEM),
        scratch_shapes=[
            pltpu.VMEM((groups, y_cells, BRICK), jnp.float32),
            pltpu.VMEM((groups, y_cells), jnp.int32),
            pltpu.SMEM((groups, y_cells), jnp.int32),
            pltpu.SemaphoreType.DMA,
        ],
        name="pack",
    )(shift, target, views)


def unpack_kernel(peers, cap, slots, id_ref, in_ref, *refs):
    outs, (placed, list_v, idx_v, idx_s, sem) = refs[:-5], refs[-5:]
    rows_per = cap + 1
    for p in range(peers):
        list_v[p : p + 1, :] = in_ref[p * rows_per + cap]
    e = list_v[...].astype(jnp.int32)
    views, size = len(outs), slots // len(outs)
    quarter, rest = div_mod(jnp.maximum(e - 1, 0), size)
    turned = quarter - id_ref[0]
    turned = jnp.where(turned < 0, turned + views, turned)
    idx_v[...] = jnp.where(e > 0, turned * size + rest, slots)
    copy = pltpu.make_async_copy(idx_v, idx_s, sem)
    copy.start()
    copy.wait()

    def per_peer(p, c):
        for base in range(0, cap, GROUP):
            places = [idx_s[p, base + i] for i in range(GROUP)]
            rows = [in_ref[p * rows_per + base + i] for i in range(GROUP)]
            for place, row in zip(places, rows):
                placed[pl.ds(place, 1), :] = row
        return c

    lax.fori_loop(0, peers, per_peer, 0, unroll=2)
    for d, out in enumerate(outs):
        out[...] = placed[d * size : (d + 1) * size, :]


def unpack(ids, arrived, peers, cap, slots, views):
    return call(
        functools.partial(unpack_kernel, peers, cap, slots), "unpack",
        [f32(slots // views, BRICK)] * views, (ids, arrived),
        scratch=[
            pltpu.VMEM((slots + SPARE, BRICK), jnp.float32),
            pltpu.VMEM((peers, BRICK), jnp.float32),
            pltpu.VMEM((peers, BRICK), jnp.int32),
            pltpu.SMEM((peers, BRICK), jnp.int32),
            pltpu.SemaphoreType.DMA,
        ],
    )


def vmem():
    return pl.BlockSpec(memory_space=pltpu.VMEM)


def smem():
    return pl.BlockSpec(memory_space=pltpu.SMEM)


def f32(*shape):
    return jax.ShapeDtypeStruct(shape, jnp.float32)


def call(kernel, name, outs, args, scalars=1, scratch=(), work=1000):
    return pl.pallas_call(
        kernel,
        out_shape=outs,
        in_specs=[smem()] * scalars + [vmem()] * (len(args) - scalars),
        out_specs=[vmem()] * len(outs),
        scratch_shapes=list(scratch),
        cost_estimate=pl.CostEstimate(flops=work, bytes_accessed=work, transcendentals=0),
        compiler_params=pltpu.CompilerParams(vmem_limit_bytes=32 * 1024 * 1024),
        name=name,
    )(*args)


def taps_of(w_ref, view, dim, flip):
    base = (view * 3 + dim) * TAPS
    return [w_ref[base + (TAPS - 1 - k if flip else k)] for k in range(TAPS)]


def blur_z(a, b, w):
    lane = lax.broadcasted_iota(jnp.int32, a.shape, 1)
    out_a, out_b = w[HALO] * a, w[HALO] * b
    for s in range(1, HALO + 1):
        keep = lane < BRICK - s
        ra, rb = pltpu.roll(a, BRICK - s, 1), pltpu.roll(b, BRICK - s, 1)
        out_a += w[HALO + s] * jnp.where(keep, ra, rb)
        out_b += w[HALO + s] * jnp.where(keep, rb, 0.0)
        fresh = lane < s
        la, lb = pltpu.roll(a, s, 1), pltpu.roll(b, s, 1)
        out_a += w[HALO - s] * jnp.where(fresh, 0.0, la)
        out_b += w[HALO - s] * jnp.where(fresh, la, lb)
    return out_a, out_b


def y_rows(ref, at, w, n):
    total = w[0] * ref[(*at, pl.ds(TRIM - HALO, n))]
    for k in range(1, TAPS):
        total += w[k] * ref[(*at, pl.ds(TRIM - HALO + k, n))]
    return total


def weigh(layers, w):
    total = w[0] * layers[0]
    for k in range(1, TAPS):
        total += w[k] * layers[k]
    return total


def spread(layers, w, x):
    total = None
    for k in range(TAPS):
        i = x + k - HALO
        if 0 <= i < len(layers):
            term = w[k] * layers[i]
            total = term if total is None else total + term
    return total


def part_kernel(id_ref, est, edge, out_ref, send_in, send_out, wide):
    x_cells, y_cells, _ = est.shape
    part = out_ref.shape[2] - 2 * TILE
    start = pl.multiple_of(id_ref[2] * part, part)
    far = TILE + y_cells

    def body(x, carry):
        for c in range(2):
            lanes = slice(c * BRICK, (c + 1) * BRICK)
            wide[c, TILE:far, :] = est[x, :, lanes]
            wide[c, 0:TILE, :] = edge[x, :, lanes]
            wide[c, far : far + TILE, :] = edge[x, :, lanes]
            out_ref[c, x] = wide[c, pl.ds(start, part + 2 * TILE), :]
        return carry

    lax.fori_loop(0, x_cells, body, 0)
    base = x_cells - HALO
    for c in range(2):
        for i in range(HALO):
            send_in[c, i] = out_ref[c, (1 - id_ref[1]) * base + i]
            send_out[c, i] = out_ref[c, id_ref[1] * base + i]


def extend_kernel(id_ref, own, outer, inner, out_ref):
    x_cells = own.shape[1]
    odd = id_ref[1]
    rows = slice(TRIM, own.shape[2] - TRIM)
    base = x_cells + HALO
    for c in range(2):
        for i in range(x_cells):
            out_ref[c, HALO + i] = own[c, i, rows, :]
        for i in range(HALO):
            out_ref[c, (1 - odd) * base + i] = inner[c, i, rows, :]
            out_ref[c, odd * base + i] = outer[c, i, rows, :]


def forward_kernel(w_ref, est, out_ref, partial):
    views, _, x_cells, part, _ = out_ref.shape

    def per_view(u, carry):
        wx, wy, wz = (taps_of(w_ref, u, dim, False) for dim in range(3))

        def per_tile(t, carry):
            at = pl.ds(pl.multiple_of(t * TILE, TILE), TILE)
            for c in range(2):
                layers = [est[c, i, at, :] for i in range(x_cells + 2 * HALO)]
                for x in range(x_cells):
                    partial[c, x, at, :] = weigh(layers[x : x + TAPS], wx)
            return carry

        lax.fori_loop(0, (part + 2 * TRIM) // TILE, per_tile, 0, unroll=True)

        def per_layer(x, carry):
            rows = [y_rows(partial, (c, x), wy, part) for c in range(2)]
            out_ref[u, 0, x], out_ref[u, 1, x] = blur_z(*rows, wz)
            return carry

        lax.fori_loop(0, x_cells, per_layer, 0, unroll=True)
        return carry

    lax.fori_loop(0, views, per_view, 0)


def forward(w, est, views, x_cells):
    rows = est.shape[2]
    return call(
        forward_kernel, "forward", [f32(views, 2, x_cells, rows - 2 * TRIM, BRICK)], (w, est),
        scratch=[pltpu.VMEM((2, x_cells, rows, BRICK), jnp.float32)],
    )[0]


def blur_x_tile(est, at, wx, out, c, x_cells, rows):
    layers = [est[c, i, at, :] for i in range(x_cells + 2 * HALO)]
    for x in range(x_cells):
        out[c, x, rows, :] = weigh(layers[x : x + TAPS], wx)


def middle_kernel(w_ref, est, total, out_ref, part_ref, fresh):
    views, _, x_cells, part, _ = out_ref.shape
    tall = part_ref.shape[3]
    rows = slice(TILE, TILE + tall)
    for c in range(2):
        for i in range(x_cells + 2 * HALO):
            fresh[c, i] = est[c, i, rows, :] * total[c, i, rows, :] / views

    def per_view(u, carry):
        wx, wy, wz = (taps_of(w_ref, u, dim, False) for dim in range(3))

        def per_tile(t, carry):
            at = pl.ds(pl.multiple_of(t * TILE, TILE), TILE)
            for c in range(2):
                blur_x_tile(fresh, at, wx, part_ref.at[u], c, x_cells, at)
            return carry

        lax.fori_loop(0, tall // TILE, per_tile, 0, unroll=True)

        def per_layer(x, carry):
            rows = [y_rows(part_ref, (u, c, x), wy, part) for c in range(2)]
            out_ref[u, 0, x], out_ref[u, 1, x] = blur_z(*rows, wz)
            return carry

        lax.fori_loop(0, x_cells, per_layer, 0, unroll=True)
        return carry

    lax.fori_loop(0, views, per_view, 0)


def middle(w, est, total, views, x_cells):
    tall = est.shape[2] - 2 * TILE
    return call(
        middle_kernel, "middle",
        [f32(views, 2, x_cells, tall - TILE, BRICK), f32(views, 2, x_cells, tall, BRICK)],
        (w, est, total), scratch=[pltpu.VMEM((2, x_cells + 2 * HALO, tall, BRICK), jnp.float32)],
    )


def renew(views, id_ref, total, outer, inner, est, out_ref):
    layers, rows = out_ref.shape[1:3]
    odd = lax.rem(id_ref[2], 2)
    spans = (slice(0, TILE), slice(TILE, rows - TILE), slice(rows - TILE, rows))
    for c in range(2):
        for i in range(layers):
            low, high = low_high(odd, inner[c, i], outer[c, i])
            for at, more in zip(spans, (low, None, high)):
                value = total[c, i, at, :]
                if more is not None:
                    value += more
                out_ref[c, i, at, :] = est[c, i, at, :] * value / views


def ends_kernel(w_ref, id_ref, total, outer, inner, est, mid, part_ref, new, out_ref, strip):
    views, _, x_cells, part, _ = out_ref.shape
    tall = part_ref.shape[3]
    renew(views, id_ref, total, outer, inner, est, new)
    sides = ((0, 0, 0, TILE, 0), (tall + TILE, TILE, tall - TILE, 0, part - TILE))

    def per_view(u, carry):
        wx, wy, wz = (taps_of(w_ref, u, dim, False) for dim in range(3))
        for s, (at, here, kept, there, to) in enumerate(sides):
            for c in range(2):
                blur_x_tile(new, slice(at, at + TILE), wx, strip.at[s], c, x_cells, slice(here, here + TILE))
        for x in range(x_cells):
            for s, (at, here, kept, there, to) in enumerate(sides):
                for c in range(2):
                    strip[s, c, x, there : there + TILE, :] = part_ref[u, c, x, kept : kept + TILE, :]
                rows = blur_z(*(y_rows(strip, (s, c, x), wy, TILE) for c in range(2)), wz)
                for c in range(2):
                    out_ref[u, c, x, to : to + TILE, :] = rows[c]
            for c in range(2):
                out_ref[u, c, x, TILE : part - TILE, :] = mid[u, c, x]
        return carry

    lax.fori_loop(0, views, per_view, 0)


def ends(w, args, mid, partial):
    views, _, x, tall, _ = partial.shape
    rows = tall + 2 * TILE
    return call(
        ends_kernel, "ends", [f32(2, x + 2 * HALO, rows, BRICK), f32(views, 2, x, tall + TILE, BRICK)],
        (w, *args, mid, partial), 2, scratch=[pltpu.VMEM((2, 2, x, 2 * TILE, BRICK), jnp.float32)],
    )


def backward_kernel(views, rels, add, w_ref, id_ref, below, *refs):
    observed, refs = refs[: len(rels)], refs[len(rels) :]
    before, refs = (refs[0], refs[1:]) if add else (None, refs)
    out_ref, *sends = refs[:-2]
    wide, partial = refs[-2:]
    x_cells, part = below.shape[2:4]
    layers_out = out_ref.shape[1]
    zeros = jnp.zeros((TILE, BRICK), jnp.float32)
    for c in range(2):
        for x in range(x_cells):
            wide[c, x, 0:TILE, :] = zeros
            wide[c, x, TILE + part : 2 * TILE + part, :] = zeros
    for d, obs in zip(rels, observed):
        u = lax.rem(id_ref[0] + d, views)
        wx, wy, wz = (taps_of(w_ref, u, dim, True) for dim in range(3))

        def per_layer(x, carry, u=u, obs=obs, wy=wy, wz=wz):
            rows = blur_z(*(obs[c, x] / below[u, c, x] for c in range(2)), wz)
            for c in range(2):
                wide[c, x, TILE : TILE + part, :] = rows[c]
                partial[c, x] = y_rows(wide, (c, x), wy, part + 2 * TRIM)
            return carry

        lax.fori_loop(0, x_cells, per_layer, 0, unroll=True)

        def per_tile(t, carry, wx=wx, source=before):
            at = pl.ds(pl.multiple_of(t * TILE, TILE), TILE)
            for c in range(2):
                layers = [partial[c, x, at, :] for x in range(x_cells)]
                for i in range(layers_out):
                    value = spread(layers, wx, i - HALO)
                    out_ref[c, i, at, :] = value if source is None else value + source[c, i, at, :]
            return carry

        lax.fori_loop(0, (part + 2 * TRIM) // TILE, per_tile, 0, unroll=True)
        before = out_ref
    odd = id_ref[1]
    for slot, send in enumerate(sends):
        base = layers_out - send.shape[1]
        for c in range(2):
            for i in range(send.shape[1]):
                send[c, i] = out_ref[c, (odd if slot else 1 - odd) * base + i]


def backward(w, ids, below, rels, observed, before, count):
    views, _, x, part, _ = below.shape
    rows = part + 2 * TRIM
    outs = [f32(2, x + 2 * HALO, rows, BRICK)] + [f32(2, count, rows, BRICK)] * (2 if count else 0)
    given = () if before is None else (before,)
    return call(
        functools.partial(backward_kernel, views, rels, before is not None), "backward", outs,
        (w, ids, below, *observed, *given), 2,
        scratch=[
            pltpu.VMEM((2, x, part + 2 * TILE, BRICK), jnp.float32),
            pltpu.VMEM((2, x, rows, BRICK), jnp.float32),
        ],
    )


def low_high(odd, inner, outer):
    return jnp.where(odd == 1, inner, outer), jnp.where(odd == 1, outer, inner)


def merge_kernel(id_ref, total, outer, inner, out_ref, send_in, send_out):
    layers, rows = out_ref.shape[1:3]
    count = inner.shape[1]
    skip = (total.shape[1] - layers) // 2
    odd, odd_part = id_ref[1], lax.rem(id_ref[2], 2)
    for c in range(2):
        for i in range(count):
            low, high = low_high(odd, inner[c, i], outer[c, i])
            out_ref[c, i] = total[c, skip + i] + low
            out_ref[c, layers - count + i] = total[c, skip + layers - count + i] + high
        for i in range(count, layers - count):
            out_ref[c, i] = total[c, skip + i]
        for i in range(layers):
            top, bottom = out_ref[c, i, 0:TILE, :], out_ref[c, i, rows - TILE : rows, :]
            send_in[c, i], send_out[c, i] = low_high(odd_part, top, bottom)


def merge(ids, total, outer, inner, layers):
    rows = total.shape[2]
    outs = [f32(2, layers, rows, BRICK)] + [f32(2, layers, TILE, BRICK)] * 2
    return call(merge_kernel, "merge", outs, (ids, total, outer, inner))


def finish_kernel(views, id_ref, total, outer, inner, est, out_a, out_b, wide):
    layers, rows = total.shape[1:3]
    odd = lax.rem(id_ref[2], 2)
    own = slice(TRIM, rows - TRIM)
    for c, out in ((0, out_a), (1, out_b)):
        for i in range(layers):
            low, high = low_high(odd, inner[c, i], outer[c, i])
            wide[c, i, 0:TILE, :] = total[c, i, 0:TILE, :] + low
            wide[c, i, TILE : rows - TILE, :] = total[c, i, TILE : rows - TILE, :]
            wide[c, i, rows - TILE : rows, :] = total[c, i, rows - TILE : rows, :] + high
    for c, out in ((0, out_a), (1, out_b)):
        for i in range(layers):
            out[i] = est[c, HALO + i, own, :] * wide[c, i, own, :] / views


def join_kernel(views, id_ref, *refs):
    pieces, out_ref = refs[: 2 * views], refs[2 * views]
    part = pieces[0].shape[1]
    for d in range(views):
        place = lax.rem(id_ref[0] + d, views)
        place = jnp.where(id_ref[3] == 1, views - 1 - place, place)
        at = pl.ds(pl.multiple_of(place * part, part), part)
        out_ref[:, at, 0:BRICK] = pieces[2 * d][...]
        out_ref[:, at, BRICK : 2 * BRICK] = pieces[2 * d + 1][...]


def snake(at, views):
    block, quarter = divmod(at, views)
    return block * views + (views - 1 - quarter if block % 2 else quarter)


def both_ways(links):
    return links + [(j, i) for i, j in links]


def swap_layers(inner, outer):
    count = lax.axis_size("rows")
    outer = lax.ppermute(outer, "rows", both_ways([(i, i + 1) for i in range(1, count - 1, 2)]))
    inner = lax.ppermute(inner, "rows", both_ways([(i, i + 1) for i in range(0, count, 2)]))
    return outer, inner


def swap_rows(inner, outer):
    axes, views = ("blocks", "views"), lax.axis_size("views")
    chain = [snake(i, views) for i in range(lax.axis_size(axes))]
    outer = lax.ppermute(outer, axes, both_ways(list(zip(chain[1:-1:2], chain[2::2]))))
    inner = lax.ppermute(inner, axes, both_ways(list(zip(chain[::2], chain[1::2]))))
    return outer, inner


def turn(value, step, count):
    return lax.ppermute(value, "views", [(i, (i + step) % count) for i in range(count)])


def per_device(estimate, views_data, target, psf_taps, shifts):
    x_cells, y_cells, z_cells = estimate.shape
    row_count = lax.axis_size("rows")
    block_count = lax.axis_size("blocks")
    peer_count = block_count * row_count
    view_count = lax.axis_size("views")
    brick_cols = z_cells // BRICK
    brick_count = x_cells * y_cells * brick_cols
    capacity = 2 * brick_count // peer_count
    part = y_cells // view_count
    all_cols = y_cells * block_count
    geo = (peer_count, capacity, x_cells, y_cells, brick_cols, row_count, all_cols, view_count)
    row, place = lax.axis_index("rows"), lax.axis_index("views")
    turned = lax.axis_index("blocks") % 2
    quarter = jnp.where(turned == 1, view_count - 1 - place, place)
    borders = [
        (snake(b * view_count - 1, view_count), snake(b * view_count, view_count))
        for b in range(1, block_count)
    ]
    edge_at = jnp.where(quarter == 0, 0, y_cells - TILE)
    edge = lax.ppermute(
        lax.dynamic_slice_in_dim(estimate, edge_at, TILE, 1), ("blocks", "views"), both_ways(borders)
    )
    outgoing = pack(shifts, target[0].transpose(0, 2, 1), views_data[0], geo)
    outgoing, edge = lax.optimization_barrier((outgoing, edge))
    arrived = lax.all_to_all(
        outgoing.reshape(peer_count, capacity + 1, 1, BRICK),
        ("blocks", "rows"), split_axis=0, concat_axis=0, tiled=True,
    ).reshape(peer_count * (capacity + 1), 1, BRICK)
    ids = jnp.stack([place, row % 2, quarter, turned]).astype(jnp.int32)
    taps = lax.all_gather(psf_taps, "views", axis=0, tiled=True)
    w = (taps / jnp.sum(taps, axis=2, keepdims=True)).reshape(-1)
    halo = f32(2, HALO, part + 2 * TILE, BRICK)
    own, *sent = call(
        part_kernel, "part", [f32(2, x_cells, part + 2 * TILE, BRICK), halo, halo],
        (ids, estimate, edge),
        scratch=[pltpu.VMEM((2, y_cells + 2 * TILE, BRICK), jnp.float32)],
    )
    wide = f32(2, x_cells + 2 * HALO, part + 2 * TRIM, BRICK)
    est = call(extend_kernel, "extend", [wide], (ids, own, *swap_layers(*sent)))[0]
    below = forward(w, est, view_count, x_cells)
    arrived, below = lax.optimization_barrier((arrived, below))
    moved = unpack(ids, arrived, peer_count, capacity, brick_count, view_count)
    moved = [m.reshape(brick_cols, x_cells, part, BRICK) for m in moved]
    behind, ahead = turn(moved[1], 1, view_count), turn(moved[3], -1, view_count)
    across = turn(moved[2], 2, view_count)
    total = backward(w, ids, below, (0,), moved[:1], None, 0)[0]
    total = backward(w, ids, below, (3, 1), (behind, ahead), total, 0)[0]
    total, *sent = backward(w, ids, below, (2,), (across,), total, 2 * HALO)
    total, *sent = merge(ids, total, *swap_layers(*sent), x_cells + 2 * HALO)
    mid, partial = middle(w, est, total, view_count, x_cells)
    est, below = ends(w, (ids, total, *swap_rows(*sent), est), mid, partial)
    observed = (moved[0], ahead, across, behind)
    total, *sent = backward(w, ids, below, (0, 1, 2, 3), observed, None, HALO)
    total, *sent = merge(ids, total, *swap_layers(*sent), x_cells)
    args = (ids, total, *swap_rows(*sent), est)
    own = call(
        functools.partial(finish_kernel, view_count), "finish",
        [f32(x_cells, part, BRICK)] * 2, args,
        scratch=[pltpu.VMEM((2, x_cells, part + 2 * TRIM, BRICK), jnp.float32)],
    )
    prev_a, next_b = turn(own[0], 1, view_count), turn(own[1], -1, view_count)
    prev_b, next_a = turn(own[1], 1, view_count), turn(own[0], -1, view_count)
    far_a, far_b = turn(prev_a, 1, view_count), turn(next_b, -1, view_count)
    pieces = (*own, next_a, next_b, far_a, far_b, prev_a, prev_b)
    return call(
        functools.partial(join_kernel, view_count), "join", [f32(x_cells, y_cells, z_cells)],
        (ids, *pieces),
    )[0]


def solution(mesh):
    placed = (
        P("rows", "blocks", None),
        P("views", "rows", "blocks", None),
        P("views", "rows", "blocks", None),
        P("views", None, None),
        P("views"),
    )
    return jax.shard_map(
        per_device, mesh=mesh, in_specs=placed, out_specs=P("rows", "blocks", None), check_vma=False
    )
```

```python
import functools
import jax
import jax.numpy as jnp
from jax import lax
from jax.experimental import pallas as pl
from jax.experimental.pallas import tpu as pltpu
from jax.sharding import PartitionSpec as P

VMEM = pltpu.VMEM
BRICK = 128
HALO = 3
ITERS = 2
GROUP = 16
SPARE = 8
TAPS = 2 * HALO + 1
TILE = 8
TRIM = 4


def div_mod(x, n):
    if n & (n - 1):
        return x // n, x % n
    return lax.shift_right_logical(x, n.bit_length() - 1), x & (n - 1)


def lane_sum(x):
    return jnp.sum(x, axis=1, keepdims=True)


def pack_kernel(geo, shift_ref, target_ref, views_ref, out_ref, rolled, pos_v, pos_s, sem):
    peers, cap, x_cells, y_cells, brick_cols, row_count, all_cols, view_count = geo
    groups = brick_cols * x_cells
    rows_per = cap + 1
    t = target_ref[...]
    t, bz = div_mod(t, brick_cols)
    line, column = div_mod(t, all_cols)
    block, y = div_mod(column, y_cells)
    row, x = div_mod(line, x_cells)
    dest = block * row_count + row
    quarter, y = div_mod(y, y_cells // view_count)
    quarter = jnp.where(block % 2 == 1, view_count - 1 - quarter, quarter)
    slot = ((quarter * brick_cols + bz) * x_cells + x) * (y_cells // view_count) + y + 1
    high, low = div_mod(slot, 64)
    peer_id = lax.broadcasted_iota(jnp.int32, (peers, y_cells), 0)
    before = (
        lax.broadcasted_iota(jnp.int32, (y_cells, y_cells), 0)
        < lax.broadcasted_iota(jnp.int32, (y_cells, y_cells), 1)
    ).astype(jnp.bfloat16)
    kid = lax.broadcasted_iota(jnp.int32, (BRICK, y_cells), 0)
    carry = jnp.zeros((peers, 1), jnp.float32)
    listed = jnp.zeros((2 * peers, BRICK), jnp.float32)
    for g in range(groups):
        here = (g % x_cells, slice(g // x_cells, g // x_cells + 1))
        d = dest[here]
        hot = d == peer_id
        hot_f = hot.astype(jnp.float32)
        ahead = jnp.dot(hot_f.astype(jnp.bfloat16), before, preferred_element_type=jnp.float32)
        ranks = jnp.sum(hot_f * (ahead + carry), axis=0, keepdims=True)
        carry = carry + lane_sum(hot_f)
        rank_i = ranks.astype(jnp.int32)
        pos_v[g : g + 1, :] = d * rows_per + rank_i
        h = hot_f * high[here].astype(jnp.float32)
        l = hot_f * low[here].astype(jnp.float32)
        both = jnp.concatenate([h, l], axis=0).astype(jnp.bfloat16)
        at = (rank_i == kid).astype(jnp.float32).astype(jnp.bfloat16)
        listed = listed + lax.dot_general(
            both, at, (((1,), (1,)), ((), ())), preferred_element_type=jnp.float32
        )
    copy = pltpu.make_async_copy(pos_v, pos_s, sem)
    copy.start()
    entries = 64.0 * listed[:peers] + listed[peers:]
    for p in range(peers):
        out_ref[p * rows_per + cap] = entries[p : p + 1, :]
    shift = shift_ref[0]
    for bz_i in range(brick_cols):
        for x in range(x_cells):
            rolled[bz_i * x_cells + x] = pltpu.roll(
                views_ref[x, :, bz_i * BRICK : (bz_i + 1) * BRICK], shift, 1
            )
    copy.wait()

    def body(g, c):
        for base in range(0, y_cells, GROUP):
            places = [pos_s[g, base + i] for i in range(GROUP)]
            rows = [rolled[g, base + i : base + i + 1, :] for i in range(GROUP)]
            for place, row in zip(places, rows):
                out_ref[place] = row
        return c

    lax.fori_loop(0, groups, body, 0, unroll=2)


def pack(shift, target, views, geo):
    peers, cap, x_cells, y_cells, brick_cols, row_count, all_cols, view_count = geo
    groups = brick_cols * x_cells
    return pl.pallas_call(
        functools.partial(pack_kernel, geo),
        out_shape=jax.ShapeDtypeStruct((peers * (cap + 1), 1, BRICK), jnp.float32),
        in_specs=[
            pl.BlockSpec(memory_space=pltpu.SMEM),
            pl.BlockSpec(memory_space=pltpu.VMEM),
            pl.BlockSpec(memory_space=pltpu.VMEM),
        ],
        out_specs=pl.BlockSpec(memory_space=pltpu.VMEM),
        scratch_shapes=[
            pltpu.VMEM((groups, y_cells, BRICK), jnp.float32),
            pltpu.VMEM((groups, y_cells), jnp.int32),
            pltpu.SMEM((groups, y_cells), jnp.int32),
            pltpu.SemaphoreType.DMA,
        ],
        name="pack",
    )(shift, target, views)


def unpack_kernel(peers, cap, slots, id_ref, in_ref, *refs):
    outs, (placed, list_v, idx_v, idx_s, sem) = refs[:-5], refs[-5:]
    rows_per = cap + 1
    for p in range(peers):
        list_v[p : p + 1, :] = in_ref[p * rows_per + cap]
    e = list_v[...].astype(jnp.int32)
    views, size = len(outs), slots // len(outs)
    quarter, rest = div_mod(jnp.maximum(e - 1, 0), size)
    turned = quarter - id_ref[0]
    turned = jnp.where(turned < 0, turned + views, turned)
    idx_v[...] = jnp.where(e > 0, turned * size + rest, slots)
    copy = pltpu.make_async_copy(idx_v, idx_s, sem)
    copy.start()
    copy.wait()

    def per_peer(p, c):
        for base in range(0, cap, GROUP):
            places = [idx_s[p, base + i] for i in range(GROUP)]
            rows = [in_ref[p * rows_per + base + i] for i in range(GROUP)]
            for place, row in zip(places, rows):
                placed[pl.ds(place, 1), :] = row
        return c

    lax.fori_loop(0, peers, per_peer, 0)
    for d, out in enumerate(outs):
        out[...] = placed[d * size : (d + 1) * size, :]


def unpack(ids, arrived, peers, cap, slots, views):
    return call(
        functools.partial(unpack_kernel, peers, cap, slots), "unpack",
        [f32(slots // views, BRICK)] * views, (ids, arrived),
        scratch=[
            pltpu.VMEM((slots + SPARE, BRICK), jnp.float32),
            pltpu.VMEM((peers, BRICK), jnp.float32),
            pltpu.VMEM((peers, BRICK), jnp.int32),
            pltpu.SMEM((peers, BRICK), jnp.int32),
            pltpu.SemaphoreType.DMA,
        ],
    )


def vmem():
    return pl.BlockSpec(memory_space=pltpu.VMEM)


def smem():
    return pl.BlockSpec(memory_space=pltpu.SMEM)


def f32(*shape):
    return jax.ShapeDtypeStruct(shape, jnp.float32)


def call(kernel, name, outs, args, scalars=1, scratch=(), work=1000):
    return pl.pallas_call(
        kernel,
        out_shape=outs,
        in_specs=[smem()] * scalars + [vmem()] * (len(args) - scalars),
        out_specs=[vmem()] * len(outs),
        scratch_shapes=list(scratch),
        cost_estimate=pl.CostEstimate(flops=work, bytes_accessed=work, transcendentals=0),
        compiler_params=pltpu.CompilerParams(vmem_limit_bytes=32 * 1024 * 1024),
        name=name,
    )(*args)


def taps_of(w_ref, view, dim, flip):
    base = (view * 3 + dim) * TAPS
    return [w_ref[base + (TAPS - 1 - k if flip else k)] for k in range(TAPS)]


def blur_z(a, b, w):
    lane = lax.broadcasted_iota(jnp.int32, a.shape, 1)
    out_a, out_b = w[HALO] * a, w[HALO] * b
    for s in range(1, HALO + 1):
        keep = lane < BRICK - s
        ra, rb = pltpu.roll(a, BRICK - s, 1), pltpu.roll(b, BRICK - s, 1)
        out_a += w[HALO + s] * jnp.where(keep, ra, rb)
        out_b += w[HALO + s] * jnp.where(keep, rb, 0.0)
        fresh = lane < s
        la, lb = pltpu.roll(a, s, 1), pltpu.roll(b, s, 1)
        out_a += w[HALO - s] * jnp.where(fresh, 0.0, la)
        out_b += w[HALO - s] * jnp.where(fresh, la, lb)
    return out_a, out_b


def y_rows(ref, at, w, n):
    total = w[0] * ref[(*at, pl.ds(TRIM - HALO, n))]
    for k in range(1, TAPS):
        total += w[k] * ref[(*at, pl.ds(TRIM - HALO + k, n))]
    return total


def weigh(layers, w):
    total = w[0] * layers[0]
    for k in range(1, TAPS):
        total += w[k] * layers[k]
    return total


def spread(layers, w, x):
    total = None
    for k in range(TAPS):
        i = x + k - HALO
        if 0 <= i < len(layers):
            term = w[k] * layers[i]
            total = term if total is None else total + term
    return total


def part_kernel(id_ref, est, edge, out_ref, send_in, send_out, wide):
    x_cells, y_cells, _ = est.shape
    part = out_ref.shape[2] - 2 * TILE
    start = pl.multiple_of(id_ref[2] * part, part)
    far = TILE + y_cells

    def body(x, carry):
        for c in range(2):
            lanes = slice(c * BRICK, (c + 1) * BRICK)
            wide[c, TILE:far, :] = est[x, :, lanes]
            wide[c, 0:TILE, :] = edge[x, :, lanes]
            wide[c, far : far + TILE, :] = edge[x, :, lanes]
            out_ref[c, x] = wide[c, pl.ds(start, part + 2 * TILE), :]
        return carry

    lax.fori_loop(0, x_cells, body, 0)
    base = x_cells - HALO
    for c in range(2):
        for i in range(HALO):
            send_in[c, i] = out_ref[c, (1 - id_ref[1]) * base + i]
            send_out[c, i] = out_ref[c, id_ref[1] * base + i]


def extend_kernel(id_ref, own, outer, inner, out_ref):
    x_cells = own.shape[1]
    odd = id_ref[1]
    rows = slice(TRIM, own.shape[2] - TRIM)
    base = x_cells + HALO
    for c in range(2):
        for i in range(x_cells):
            out_ref[c, HALO + i] = own[c, i, rows, :]
        for i in range(HALO):
            out_ref[c, (1 - odd) * base + i] = inner[c, i, rows, :]
            out_ref[c, odd * base + i] = outer[c, i, rows, :]


def forward_kernel(w_ref, est, out_ref, partial):
    views, _, x_cells, part, _ = out_ref.shape

    def per_view(u, carry):
        wx, wy, wz = (taps_of(w_ref, u, dim, False) for dim in range(3))

        def per_tile(t, carry):
            at = pl.ds(pl.multiple_of(t * TILE, TILE), TILE)
            for c in range(2):
                layers = [est[c, i, at, :] for i in range(x_cells + 2 * HALO)]
                for x in range(x_cells):
                    partial[c, x, at, :] = weigh(layers[x : x + TAPS], wx)
            return carry

        lax.fori_loop(0, (part + 2 * TRIM) // TILE, per_tile, 0, unroll=True)

        def per_layer(x, carry):
            rows = [y_rows(partial, (c, x), wy, part) for c in range(2)]
            out_ref[u, 0, x], out_ref[u, 1, x] = blur_z(*rows, wz)
            return carry

        lax.fori_loop(0, x_cells, per_layer, 0, unroll=True)
        return carry

    lax.fori_loop(0, views, per_view, 0)


def forward(w, est, views, x_cells):
    rows = est.shape[2]
    return call(
        forward_kernel, "forward", [f32(views, 2, x_cells, rows - 2 * TRIM, BRICK)], (w, est),
        scratch=[pltpu.VMEM((2, x_cells, rows, BRICK), jnp.float32)],
    )[0]


def blur_x_tile(est, at, wx, out, c, x_cells, rows):
    layers = [est[c, i, at, :] for i in range(x_cells + 2 * HALO)]
    for x in range(x_cells):
        out[c, x, rows, :] = weigh(layers[x : x + TAPS], wx)


def middle_kernel(w_ref, est, total, out_ref, part_ref, fresh):
    views, _, x_cells, part, _ = out_ref.shape
    tall = part_ref.shape[3]
    rows = slice(TILE, TILE + tall)
    for c in range(2):
        for i in range(x_cells + 2 * HALO):
            fresh[c, i] = est[c, i, rows, :] * total[c, i, rows, :] / views

    def per_view(u, carry):
        wx, wy, wz = (taps_of(w_ref, u, dim, False) for dim in range(3))

        def per_tile(t, carry):
            at = pl.ds(pl.multiple_of(t * TILE, TILE), TILE)
            for c in range(2):
                blur_x_tile(fresh, at, wx, part_ref.at[u], c, x_cells, at)
            return carry

        lax.fori_loop(0, tall // TILE, per_tile, 0, unroll=True)

        def per_layer(x, carry):
            rows = [y_rows(part_ref, (u, c, x), wy, part) for c in range(2)]
            out_ref[u, 0, x], out_ref[u, 1, x] = blur_z(*rows, wz)
            return carry

        lax.fori_loop(0, x_cells, per_layer, 0, unroll=True)
        return carry

    lax.fori_loop(0, views, per_view, 0)


def middle(w, est, total, views, x_cells):
    tall = est.shape[2] - 2 * TILE
    return call(
        middle_kernel, "middle",
        [f32(views, 2, x_cells, tall - TILE, BRICK), f32(views, 2, x_cells, tall, BRICK)],
        (w, est, total), scratch=[pltpu.VMEM((2, x_cells + 2 * HALO, tall, BRICK), jnp.float32)],
    )


def renew(views, id_ref, total, outer, inner, est, out_ref):
    layers, rows = out_ref.shape[1:3]
    odd = lax.rem(id_ref[2], 2)
    spans = (slice(0, TILE), slice(TILE, rows - TILE), slice(rows - TILE, rows))
    for c in range(2):
        for i in range(layers):
            low, high = low_high(odd, inner[c, i], outer[c, i])
            for at, more in zip(spans, (low, None, high)):
                value = total[c, i, at, :]
                if more is not None:
                    value += more
                out_ref[c, i, at, :] = est[c, i, at, :] * value / views


def ends_kernel(w_ref, id_ref, total, outer, inner, est, mid, part_ref, new, out_ref, strip):
    views, _, x_cells, part, _ = out_ref.shape
    tall = part_ref.shape[3]
    renew(views, id_ref, total, outer, inner, est, new)
    sides = ((0, 0, 0, TILE, 0), (tall + TILE, TILE, tall - TILE, 0, part - TILE))

    def per_view(u, carry):
        wx, wy, wz = (taps_of(w_ref, u, dim, False) for dim in range(3))
        for s, (at, here, kept, there, to) in enumerate(sides):
            for c in range(2):
                blur_x_tile(new, slice(at, at + TILE), wx, strip.at[s], c, x_cells, slice(here, here + TILE))
        for x in range(x_cells):
            for s, (at, here, kept, there, to) in enumerate(sides):
                for c in range(2):
                    strip[s, c, x, there : there + TILE, :] = part_ref[u, c, x, kept : kept + TILE, :]
                rows = blur_z(*(y_rows(strip, (s, c, x), wy, TILE) for c in range(2)), wz)
                for c in range(2):
                    out_ref[u, c, x, to : to + TILE, :] = rows[c]
            for c in range(2):
                out_ref[u, c, x, TILE : part - TILE, :] = mid[u, c, x]
        return carry

    lax.fori_loop(0, views, per_view, 0)


def ends(w, args, mid, partial):
    views, _, x, tall, _ = partial.shape
    rows = tall + 2 * TILE
    return call(
        ends_kernel, "ends", [f32(2, x + 2 * HALO, rows, BRICK), f32(views, 2, x, tall + TILE, BRICK)],
        (w, *args, mid, partial), 2, scratch=[pltpu.VMEM((2, 2, x, 2 * TILE, BRICK), jnp.float32)],
    )


def backward_kernel(views, rels, add, w_ref, id_ref, below, *refs):
    observed, refs = refs[: len(rels)], refs[len(rels) :]
    before, refs = (refs[0], refs[1:]) if add else (None, refs)
    out_ref, *sends = refs[:-2]
    wide, partial = refs[-2:]
    x_cells, part = below.shape[2:4]
    layers_out = out_ref.shape[1]
    zeros = jnp.zeros((TILE, BRICK), jnp.float32)
    for c in range(2):
        for x in range(x_cells):
            wide[c, x, 0:TILE, :] = zeros
            wide[c, x, TILE + part : 2 * TILE + part, :] = zeros
    for d, obs in zip(rels, observed):
        u = lax.rem(id_ref[0] + d, views)
        wx, wy, wz = (taps_of(w_ref, u, dim, True) for dim in range(3))

        def per_layer(x, carry, u=u, obs=obs, wy=wy, wz=wz):
            rows = blur_z(*(obs[c, x] / below[u, c, x] for c in range(2)), wz)
            for c in range(2):
                wide[c, x, TILE : TILE + part, :] = rows[c]
                partial[c, x] = y_rows(wide, (c, x), wy, part + 2 * TRIM)
            return carry

        lax.fori_loop(0, x_cells, per_layer, 0, unroll=True)

        def per_tile(t, carry, wx=wx, source=before):
            at = pl.ds(pl.multiple_of(t * TILE, TILE), TILE)
            for c in range(2):
                layers = [partial[c, x, at, :] for x in range(x_cells)]
                for i in range(layers_out):
                    value = spread(layers, wx, i - HALO)
                    out_ref[c, i, at, :] = value if source is None else value + source[c, i, at, :]
            return carry

        lax.fori_loop(0, (part + 2 * TRIM) // TILE, per_tile, 0, unroll=True)
        before = out_ref
    odd = id_ref[1]
    for slot, send in enumerate(sends):
        base = layers_out - send.shape[1]
        for c in range(2):
            for i in range(send.shape[1]):
                send[c, i] = out_ref[c, (odd if slot else 1 - odd) * base + i]


def backward(w, ids, below, rels, observed, before, count):
    views, _, x, part, _ = below.shape
    rows = part + 2 * TRIM
    outs = [f32(2, x + 2 * HALO, rows, BRICK)] + [f32(2, count, rows, BRICK)] * (2 if count else 0)
    given = () if before is None else (before,)
    return call(
        functools.partial(backward_kernel, views, rels, before is not None), "backward", outs,
        (w, ids, below, *observed, *given), 2,
        scratch=[
            pltpu.VMEM((2, x, part + 2 * TILE, BRICK), jnp.float32),
            pltpu.VMEM((2, x, rows, BRICK), jnp.float32),
        ],
    )


def low_high(odd, inner, outer):
    return jnp.where(odd == 1, inner, outer), jnp.where(odd == 1, outer, inner)


def merge_kernel(id_ref, total, outer, inner, out_ref, send_in, send_out):
    layers, rows = out_ref.shape[1:3]
    count = inner.shape[1]
    skip = (total.shape[1] - layers) // 2
    odd, odd_part = id_ref[1], lax.rem(id_ref[2], 2)
    for c in range(2):
        for i in range(count):
            low, high = low_high(odd, inner[c, i], outer[c, i])
            out_ref[c, i] = total[c, skip + i] + low
            out_ref[c, layers - count + i] = total[c, skip + layers - count + i] + high
        for i in range(count, layers - count):
            out_ref[c, i] = total[c, skip + i]
        for i in range(layers):
            top, bottom = out_ref[c, i, 0:TILE, :], out_ref[c, i, rows - TILE : rows, :]
            send_in[c, i], send_out[c, i] = low_high(odd_part, top, bottom)


def merge(ids, total, outer, inner, layers):
    rows = total.shape[2]
    outs = [f32(2, layers, rows, BRICK)] + [f32(2, layers, TILE, BRICK)] * 2
    return call(merge_kernel, "merge", outs, (ids, total, outer, inner))


def finish_kernel(views, id_ref, total, outer, inner, est, out_a, out_b, wide):
    layers, rows = total.shape[1:3]
    odd = lax.rem(id_ref[2], 2)
    own = slice(TRIM, rows - TRIM)
    for c, out in ((0, out_a), (1, out_b)):
        for i in range(layers):
            low, high = low_high(odd, inner[c, i], outer[c, i])
            wide[c, i, 0:TILE, :] = total[c, i, 0:TILE, :] + low
            wide[c, i, TILE : rows - TILE, :] = total[c, i, TILE : rows - TILE, :]
            wide[c, i, rows - TILE : rows, :] = total[c, i, rows - TILE : rows, :] + high
    for c, out in ((0, out_a), (1, out_b)):
        for i in range(layers):
            out[i] = est[c, HALO + i, own, :] * wide[c, i, own, :] / views


def join_kernel(views, id_ref, *refs):
    pieces, out_ref = refs[: 2 * views], refs[2 * views]
    part = pieces[0].shape[1]
    for d in range(views):
        place = lax.rem(id_ref[0] + d, views)
        place = jnp.where(id_ref[3] == 1, views - 1 - place, place)
        at = pl.ds(pl.multiple_of(place * part, part), part)
        out_ref[:, at, 0:BRICK] = pieces[2 * d][...]
        out_ref[:, at, BRICK : 2 * BRICK] = pieces[2 * d + 1][...]


def snake(at, views):
    block, quarter = divmod(at, views)
    return block * views + (views - 1 - quarter if block % 2 else quarter)


def both_ways(links):
    return links + [(j, i) for i, j in links]


def swap_layers(inner, outer):
    count = lax.axis_size("rows")
    outer = lax.ppermute(outer, "rows", both_ways([(i, i + 1) for i in range(1, count - 1, 2)]))
    inner = lax.ppermute(inner, "rows", both_ways([(i, i + 1) for i in range(0, count, 2)]))
    return outer, inner


def swap_rows(inner, outer):
    axes, views = ("blocks", "views"), lax.axis_size("views")
    chain = [snake(i, views) for i in range(lax.axis_size(axes))]
    outer = lax.ppermute(outer, axes, both_ways(list(zip(chain[1:-1:2], chain[2::2]))))
    inner = lax.ppermute(inner, axes, both_ways(list(zip(chain[::2], chain[1::2]))))
    return outer, inner


def turn(value, step, count):
    return lax.ppermute(value, "views", [(i, (i + step) % count) for i in range(count)])


def per_device(estimate, views_data, target, psf_taps, shifts):
    x_cells, y_cells, z_cells = estimate.shape
    row_count = lax.axis_size("rows")
    block_count = lax.axis_size("blocks")
    peer_count = block_count * row_count
    view_count = lax.axis_size("views")
    brick_cols = z_cells // BRICK
    brick_count = x_cells * y_cells * brick_cols
    capacity = 2 * brick_count // peer_count
    part = y_cells // view_count
    all_cols = y_cells * block_count
    geo = (peer_count, capacity, x_cells, y_cells, brick_cols, row_count, all_cols, view_count)
    row, place = lax.axis_index("rows"), lax.axis_index("views")
    turned = lax.axis_index("blocks") % 2
    quarter = jnp.where(turned == 1, view_count - 1 - place, place)
    borders = [
        (snake(b * view_count - 1, view_count), snake(b * view_count, view_count))
        for b in range(1, block_count)
    ]
    edge_at = jnp.where(quarter == 0, 0, y_cells - TILE)
    edge = lax.ppermute(
        lax.dynamic_slice_in_dim(estimate, edge_at, TILE, 1), ("blocks", "views"), both_ways(borders)
    )
    outgoing = pack(shifts, target[0].transpose(0, 2, 1), views_data[0], geo)
    outgoing, edge = lax.optimization_barrier((outgoing, edge))
    arrived = lax.all_to_all(
        outgoing.reshape(peer_count, capacity + 1, 1, BRICK),
        ("blocks", "rows"), split_axis=0, concat_axis=0, tiled=True,
    ).reshape(peer_count * (capacity + 1), 1, BRICK)
    ids = jnp.stack([place, row % 2, quarter, turned]).astype(jnp.int32)
    taps = lax.all_gather(psf_taps, "views", axis=0, tiled=True)
    w = (taps / jnp.sum(taps, axis=2, keepdims=True)).reshape(-1)
    halo = f32(2, HALO, part + 2 * TILE, BRICK)
    own, *sent = call(
        part_kernel, "part", [f32(2, x_cells, part + 2 * TILE, BRICK), halo, halo],
        (ids, estimate, edge),
        scratch=[pltpu.VMEM((2, y_cells + 2 * TILE, BRICK), jnp.float32)],
    )
    wide = f32(2, x_cells + 2 * HALO, part + 2 * TRIM, BRICK)
    est = call(extend_kernel, "extend", [wide], (ids, own, *swap_layers(*sent)))[0]
    below = forward(w, est, view_count, x_cells)
    arrived, below = lax.optimization_barrier((arrived, below))
    moved = unpack(ids, arrived, peer_count, capacity, brick_count, view_count)
    moved = [m.reshape(brick_cols, x_cells, part, BRICK) for m in moved]
    behind, ahead = turn(moved[1], 1, view_count), turn(moved[3], -1, view_count)
    across = turn(moved[2], 2, view_count)
    total = backward(w, ids, below, (0,), moved[:1], None, 0)[0]
    total = backward(w, ids, below, (3, 1), (behind, ahead), total, 0)[0]
    total, *sent = backward(w, ids, below, (2,), (across,), total, 2 * HALO)
    total, *sent = merge(ids, total, *swap_layers(*sent), x_cells + 2 * HALO)
    mid, partial = middle(w, est, total, view_count, x_cells)
    est, below = ends(w, (ids, total, *swap_rows(*sent), est), mid, partial)
    observed = (moved[0], ahead, across, behind)
    total, *sent = backward(w, ids, below, (0, 1, 2, 3), observed, None, HALO)
    total, *sent = merge(ids, total, *swap_layers(*sent), x_cells)
    args = (ids, total, *swap_rows(*sent), est)
    own = call(
        functools.partial(finish_kernel, view_count), "finish",
        [f32(x_cells, part, BRICK)] * 2, args,
        scratch=[pltpu.VMEM((2, x_cells, part + 2 * TRIM, BRICK), jnp.float32)],
    )
    prev_a, next_b = turn(own[0], 1, view_count), turn(own[1], -1, view_count)
    prev_b, next_a = turn(own[1], 1, view_count), turn(own[0], -1, view_count)
    far_a, far_b = turn(prev_a, 1, view_count), turn(next_b, -1, view_count)
    pieces = (*own, next_a, next_b, far_a, far_b, prev_a, prev_b)
    return call(
        functools.partial(join_kernel, view_count), "join", [f32(x_cells, y_cells, z_cells)],
        (ids, *pieces),
    )[0]


def solution(mesh):
    placed = (
        P("rows", "blocks", None),
        P("views", "rows", "blocks", None),
        P("views", "rows", "blocks", None),
        P("views", None, None),
        P("views"),
    )
    return jax.shard_map(
        per_device, mesh=mesh, in_specs=placed, out_specs=P("rows", "blocks", None), check_vma=False
    )
```
